32 devices in a mesh: wide: 8 (over y, x, core), narrow: 4 (over z).
Axes of the slice: x: 2, y: 2, z: 4, core: 2. Of those that a mesh axis runs over, the one named last changes fastest.
Arguments:
- populations: float32 [19, 4, 256, 1024], P(None, None, ('wide', 'narrow')), as said below
- phase: int32 [4, 256, 1024], P(None, ('wide', 'narrow')), may hold values from 0 to 2, as said below
- porosity: float32 [4, 256, 1024], P(None, ('wide', 'narrow')), may hold values from 0 to 1, as said below
- napl: float32 [4, 256, 1024], P(None, ('wide', 'narrow')), may hold values from 0 to 0.9, as said below
- concentration: float32 [4, 256, 1024], P(None, ('wide', 'narrow')), may hold values from 0 to 1
- flags: int32 [2, 4, 1024], replicated, may hold values 0 or 1
Outputs:
- populations_out: float32 [19, 4, 256, 1024], P(None, None, ('wide', 'narrow'))
- concentration_out: float32 [4, 256, 1024], P(None, 'wide', 'narrow')
- napl_out: float32 [4, 256, 1024], P(None, 'wide', 'narrow')
The draws below stay inside these ranges and needn't reach their ends.
Inputs may be any that keep to these rules, and one draw needn't show every extreme that they name: `phase`: 0 open pore, 1 pore holding NAPL, 2 solid. `porosity`: exactly 0 on voxels of phase 2 and 0.35 or more elsewhere. `napl`: above 0 exactly on voxels of phase 1, 0 elsewhere. `populations`: every entry positive.
All inputs are finite; a program needn't handle non-finite values.
Results may differ from the reference program's by a relative error of at most 0.0003.
Values sent between devices are 32-bit elements; how exact they have to be, the bound alone decides.
No kernel may reach another device: no remote copies, remote signals or barrier semaphores. Data moves between devices by JAX's collectives and lax.ppermute only.
A program may use at most 128 MiB of HBM per device.

```python
import jax
import jax.numpy as jnp
import numpy as np
from jax import lax

Z = 4
LBM_STEPS = 4
TVD_STEPS = 2
X = 256
Y = 1024


lattice_dirs = np.array([[0, 0, 0], [1, 0, 0], [-1, 0, 0], [0, 1, 0], [0, -1, 0], [0, 0, 1], [0, 0, -1], [1, 1, 0], [-1, -1, 0], [1, -1, 0], [-1, 1, 0], [1, 0, 1], [-1, 0, -1], [1, 0, -1], [-1, 0, 1], [0, 1, 1], [0, -1, -1], [0, 1, -1], [0, -1, 1]])


lattice_weights = np.array([1.0 / 3.0] + [1.0 / 18.0] * 6 + [1.0 / 36.0] * 12)


def phase_labels(key):
    scores = jax.random.randint(jax.random.fold_in(key, 5), (Z, X, Y), 0, 100)
    return jnp.where(scores < 30, 2, jnp.where(scores < 45, 1, 0)).astype(jnp.int32)


def draw_phase(key, part):
    return phase_labels(key)


def draw_porosity(key, part):
    labels = phase_labels(key)
    spread = jax.random.uniform(jax.random.fold_in(key, 6), (Z, X, Y), jnp.float32)
    return jnp.where(labels == 2, 0.0, 0.35 + 0.65 * spread).astype(jnp.float32)


def draw_napl(key, part):
    labels = phase_labels(key)
    spread = jax.random.uniform(jax.random.fold_in(key, 7), (Z, X, Y), jnp.float32)
    return jnp.where(labels == 1, 0.2 + 0.7 * spread, 0.0).astype(jnp.float32)


def draw_populations(key, part):
    density = jax.random.uniform(jax.random.fold_in(key, 8), (Z, X, Y), jnp.float32, 0.9, 1.1)
    velocity = jax.random.uniform(jax.random.fold_in(key, 9), (3, Z, X, Y), jnp.float32, -0.12, 0.12)
    jitter = jax.random.uniform(jax.random.fold_in(key, 10), (19, Z, X, Y), jnp.float32, 0.85, 1.15)
    planes = []
    for direction in range(19):
        layer_c = float(lattice_dirs[direction][2])
        flow_c = float(lattice_dirs[direction][0])
        cross_c = float(lattice_dirs[direction][1])
        proj = layer_c * velocity[0] + flow_c * velocity[1] + cross_c * velocity[2]
        planes.append(float(lattice_weights[direction]) * density * (1.0 + 3.0 * proj))
    return (jnp.stack(planes) * jitter).astype(jnp.float32)


def set_ends(drawn, key, smallest, largest):
    shape = drawn.shape
    place = [jax.random.randint(jax.random.fold_in(key, axis), (), 0, shape[axis]) for axis in range(len(shape))]
    drawn = drawn.at[tuple(place)].set(smallest)
    longest = shape.index(max(shape))
    place[longest] = (place[longest] + 1) % shape[longest]
    return drawn.at[tuple(place)].set(largest)


def block_scale(stream_key, shape, split, smallest, top_value):
    def one(axis_at, blocks):
        draws = jax.random.uniform(jax.random.fold_in(jax.random.fold_in(stream_key, 6), axis_at), (blocks,), jnp.float32, smallest / len(split), top_value / len(split))
        return jnp.repeat(jnp.exp(draws), shape[axis_at] // blocks).reshape((-1,) + (1,) * (len(shape) - axis_at - 1))

    level = one(*split[0])
    for cut in split[1:]:
        level = level * one(*cut)
    return level


def setup_inputs(seed: int = 0) -> dict:
    arg_keys = jax.random.split(jax.random.key(seed), 7)
    return {
        "populations": draw_populations(jax.random.fold_in(arg_keys[6], 71), 0),
        "phase": draw_phase(jax.random.fold_in(arg_keys[6], 71), 0),
        "porosity": draw_porosity(jax.random.fold_in(arg_keys[6], 71), 0),
        "napl": draw_napl(jax.random.fold_in(arg_keys[6], 71), 0),
        "concentration": jnp.clip(1.0 * jax.random.uniform(arg_keys[4], (Z, X, Y), jnp.float32) ** block_scale(arg_keys[4], (Z, X, Y), ((1, 32),), -0.2, 0.2), 0.0, 1.0),
        "flags": set_ends((jax.random.randint(arg_keys[5], (2, Z, Y), 0, 2) < 1).astype(jnp.int32), jax.random.fold_in(arg_keys[5], 1), 0, 1),
    }


lattice_dirs = np.array([[0, 0, 0], [1, 0, 0], [-1, 0, 0], [0, 1, 0], [0, -1, 0], [0, 0, 1], [0, 0, -1],
                         [1, 1, 0], [-1, -1, 0], [1, -1, 0], [-1, 1, 0], [1, 0, 1], [-1, 0, -1], [1, 0, -1],
                         [-1, 0, 1], [0, 1, 1], [0, -1, -1], [0, 1, -1], [0, -1, 1]])
lattice_weights = np.array([1.0 / 3.0] + [1.0 / 18.0] * 6 + [1.0 / 36.0] * 12)
opposite_dir = [0, 2, 1, 4, 3, 6, 5, 8, 7, 10, 9, 12, 11, 14, 13, 16, 15, 18, 17]
relax_time = 0.8
napl_drag = 0.5
diffusion = 0.15
transfer = 0.3
depletion = 0.5
porosity_floor = 0.3


def moments(popul):
    dirs = jnp.asarray(lattice_dirs.T, jnp.float32)
    return jnp.einsum('kq,qzxy->kzxy', dirs, popul, precision=lax.Precision.HIGHEST)


def collide(popul, phase):
    density = jnp.sum(popul, axis=0)
    moment = moments(popul)
    factor = jnp.where(phase == 1, napl_drag, 1.0)
    velocity = moment / density[None] * factor[None]
    dirs = jnp.asarray(lattice_dirs, jnp.float32)
    proj = jnp.einsum('qk,kzxy->qzxy', dirs, velocity, precision=lax.Precision.HIGHEST)
    square = jnp.sum(velocity * velocity, axis=0)
    weights = jnp.asarray(lattice_weights, jnp.float32)[:, None, None, None]
    equil = weights * density[None] * (1.0 + 3.0 * proj + 4.5 * proj * proj - 1.5 * square[None])
    return popul - (popul - equil) / relax_time


def shift_cells(field, offset, fill):
    if offset == 0:
        return field
    edge = jnp.full(field.shape[:-1] + (1,), fill, field.dtype)
    if offset > 0:
        return jnp.concatenate([edge, field[..., :-1]], axis=-1)
    return jnp.concatenate([field[..., 1:], edge], axis=-1)


def minmod(left, right):
    return 0.5 * (jnp.sign(left) + jnp.sign(right)) * jnp.minimum(jnp.abs(left), jnp.abs(right))


def face_balance(conc_pad, poro_pad, vel_pad, along, extent):
    def layer_at(field, start):
        return lax.slice_in_dim(field, start, start + extent + 1, axis=along)
    conc_back = layer_at(conc_pad, 0)
    conc_here = layer_at(conc_pad, 1)
    conc_next = layer_at(conc_pad, 2)
    conc_far = layer_at(conc_pad, 3)
    open_face = layer_at(poro_pad, 1) * layer_at(poro_pad, 2)
    carried = open_face * 0.5 * (layer_at(vel_pad, 1) + layer_at(vel_pad, 2))
    upwind = conc_here + 0.5 * minmod(conc_here - conc_back, conc_next - conc_here)
    downwind = conc_next - 0.5 * minmod(conc_next - conc_here, conc_far - conc_next)
    flux = carried * jnp.where(carried > 0, upwind, downwind) - diffusion * open_face * (conc_next - conc_here)
    return lax.slice_in_dim(flux, 0, extent, axis=along) - lax.slice_in_dim(flux, 1, extent + 1, axis=along)


def pad_ends(field, low_rows, high_rows):
    return jnp.concatenate([low_rows, low_rows, field, high_rows, high_rows], axis=-2)


def pad_side(field):
    return jnp.pad(field, ((0, 0), (0, 0), (2, 2)))


def wrap_layers(field):
    return jnp.concatenate([field[-2:], field, field[:2]], axis=0)


def reference(populations, phase, porosity, napl, concentration, flags):
    solid = phase == 2
    popul = populations
    for _ in range(LBM_STEPS):
        post = collide(popul, phase)
        moved_all = []
        for direction in range(19):
            x_step = int(lattice_dirs[direction][0])
            y_step = int(lattice_dirs[direction][1])
            z_step = int(lattice_dirs[direction][2])
            moved = jnp.roll(post[direction], x_step, axis=1)
            moved = jnp.roll(shift_cells(moved, y_step, 0.0), z_step, axis=0)
            source = jnp.roll(solid, x_step, axis=1)
            source = jnp.roll(shift_cells(source, y_step, True), z_step, axis=0)
            bounced = jnp.where(source, post[opposite_dir[direction]], moved)
            moved_all.append(jnp.where(solid, popul[direction], bounced))
        popul = jnp.stack(moved_all)
    density = jnp.sum(popul, axis=0)
    momentum = jnp.where(solid[None], 0.0, moments(popul) / density[None])
    velocity = jnp.stack([momentum[2], momentum[0], momentum[1]])
    flag_rows = flags.astype(jnp.float32)
    poro_x = pad_ends(porosity, flag_rows[0][:, None, :], flag_rows[1][:, None, :])
    xvel_x = pad_ends(velocity[1], velocity[1][:, :1, :], velocity[1][:, -1:, :])
    poro_y = pad_side(porosity)
    yvel_y = pad_side(velocity[2])
    poro_z = wrap_layers(porosity)
    zvel_z = wrap_layers(velocity[0])
    conc = concentration
    remain = napl
    for _ in range(TVD_STEPS):
        conc_x = pad_ends(conc, jnp.zeros_like(conc[:, :1, :]), conc[:, -1:, :])
        change = face_balance(conc_x, poro_x, xvel_x, 1, conc.shape[1])
        change = change + face_balance(pad_side(conc), poro_y, yvel_y, 2, conc.shape[2])
        change = change + face_balance(wrap_layers(conc), poro_z, zvel_z, 0, conc.shape[0])
        rate = transfer * remain * (1.0 - conc)
        conc = conc + (change + rate) / jnp.maximum(porosity, porosity_floor)
        remain = remain - depletion * rate
    return popul, conc, remain
```

```python
import functools

import jax
import jax.numpy as jnp
import numpy as np
from jax import lax
from jax.experimental import pallas as pl
from jax.experimental.pallas import tpu as pltpu
from jax.sharding import PartitionSpec as P

LBM_STEPS = 4
F32 = jnp.float32

DIRS = [
    (0, 0, 0), (1, 0, 0), (-1, 0, 0), (0, 1, 0), (0, -1, 0), (0, 0, 1), (0, 0, -1),
    (1, 1, 0), (-1, -1, 0), (1, -1, 0), (-1, 1, 0), (1, 0, 1), (-1, 0, -1), (1, 0, -1),
    (-1, 0, 1), (0, 1, 1), (0, -1, -1), (0, 1, -1), (0, -1, 1),
]
OPP = [0, 2, 1, 4, 3, 6, 5, 8, 7, 10, 9, 12, 11, 14, 13, 16, 15, 18, 17]
UP = [1, 7, 9, 11, 13]
DOWN = [2, 8, 10, 12, 14]
DIFFUSION = 0.15
TRANSFER = 0.3
DEPLETION = 0.5
FLOOR = 0.3
SUBS = 8
LANES = 128
VMEM_LIMIT = 16 * 1024 * 1024


def to_view(array):
    *lead, rows, width = array.shape
    n = len(lead)
    t = array.reshape(*lead, rows // SUBS, SUBS, width // LANES, LANES)
    t = t.transpose(*range(n), n, n + 2, n + 1, n + 3)
    return t.reshape(*lead[:-1], lead[-1] * rows * width // LANES, LANES)


def from_view(view, shape):
    *lead, rows, width = shape
    n = len(lead)
    t = view.reshape(*lead, rows // SUBS, width // LANES, SUBS, LANES)
    t = t.transpose(*range(n), n, n + 2, n + 1, n + 3)
    return t.reshape(shape)


def iotas():
    lane = lax.broadcasted_iota(jnp.int32, (SUBS, LANES), 1)
    sub = lax.broadcasted_iota(jnp.int32, (SUBS, LANES), 0)
    return lane, sub


def cut(c):
    return slice(c * LANES, (c + 1) * LANES)


def strided(tiles, c, x):
    return pl.ds(c * SUBS + x, SUBS, stride=tiles * SUBS)


def collide(f, fac):
    s = [f[2 * p + 1] + f[2 * p + 2] for p in range(9)]
    d = [f[2 * p + 1] - f[2 * p + 2] for p in range(9)]
    rho = f[0] + (((s[0] + s[1]) + (s[2] + s[3])) + ((s[4] + s[5]) + (s[6] + s[7])) + s[8])
    jx = d[0] + ((d[3] + d[4]) + (d[5] + d[6]))
    jy = d[1] + ((d[3] - d[4]) + (d[7] + d[8]))
    jz = d[2] + ((d[5] - d[6]) + (d[7] - d[8]))
    inv = fac / rho
    vx, vy, vz = jx * inv, jy * inv, jz * inv
    w1 = rho * np.float32(1.25 / 18)
    w2 = rho * np.float32(1.25 / 36)
    w4 = rho * np.float32(1.25 / 72)
    a1 = w1 - w1 * ((vx * vx + vy * vy + vz * vz) * np.float32(1.0 / 6))
    a2 = a1 * np.float32(0.5)
    post = [a1 * np.float32(6.0) - f[0] * np.float32(0.25)]
    axes = [vx, vy, vz, vx + vy, vx - vy, vx + vz, vx - vz, vy + vz, vy - vz]
    for p, v in enumerate(axes):
        wa, wh, base = (w1, w2, a1) if p < 3 else (w2, w4, a2)
        even = (base + (wh * v) * v) - s[p] * np.float32(0.125)
        odd = wa * v - d[p] * np.float32(0.125)
        post += [even + odd, even - odd]
    return post


def pull(load, q, c, tiles, halves, lane, sub):
    _, cross, layer = DIRS[q]
    v = load(q, c)
    if cross == 1:
        if c > 0:
            side = load(q, c - 1)
        else:
            side = jnp.where(sub % halves == 0, jnp.nan, pltpu.roll(load(q, tiles - 1), 1, 0))
        v = pltpu.roll(jnp.where(lane == LANES - 1, side, v), 1, 1)
    elif cross == -1:
        if c < tiles - 1:
            side = load(q, c + 1)
        else:
            side = jnp.where(sub % halves == halves - 1, jnp.nan, pltpu.roll(load(q, 0), SUBS - 1, 0))
        v = pltpu.roll(jnp.where(lane == 0, side, v), LANES - 1, 1)
    if layer:
        v = pltpu.roll(v, (layer * halves) % SUBS, 0)
    return v


def stream(g, lo, hi, x, c, tiles, halves, lane, sub, place):
    def load(q, cc):
        flow = DIRS[q][0]
        if flow == 1 and place == "first":
            return lo[UP.index(q), :, cut(cc)]
        if flow == -1 and place == "last":
            return hi[DOWN.index(q), :, cut(cc)]
        return g[q, x - flow, :, cut(cc)]

    f = [g[0, x, :, cut(c)]]
    for q in range(1, 19):
        v = pull(load, q, c, tiles, halves, lane, sub)
        f.append(jnp.where(v != v, g[OPP[q], x, :, cut(c)], v))
    return f


def first_edge_kernel(
    tiles, pop_h, phase_h, conc_h, napl_h, poro_h, flags_h,
    pop, phase, conc, napl, poro, flags, ge, up, down, sems,
):
    small = [
        pltpu.make_async_copy(a, b, sems.at[tiles + i])
        for i, (a, b) in enumerate(
            ((phase_h, phase), (conc_h, conc), (poro_h, poro), (napl_h, napl), (flags_h, flags))
        )
    ]
    small[0].start()
    parts = [pltpu.make_async_copy(pop_h.at[:, :, c], pop.at[:, :, c], sems.at[c]) for c in range(tiles)]
    for copy in parts:
        copy.start()
    for copy in small[1:]:
        copy.start()
    flat = pop.reshape(pop.shape[0], SUBS * tiles * SUBS, LANES)
    rows = SUBS
    small[0].wait()
    for c in range(tiles):
        parts[c].wait()
        for k, x in enumerate((0, rows - 1)):
            at = strided(tiles, c, x)
            post = collide([flat[q, at, :] for q in range(19)], drag(phase[at, :]))
            for q in range(19):
                ge[q, k, :, cut(c)] = post[q]
            for i, q in enumerate(DOWN if k == 0 else UP):
                (down if k == 0 else up)[i, :, cut(c)] = post[q]
    for copy in small[1:]:
        copy.wait()
    for n, (ref, r) in enumerate(((conc, 0), (conc, 1), (poro, 0))):
        for c in range(tiles):
            down[5 + n, :, cut(c)] = ref[strided(tiles, c, r), :]
            up[5 + n, :, cut(c)] = ref[strided(tiles, c, rows - 1 - r), :]


def drag(ph):
    return jnp.where(ph == 2, jnp.nan, jnp.where(ph == 1, np.float32(1.5), np.float32(3.0)))


def first_inner_kernel(tiles, halves, pop, phase, conc, napl, poro, flags, ge, g, fac, start, slabs, open_ends):
    rows = g.shape[1]
    length = tiles * LANES
    for k in range(2):
        for z in range(SUBS // halves):
            for h in range(halves):
                line = flags[k, z : z + 1, h * length : (h + 1) * length]
                open_ends[k, z * halves + h : z * halves + h + 1, :] = line.astype(F32)

    def row(x, inner):
        for c in range(tiles):
            at = strided(tiles, c, x)
            fc = drag(phase[at, :])
            fac[x, :, cut(c)] = fc
            f = [pop[q, at, :] for q in range(19)]
            post = collide(f, fc) if inner else None
            for q in range(19):
                start[q, x, :, cut(c)] = f[q]
                g[q, x, :, cut(c)] = post[q] if inner else ge[q, 0 if x == 0 else 1, :, cut(c)]
            for k, ref in enumerate((conc, napl, poro)):
                slabs[k, x, :, cut(c)] = ref[at, :]
        return 0

    row(0, False)
    lax.fori_loop(1, rows - 1, lambda x, _: row(x, True), 0)
    row(rows - 1, False)


def edge_kernel(tiles, halves, g, fac, lo, hi, ge, up, down):
    rows = g.shape[1]
    lane, sub = iotas()
    for k, (x, place) in enumerate(((0, "first"), (rows - 1, "last"))):
        for c in range(tiles):
            f = stream(g, lo, hi, x, c, tiles, halves, lane, sub, place)
            post = collide(f, fac[x, :, cut(c)])
            for q in range(19):
                ge[q, k, :, cut(c)] = post[q]
            for i, q in enumerate(DOWN if k == 0 else UP):
                (down if k == 0 else up)[i, :, cut(c)] = post[q]


def inner_kernel(tiles, halves, g, ge, fac, out):
    rows = g.shape[1]
    lane, sub = iotas()

    def row(x, _):
        for c in range(tiles):
            f = stream(g, None, None, x, c, tiles, halves, lane, sub, "mid")
            post = collide(f, fac[x, :, cut(c)])
            for q in range(19):
                out[q, x, :, cut(c)] = post[q]
        return 0

    lax.fori_loop(1, rows - 1, row, 0)
    for q in range(19):
        out[q, 0] = ge[q, 0]
        out[q, rows - 1] = ge[q, 1]


def speed(f, fc):
    s = [f[2 * p + 1] + f[2 * p + 2] for p in range(9)]
    d = [f[2 * p + 1] - f[2 * p + 2] for p in range(9)]
    rho = f[0] + (((s[0] + s[1]) + (s[2] + s[3])) + ((s[4] + s[5]) + (s[6] + s[7])) + s[8])
    jx = d[0] + ((d[3] + d[4]) + (d[5] + d[6]))
    jy = d[1] + ((d[3] - d[4]) + (d[7] + d[8]))
    jz = d[2] + ((d[5] - d[6]) + (d[7] - d[8]))
    inv = np.float32(1.0) / rho
    return [jnp.where(fc != fc, np.float32(0.0), j * inv) for j in (jz, jx, jy)]


def edge_speed_kernel(tiles, halves, g, fac, lo, hi, ue, up, down):
    rows = g.shape[1]
    lane, sub = iotas()
    for k, (x, place) in enumerate(((0, "first"), (rows - 1, "last"))):
        for c in range(tiles):
            f = stream(g, lo, hi, x, c, tiles, halves, lane, sub, place)
            for i, v in enumerate(speed(f, fac[x, :, cut(c)])):
                ue[i, k, :, cut(c)] = v
                if i == 1:
                    (down if k == 0 else up)[:, cut(c)] = v


def inner_speed_kernel(tiles, halves, g, fac, ue, u):
    rows = g.shape[1]
    lane, sub = iotas()

    def row(x, _):
        for c in range(tiles):
            f = stream(g, None, None, x, c, tiles, halves, lane, sub, "mid")
            for i, v in enumerate(speed(f, fac[x, :, cut(c)])):
                u[i, x, :, cut(c)] = v
        return 0

    lax.fori_loop(1, rows - 1, row, 0)
    for i in range(3):
        u[i, 0] = ue[i, 0]
        u[i, rows - 1] = ue[i, 1]


def swap_tile(v, sub):
    v = list(v)
    for k in (4, 2, 1):
        low = sub & k == 0
        for i in range(SUBS):
            if not i & k:
                a, b = v[i], v[i + k]
                v[i] = jnp.where(low, a, pltpu.roll(b, k, 0))
                v[i + k] = jnp.where(low, pltpu.roll(a, SUBS - k, 0), b)
    return v


def final_kernel(tiles, halves, g, fac, lo, hi, start, out, buf, sems):
    rows = g.shape[1]
    lane, sub = iotas()

    def row_of(q, x):
        at = x - DIRS[q][0]
        if at < 0:
            return lambda qq, cc: lo[UP.index(qq), :, cut(cc)]
        if at >= rows:
            return lambda qq, cc: hi[DOWN.index(qq), :, cut(cc)]
        return lambda qq, cc: g[qq, at, :, cut(cc)]

    copies = []
    for q in range(19):
        for c in range(tiles):
            new = []
            for x in range(rows):
                fc = fac[x, :, cut(c)]
                if q == 0:
                    v = g[0, x, :, cut(c)]
                else:
                    v = pull(row_of(q, x), q, c, tiles, halves, lane, sub)
                    v = jnp.where(v != v, g[OPP[q], x, :, cut(c)], v)
                new.append(jnp.where(fc != fc, start[q, x, :, cut(c)], v))
            for i, t in enumerate(swap_tile(new, sub)):
                first = (i * tiles + c) * SUBS
                buf[q, first : first + SUBS, :] = t
        copy = pltpu.make_async_copy(buf.at[q], out.at[q], sems.at[q])
        copy.start()
        copies.append(copy)
    for copy in copies:
        copy.wait()


def slope(p, q):
    return np.float32(0.5) * (
        jnp.maximum(jnp.minimum(p, q), np.float32(0.0)) + jnp.minimum(jnp.maximum(p, q), np.float32(0.0))
    )


def loss(s, c):
    return [np.float32(TRANSFER) * a * (np.float32(1.0) - b) for a, b in zip(s, c)]


def ends_of(parts, strips):
    place = lax.axis_index("wide") * parts + lax.axis_index("narrow")
    return place == 0, place == strips - 1


class Row:
    def __init__(self, tiles, halves):
        self.tiles, self.halves = tiles, halves
        self.lane, self.sub = iotas()

    def read(self, slab):
        return [slab[:, cut(c)] for c in range(self.tiles)]

    def after(self, v):
        out = []
        for c in range(self.tiles):
            if c < self.tiles - 1:
                side = v[c + 1]
            else:
                edge = self.sub % self.halves == self.halves - 1
                side = jnp.where(edge, np.float32(0.0), pltpu.roll(v[0], SUBS - 1, 0))
            out.append(pltpu.roll(jnp.where(self.lane == 0, side, v[c]), LANES - 1, 1))
        return out

    def before(self, v):
        out = []
        for c in range(self.tiles):
            if c > 0:
                side = v[c - 1]
            else:
                edge = self.sub % self.halves == 0
                side = jnp.where(edge, np.float32(0.0), pltpu.roll(v[self.tiles - 1], 1, 0))
            out.append(pltpu.roll(jnp.where(self.lane == LANES - 1, side, v[c]), 1, 1))
        return out

    def above(self, v):
        return [pltpu.roll(t, SUBS - self.halves, 0) for t in v]

    def below(self, v):
        return [pltpu.roll(t, self.halves, 0) for t in v]

    def step(self, r, conc, poro, flow, u, s):
        def each(f, *lists):
            return [f(*t) for t in zip(*lists)]

        def less(a, b):
            return each(lambda x, y: x - y, a, b)

        def times(a, b):
            return each(lambda x, y: x * y, a, b)

        def slopes(a, b):
            return each(slope, a, b)

        def face(w, va, vb, c, cn, sl, sn, dn):
            a = each(lambda w, x, y: w * np.float32(0.5) * (x + y), w, va, vb)
            return each(
                lambda a, w, c, cn, sl, sn, dn: a * jnp.where(a > 0, c + sl, cn - sn)
                - np.float32(DIFFUSION) * w * dn,
                a, w, c, cn, sl, sn, dn,
            )

        cm2, cm1, c, cp1, cp2 = (conc(r + k) for k in (-2, -1, 0, 1, 2))
        pm, p, pn = (poro(r + k) for k in (-1, 0, 1))
        vm, v0, vn = (flow(r + k) for k in (-1, 0, 1))
        d0, d1, d2, d3 = less(cm1, cm2), less(c, cm1), less(cp1, c), less(cp2, cp1)
        sm, s0, sp = slopes(d0, d1), slopes(d1, d2), slopes(d2, d3)
        change = less(
            face(times(pm, p), vm, v0, cm1, c, sm, s0, d1), face(times(p, pn), v0, vn, c, cp1, s0, sp, d2)
        )
        for after, before, vel, open_ends in (
            (self.after, self.before, u[1], True), (self.above, self.below, u[0], False),
        ):
            cn = after(c)
            dn = less(cn, c)
            dm = less(c, before(c)) if open_ends else before(dn)
            s0 = slopes(dm, dn)
            flux = face(times(p, after(p)), vel, after(vel), c, cn, s0, after(s0), dn)
            change = each(lambda t, a, b: t + (a - b), change, before(flux), flux)
        rate = loss(s, c)
        cnew = each(
            lambda c, t, k, p: c + (t + k) / jnp.maximum(p, np.float32(FLOOR)), c, change, rate, p
        )
        return cnew, each(lambda s, k: s - np.float32(DEPLETION) * k, s, rate)


def row_readers(row, rows, ends, conc_at, lo_c, hi_c, slabs, lo1, hi1, flags, u, ulo, uhi):
    first, last = ends_of(*ends)

    def pick(flag, a, b):
        there = [np.float32(0.0)] * row.tiles if a is None else row.read(a)
        return [jnp.where(flag, x, y) for x, y in zip(there, row.read(b))]

    def conc(r):
        if r < 0:
            return pick(first, None, lo_c(-1 - r))
        if r >= rows:
            return pick(last, conc_at(rows - 1), hi_c(r - rows))
        return row.read(conc_at(r))

    def poro(r):
        if r < 0:
            return pick(first, flags.at[0], lo1.at[7])
        if r >= rows:
            return pick(last, flags.at[1], hi1.at[7])
        return row.read(slabs.at[2, r])

    def flow(r):
        if r < 0:
            return pick(first, u.at[1, 0], ulo)
        if r >= rows:
            return pick(last, u.at[1, rows - 1], uhi)
        return row.read(u.at[1, r])

    return conc, poro, flow


def early_kernel(tiles, halves, ends, slabs, lo1, hi1, u, flags, cs):
    rows = u.shape[1]
    row = Row(tiles, halves)
    conc, poro, flow = row_readers(
        row, rows, ends, lambda r: slabs.at[0, r], lambda k: lo1.at[5 + k], lambda k: hi1.at[5 + k],
        slabs, lo1, hi1, flags, u, None, None,
    )
    for r in range(1, rows - 1):
        new = row.step(r, conc, poro, flow, (row.read(u.at[0, r]), row.read(u.at[2, r])), row.read(slabs.at[1, r]))
        for k in range(2):
            for c in range(tiles):
                cs[k, r - 1, :, cut(c)] = new[k][c]


def rim_kernel(tiles, halves, ends, slabs, lo1, hi1, u, flags, ulo, uhi, inner, cs, up, down):
    rows = u.shape[1]
    row = Row(tiles, halves)
    conc, poro, flow = row_readers(
        row, rows, ends, lambda r: slabs.at[0, r], lambda k: lo1.at[5 + k], lambda k: hi1.at[5 + k],
        slabs, lo1, hi1, flags, u, ulo, uhi,
    )
    for i, r in enumerate((0, rows - 1)):
        new = row.step(r, conc, poro, flow, (row.read(u.at[0, r]), row.read(u.at[2, r])), row.read(slabs.at[1, r]))
        for k in range(2):
            for c in range(tiles):
                cs[k, i, :, cut(c)] = new[k][c]
        for c in range(tiles):
            (down if i == 0 else up)[0, :, cut(c)] = new[0][c]
    down[1] = inner[0, 0]
    up[1] = inner[0, rows - 3]


def late_rows(tiles, halves, ends, which, slabs, lo1, hi1, u, flags, ulo, uhi, inner, rim, clo, chi, store):
    rows = u.shape[1]
    row = Row(tiles, halves)

    def state(k, r):
        return rim.at[k, 0 if r == 0 else 1] if r in (0, rows - 1) else inner.at[k, r - 1]

    conc, poro, flow = row_readers(
        row, rows, ends, lambda r: state(0, r), lambda k: clo.at[k], lambda k: chi.at[k],
        slabs, lo1, hi1, flags, u, ulo, uhi,
    )
    for r in which:
        new = row.step(r, conc, poro, flow, (row.read(u.at[0, r]), row.read(u.at[2, r])), row.read(state(1, r)))
        for c in range(tiles):
            store(r, c, new[0][c])


def middle_kernel(tiles, halves, ends, slabs, lo1, hi1, u, flags, inner, rim, out):
    def store(r, c, v):
        out[r - 2, :, cut(c)] = v

    late_rows(
        tiles, halves, ends, range(2, u.shape[1] - 2), slabs, lo1, hi1, u, flags, None, None, inner, rim,
        None, None, store,
    )


def deal(tiles, halves, parts, natural, blocks):
    depth = halves * tiles * SUBS
    run = depth // parts
    for k in range(parts):
        dest = lax.axis_index("narrow") ^ k
        for z in range(SUBS // halves):
            at = pl.multiple_of(z * depth + dest * run, SUBS)
            blocks[k][z] = natural[pl.ds(at, run), :]


def napl_kernel(tiles, halves, parts, inner, rim, *refs):
    *blocks, natural = refs
    rows = inner.shape[1] + 2
    for r in range(rows):
        for c in range(tiles):
            if r in (0, rows - 1):
                cc, ss = (rim[k, 0 if r == 0 else 1, :, cut(c)] for k in range(2))
            else:
                cc, ss = (inner[k, r - 1, :, cut(c)] for k in range(2))
            natural[strided(tiles, c, r), :] = ss - np.float32(DEPLETION) * loss([ss], [cc])[0]
    deal(tiles, halves, parts, natural, blocks)


def last_kernel(
    tiles, halves, ends, parts, slabs, lo1, hi1, u, flags, ulo, uhi, inner, rim, clo, chi, mid, *refs
):
    *blocks, natural = refs
    rows = u.shape[1]

    def store(r, c, v):
        natural[strided(tiles, c, r), :] = v

    for r in range(2, rows - 2):
        for c in range(tiles):
            store(r, c, mid[r - 2, :, cut(c)])
    late_rows(
        tiles, halves, ends, (0, 1, rows - 2, rows - 1), slabs, lo1, hi1, u, flags, ulo, uhi, inner, rim,
        clo, chi, store,
    )
    deal(tiles, halves, parts, natural, blocks)


def gather_kernel(parts, *refs):
    conc, napl, sems = refs[2 * parts :]
    copies = []
    for k in range(parts):
        origin = lax.axis_index("narrow") ^ k
        for i, (blocks, out) in enumerate(((refs[:parts], conc), (refs[parts : 2 * parts], napl))):
            copies.append(pltpu.make_async_copy(blocks[k], out.at[:, origin], sems.at[i * parts + k]))
            copies[-1].start()
    for copy in copies:
        copy.wait()


def call(kernel, out_shape, scratch=(), hbm=(), hbm_out=False, name=None, flops=0, n_in=0):
    specs = [pl.BlockSpec(memory_space=pltpu.HBM if i in hbm else pltpu.VMEM) for i in range(n_in)]
    if hbm_out:
        out_specs = jax.tree.map(lambda _: pl.BlockSpec(memory_space=pltpu.HBM), out_shape)
    else:
        out_specs = jax.tree.map(lambda _: pl.BlockSpec(memory_space=pltpu.VMEM), out_shape)
    return pl.pallas_call(
        kernel,
        out_shape=out_shape,
        in_specs=specs,
        out_specs=out_specs,
        scratch_shapes=list(scratch),
        name=name,
        compiler_params=pltpu.CompilerParams(vmem_limit_bytes=VMEM_LIMIT),
        cost_estimate=pl.CostEstimate(flops=flops, bytes_accessed=flops // 10, transcendentals=0),
    )


def local(populations, phase, porosity, napl, concentration, flags):
    layers, rows, width = phase.shape
    halves = SUBS // layers
    length = width // halves
    tiles = length // LANES
    parts = lax.axis_size("narrow")
    strips = lax.axis_size("wide") * parts
    both = ("wide", "narrow")
    ahead = [(i, (i + 1) % strips) for i in range(strips)]
    back = [(j, i) for i, j in ahead]
    cells = rows * SUBS * length
    slab = (SUBS, length)
    ends = (parts, strips)
    run = width // LANES * SUBS // parts

    def hold(*shape, dtype=F32):
        return pltpu.VMEM(shape, dtype)

    def exchange(up, down):
        return lax.ppermute(up, both, ahead), lax.ppermute(down, both, back)

    def pairwise(blocks):
        out = [blocks[0]] * parts
        for k in reversed(range(1, parts)):
            out[k] = lax.ppermute(blocks[k], "narrow", [(i, i ^ k) for i in range(parts)])
        return out

    pop = to_view(populations).reshape(19, SUBS, tiles, SUBS, LANES)
    views = [to_view(a) for a in (phase, concentration, napl, porosity)]
    flat = views[0].shape
    given = [pltpu.with_memory_space_constraint(a, pltpu.HBM) for a in (pop, *views, flags)]
    popv, phv, cov, nav, pov, flv, ge, up, down = call(
        functools.partial(first_edge_kernel, tiles),
        (
            hold(*pop.shape), hold(*flat, dtype=jnp.int32), hold(*flat), hold(*flat), hold(*flat),
            hold(*flags.shape, dtype=jnp.int32), hold(19, 2, *slab), hold(8, *slab), hold(8, *slab),
        ),
        scratch=(pltpu.SemaphoreType.DMA((tiles + 5,)),),
        hbm=range(6), name="first_edge", flops=100 * cells, n_in=6,
    )(*given)
    lo, hi = lo1, hi1 = exchange(up, down)
    g, fac, start, slabs, open_ends = call(
        functools.partial(first_inner_kernel, tiles, halves),
        (
            hold(19, rows, *slab), hold(rows, *slab), hold(19, rows, *slab), hold(3, rows, *slab),
            hold(2, *slab),
        ),
        name="first_inner", flops=400 * cells, n_in=7,
    )(popv.reshape(19, *flat), phv, cov, nav, pov, flv, ge)
    for _ in range(1, LBM_STEPS):
        ge, up, down = call(
            functools.partial(edge_kernel, tiles, halves),
            (hold(19, 2, *slab), hold(5, *slab), hold(5, *slab)),
            name="edge", flops=60 * cells, n_in=4,
        )(g, fac, lo, hi)
        lo, hi = exchange(up, down)
        g = call(
            functools.partial(inner_kernel, tiles, halves),
            hold(19, rows, *slab), name="inner", flops=250 * cells, n_in=3,
        )(g, ge, fac)
    ue, up, down = call(
        functools.partial(edge_speed_kernel, tiles, halves),
        (hold(3, 2, *slab), hold(*slab), hold(*slab)),
        name="edge_speed", flops=40 * cells, n_in=4,
    )(g, fac, lo, hi)
    ulo, uhi = exchange(up, down)
    u = call(
        functools.partial(inner_speed_kernel, tiles, halves),
        hold(3, rows, *slab), name="inner_speed", flops=150 * cells, n_in=3,
    )(g, fac, ue)
    inner = call(
        functools.partial(early_kernel, tiles, halves, ends),
        hold(2, rows - 2, *slab), name="early", flops=100 * cells, n_in=5,
    )(slabs, lo1, hi1, u, open_ends)
    rim, up, down = call(
        functools.partial(rim_kernel, tiles, halves, ends),
        (hold(2, 2, *slab), hold(2, *slab), hold(2, *slab)),
        name="rim", flops=30 * cells, n_in=8,
    )(slabs, lo1, hi1, u, open_ends, ulo, uhi, inner)
    clo, chi = exchange(up, down)
    blocks = call(
        functools.partial(napl_kernel, tiles, halves, parts),
        tuple(hold(layers, run, LANES) for _ in range(parts)),
        scratch=(pltpu.VMEM(flat, F32),), name="napl", flops=20 * cells, n_in=2,
    )(inner, rim)
    napl_blocks = pairwise(blocks)
    mid = call(
        functools.partial(middle_kernel, tiles, halves, ends),
        hold(rows - 4, *slab), name="middle", flops=60 * cells, n_in=7,
    )(slabs, lo1, hi1, u, open_ends, inner, rim)
    blocks = call(
        functools.partial(last_kernel, tiles, halves, ends, parts),
        tuple(hold(layers, run, LANES) for _ in range(parts)),
        scratch=(pltpu.VMEM(flat, F32),), name="last", flops=60 * cells, n_in=12,
    )(slabs, lo1, hi1, u, open_ends, ulo, uhi, inner, rim, clo, chi, mid)
    conc_blocks = pairwise(blocks)
    out = call(
        functools.partial(final_kernel, tiles, halves),
        jax.ShapeDtypeStruct((19, *flat), F32),
        scratch=(pltpu.VMEM((19, *flat), F32), pltpu.SemaphoreType.DMA((19,))),
        hbm_out=True, name="final", flops=400 * cells, n_in=5,
    )(g, fac, lo, hi, start)
    tile = (layers, parts, run, LANES)
    conc_out, napl_out = call(
        functools.partial(gather_kernel, parts),
        (jax.ShapeDtypeStruct(tile, F32), jax.ShapeDtypeStruct(tile, F32)),
        scratch=(pltpu.SemaphoreType.DMA((2 * parts,)),),
        hbm_out=True, name="gather", flops=10 * cells, n_in=2 * parts,
    )(*conc_blocks, *napl_blocks)
    shape = (layers, rows * parts, width // parts)

    def tile_of(a):
        return from_view(a.reshape(layers * parts * run, LANES), shape)

    return from_view(out, populations.shape), tile_of(conc_out), tile_of(napl_out)


def solution(mesh):
    strip = P(None, ("wide", "narrow"), None)
    in_specs = (P(None, None, ("wide", "narrow"), None), strip, strip, strip, strip, P())
    tile = P(None, "wide", "narrow")
    out_specs = (P(None, None, ("wide", "narrow"), None), tile, tile)
    return jax.shard_map(local, mesh=mesh, in_specs=in_specs, out_specs=out_specs, check_vma=False)
```

```python
import functools

import jax
import jax.numpy as jnp
import numpy as np
from jax import lax
from jax.experimental import pallas as pl
from jax.experimental.pallas import tpu as pltpu
from jax.sharding import PartitionSpec as P

LBM_STEPS = 4
F32 = jnp.float32

DIRS = [
    (0, 0, 0), (1, 0, 0), (-1, 0, 0), (0, 1, 0), (0, -1, 0), (0, 0, 1), (0, 0, -1),
    (1, 1, 0), (-1, -1, 0), (1, -1, 0), (-1, 1, 0), (1, 0, 1), (-1, 0, -1), (1, 0, -1),
    (-1, 0, 1), (0, 1, 1), (0, -1, -1), (0, 1, -1), (0, -1, 1),
]
OPP = [0, 2, 1, 4, 3, 6, 5, 8, 7, 10, 9, 12, 11, 14, 13, 16, 15, 18, 17]
UP = [1, 7, 9, 11, 13]
DOWN = [2, 8, 10, 12, 14]
DIFFUSION = 0.15
TRANSFER = 0.3
DEPLETION = 0.5
FLOOR = 0.3
SUBS = 8
LANES = 128
VMEM_LIMIT = 16 * 1024 * 1024


def to_view(array):
    *lead, rows, width = array.shape
    n = len(lead)
    t = array.reshape(*lead, rows // SUBS, SUBS, width // LANES, LANES)
    t = t.transpose(*range(n), n, n + 2, n + 1, n + 3)
    return t.reshape(*lead[:-1], lead[-1] * rows * width // LANES, LANES)


def from_view(view, shape):
    *lead, rows, width = shape
    n = len(lead)
    t = view.reshape(*lead, rows // SUBS, width // LANES, SUBS, LANES)
    t = t.transpose(*range(n), n, n + 2, n + 1, n + 3)
    return t.reshape(shape)


def iotas():
    lane = lax.broadcasted_iota(jnp.int32, (SUBS, LANES), 1)
    sub = lax.broadcasted_iota(jnp.int32, (SUBS, LANES), 0)
    return lane, sub


def cut(c):
    return slice(c * LANES, (c + 1) * LANES)


def strided(tiles, c, x):
    return pl.ds(c * SUBS + x, SUBS, stride=tiles * SUBS)


def collide(f, fac):
    s = [f[2 * p + 1] + f[2 * p + 2] for p in range(9)]
    d = [f[2 * p + 1] - f[2 * p + 2] for p in range(9)]
    rho = f[0] + (((s[0] + s[1]) + (s[2] + s[3])) + ((s[4] + s[5]) + (s[6] + s[7])) + s[8])
    jx = d[0] + ((d[3] + d[4]) + (d[5] + d[6]))
    jy = d[1] + ((d[3] - d[4]) + (d[7] + d[8]))
    jz = d[2] + ((d[5] - d[6]) + (d[7] - d[8]))
    inv = fac / rho
    vx, vy, vz = jx * inv, jy * inv, jz * inv
    w1 = rho * np.float32(1.25 / 18)
    w2 = rho * np.float32(1.25 / 36)
    w4 = rho * np.float32(1.25 / 72)
    a1 = w1 - w1 * ((vx * vx + vy * vy + vz * vz) * np.float32(1.0 / 6))
    a2 = a1 * np.float32(0.5)
    post = [a1 * np.float32(6.0) - f[0] * np.float32(0.25)]
    axes = [vx, vy, vz, vx + vy, vx - vy, vx + vz, vx - vz, vy + vz, vy - vz]
    for p, v in enumerate(axes):
        wa, wh, base = (w1, w2, a1) if p < 3 else (w2, w4, a2)
        even = (base + (wh * v) * v) - s[p] * np.float32(0.125)
        odd = wa * v - d[p] * np.float32(0.125)
        post += [even + odd, even - odd]
    return post


def pull(load, q, c, tiles, halves, lane, sub):
    _, cross, layer = DIRS[q]
    v = load(q, c)
    if cross == 1:
        if c > 0:
            side = load(q, c - 1)
        else:
            side = jnp.where(sub % halves == 0, jnp.nan, pltpu.roll(load(q, tiles - 1), 1, 0))
        v = pltpu.roll(jnp.where(lane == LANES - 1, side, v), 1, 1)
    elif cross == -1:
        if c < tiles - 1:
            side = load(q, c + 1)
        else:
            side = jnp.where(sub % halves == halves - 1, jnp.nan, pltpu.roll(load(q, 0), SUBS - 1, 0))
        v = pltpu.roll(jnp.where(lane == 0, side, v), LANES - 1, 1)
    if layer:
        v = pltpu.roll(v, (layer * halves) % SUBS, 0)
    return v


def stream(g, lo, hi, x, c, tiles, halves, lane, sub, place):
    def load(q, cc):
        flow = DIRS[q][0]
        if flow == 1 and place == "first":
            return lo[UP.index(q), :, cut(cc)]
        if flow == -1 and place == "last":
            return hi[DOWN.index(q), :, cut(cc)]
        return g[q, x - flow, :, cut(cc)]

    f = [g[0, x, :, cut(c)]]
    for q in range(1, 19):
        v = pull(load, q, c, tiles, halves, lane, sub)
        f.append(jnp.where(v != v, g[OPP[q], x, :, cut(c)], v))
    return f


def drag(ph):
    return jnp.where(ph == 2, jnp.nan, jnp.where(ph == 1, np.float32(1.5), np.float32(3.0)))


def swap_tile(v, sub):
    v = list(v)
    for k in (4, 2, 1):
        low = sub & k == 0
        for i in range(SUBS):
            if not i & k:
                a, b = v[i], v[i + k]
                v[i] = jnp.where(low, a, pltpu.roll(b, k, 0))
                v[i + k] = jnp.where(low, pltpu.roll(a, SUBS - k, 0), b)
    return v


def upper(chain):
    odd = lax.rem(lax.axis_index("narrow"), 2) == 1
    return odd if chain else jnp.logical_not(odd)


def by_side(chain, side):
    pl.when(upper(chain))(lambda: side(True))
    pl.when(jnp.logical_not(upper(chain)))(lambda: side(False))


def pick(flag, a, b):
    return [jnp.where(flag, x, y) for x, y in zip(a, b)]


def start_face(tiles, chain, pop, phase, conc, poro, row, send):
    up = upper(chain)
    x = jnp.where(up, SUBS - 1, 0)
    beside = jnp.where(up, SUBS - 2, 1)
    for c in range(tiles):
        at = strided(tiles, c, x)
        post = collide([pop[q, at, :] for q in range(19)], drag(phase[at, :]))
        for q in range(19):
            row[q, :, cut(c)] = post[q]
        for i in range(5):
            send[i, :, cut(c)] = jnp.where(up, post[UP[i]], post[DOWN[i]])
        send[5, :, cut(c)] = conc[at, :]
        send[6, :, cut(c)] = conc[strided(tiles, c, beside), :]
        send[7, :, cut(c)] = poro[at, :]


def first_kernel(
    tiles, pop_h, phase_h, conc_h, napl_h, poro_h, flags_h,
    pop, phase, conc, napl, poro, flags, row, send, sems,
):
    small = [
        pltpu.make_async_copy(a, b, sems.at[i])
        for i, (a, b) in enumerate(
            ((phase_h, phase), (conc_h, conc), (poro_h, poro), (napl_h, napl), (flags_h, flags))
        )
    ]
    large = pltpu.make_async_copy(pop_h, pop, sems.at[len(small)])
    large.start()
    for copy in small:
        copy.start()
    for copy in small:
        copy.wait()
    large.wait()
    start_face(tiles, 0, pop, phase, conc, poro, row, send)


def second_kernel(tiles, pop, phase, conc, poro, after, row, send):
    start_face(tiles, 1, pop, phase, conc, poro, row, send)


def merge_rows(out, row0, row1, count):
    rows = out.shape[1]

    def side(up):
        for k in range(count):
            out[k, 0] = (row0 if up else row1)[k]
            out[k, rows - 1] = (row1 if up else row0)[k]

    by_side(1, side)


def first_inner_kernel(
    tiles, halves, pop, phase, conc, napl, poro, flags, row0, row1, g, fac, start, slabs, open_ends
):
    rows = g.shape[1]
    length = tiles * LANES
    _, sub = iotas()

    def to_slabs(read, write):
        for c in range(tiles):
            v = [read(pl.ds((i * tiles + c) * SUBS, SUBS)) for i in range(SUBS)]
            for x, t in enumerate(swap_tile(v, sub)):
                write(x, cut(c), t)

    def store(ref, k):
        def write(x, at, t):
            ref[k, x, :, at] = t

        return write

    def store_fac(x, at, t):
        fac[x, :, at] = t

    to_slabs(lambda at: drag(phase[at, :]), store_fac)

    def direction(q, _):
        to_slabs(lambda at: pop[q, at, :], store(start, q))
        return 0

    lax.fori_loop(0, 19, direction, 0)

    def row(x, _):
        for c in range(tiles):
            post = collide([start[q, x, :, cut(c)] for q in range(19)], fac[x, :, cut(c)])
            for q in range(19):
                g[q, x, :, cut(c)] = post[q]
        return 0

    lax.fori_loop(1, rows - 1, row, 0)
    merge_rows(g, row0, row1, 19)
    for k, ref in enumerate((conc, napl, poro)):
        to_slabs(lambda at, ref=ref: ref[at, :], store(slabs, k))
    for k in range(2):
        for z in range(SUBS // halves):
            for h in range(halves):
                line = flags[k, z : z + 1, h * length : (h + 1) * length]
                open_ends[k, z * halves + h : z * halves + h + 1, :] = line.astype(F32)


def edge_kernel(tiles, halves, chain, g, fac, halo, after, row, send):
    rows = g.shape[1]
    lane, sub = iotas()

    def side(up):
        x = rows - 1 if up else 0
        lo, hi, place = (None, halo, "last") if up else (halo, None, "first")
        for c in range(tiles):
            post = collide(stream(g, lo, hi, x, c, tiles, halves, lane, sub, place), fac[x, :, cut(c)])
            for q in range(19):
                row[q, :, cut(c)] = post[q]
            for i, q in enumerate(UP if up else DOWN):
                send[i, :, cut(c)] = post[q]

    by_side(chain, side)


def inner_kernel(tiles, halves, g, row0, row1, fac, out):
    rows = g.shape[1]
    lane, sub = iotas()

    def row(x, _):
        for c in range(tiles):
            f = stream(g, None, None, x, c, tiles, halves, lane, sub, "mid")
            post = collide(f, fac[x, :, cut(c)])
            for q in range(19):
                out[q, x, :, cut(c)] = post[q]
        return 0

    lax.fori_loop(1, rows - 1, row, 0)
    merge_rows(out, row0, row1, 19)


def speed(f, fc):
    s = [f[2 * p + 1] + f[2 * p + 2] for p in range(9)]
    d = [f[2 * p + 1] - f[2 * p + 2] for p in range(9)]
    rho = f[0] + (((s[0] + s[1]) + (s[2] + s[3])) + ((s[4] + s[5]) + (s[6] + s[7])) + s[8])
    jx = d[0] + ((d[3] + d[4]) + (d[5] + d[6]))
    jy = d[1] + ((d[3] - d[4]) + (d[7] + d[8]))
    jz = d[2] + ((d[5] - d[6]) + (d[7] - d[8]))
    inv = np.float32(1.0) / rho
    return [jnp.where(fc != fc, np.float32(0.0), j * inv) for j in (jz, jx, jy)]


def edge_speed_kernel(tiles, halves, chain, g, fac, halo, after, ue, send):
    rows = g.shape[1]
    lane, sub = iotas()

    def side(up):
        x = rows - 1 if up else 0
        lo, hi, place = (None, halo, "last") if up else (halo, None, "first")
        for c in range(tiles):
            f = stream(g, lo, hi, x, c, tiles, halves, lane, sub, place)
            for i, v in enumerate(speed(f, fac[x, :, cut(c)])):
                ue[i, :, cut(c)] = v
                if i == 1:
                    send[:, cut(c)] = v

    by_side(chain, side)


def inner_speed_kernel(tiles, halves, g, fac, u):
    rows = g.shape[1]
    lane, sub = iotas()
    for i in range(3):
        u[i, 0] = jnp.zeros(u.shape[2:], F32)
        u[i, rows - 1] = jnp.zeros(u.shape[2:], F32)

    def row(x, _):
        for c in range(tiles):
            f = stream(g, None, None, x, c, tiles, halves, lane, sub, "mid")
            for i, v in enumerate(speed(f, fac[x, :, cut(c)])):
                u[i, x, :, cut(c)] = v
        return 0

    lax.fori_loop(1, rows - 1, row, 0)


def final_kernel(tiles, halves, dirs, passed, aliased, *refs):
    g, fac, halo0, halo1, start = refs[:5]
    blocks = refs[5 : 5 + passed]
    out, *through = refs[6 + passed + aliased : 7 + 2 * passed + aliased]
    buf, sems = refs[7 + 2 * passed + aliased :]
    rows = g.shape[1]
    lane, sub = iotas()
    odd = upper(1)
    for a, b in zip(blocks, through):
        b[...] = a[...]

    def row_of(q, x):
        at = x - DIRS[q][0]
        if at < 0:
            return lambda qq, cc: jnp.where(
                odd, halo0[UP.index(qq), :, cut(cc)], halo1[UP.index(qq), :, cut(cc)]
            )
        if at >= rows:
            return lambda qq, cc: jnp.where(
                odd, halo1[DOWN.index(qq), :, cut(cc)], halo0[DOWN.index(qq), :, cut(cc)]
            )
        return lambda qq, cc: g[qq, at, :, cut(cc)]

    copies = []
    for n, q in enumerate(dirs):
        for c in range(tiles):
            new = []
            for x in range(rows):
                fc = fac[x, :, cut(c)]
                if q == 0:
                    v = g[0, x, :, cut(c)]
                else:
                    v = pull(row_of(q, x), q, c, tiles, halves, lane, sub)
                    v = jnp.where(v != v, g[OPP[q], x, :, cut(c)], v)
                new.append(jnp.where(fc != fc, start[q, x, :, cut(c)], v))
            for i, t in enumerate(swap_tile(new, sub)):
                first = (i * tiles + c) * SUBS
                buf[n, first : first + SUBS, :] = t
        copy = pltpu.make_async_copy(buf.at[n], out.at[q], sems.at[n])
        copy.start()
        copies.append(copy)
    for copy in copies:
        copy.wait()


def slope(p, q):
    return np.float32(0.5) * (
        jnp.maximum(jnp.minimum(p, q), np.float32(0.0)) + jnp.minimum(jnp.maximum(p, q), np.float32(0.0))
    )


def loss(s, c):
    return [np.float32(TRANSFER) * a * (np.float32(1.0) - b) for a, b in zip(s, c)]


def ends_of(parts, strips):
    place = lax.axis_index("wide") * parts + lax.axis_index("narrow")
    return place == 0, place == strips - 1


class Row:
    def __init__(self, tiles, halves):
        self.tiles, self.halves = tiles, halves
        self.lane, self.sub = iotas()

    def read(self, slab):
        return [slab[:, cut(c)] for c in range(self.tiles)]

    def after(self, v):
        out = []
        for c in range(self.tiles):
            if c < self.tiles - 1:
                side = v[c + 1]
            else:
                edge = self.sub % self.halves == self.halves - 1
                side = jnp.where(edge, np.float32(0.0), pltpu.roll(v[0], SUBS - 1, 0))
            out.append(pltpu.roll(jnp.where(self.lane == 0, side, v[c]), LANES - 1, 1))
        return out

    def before(self, v):
        out = []
        for c in range(self.tiles):
            if c > 0:
                side = v[c - 1]
            else:
                edge = self.sub % self.halves == 0
                side = jnp.where(edge, np.float32(0.0), pltpu.roll(v[self.tiles - 1], 1, 0))
            out.append(pltpu.roll(jnp.where(self.lane == LANES - 1, side, v[c]), 1, 1))
        return out

    def above(self, v):
        return [pltpu.roll(t, SUBS - self.halves, 0) for t in v]

    def below(self, v):
        return [pltpu.roll(t, self.halves, 0) for t in v]

    def step(self, r, conc, poro, flow, u, s):
        def each(f, *lists):
            return [f(*t) for t in zip(*lists)]

        def less(a, b):
            return each(lambda x, y: x - y, a, b)

        def times(a, b):
            return each(lambda x, y: x * y, a, b)

        def slopes(a, b):
            return each(slope, a, b)

        def face(w, va, vb, c, cn, sl, sn, dn):
            a = each(lambda w, x, y: w * np.float32(0.5) * (x + y), w, va, vb)
            return each(
                lambda a, w, c, cn, sl, sn, dn: a * jnp.where(a > 0, c + sl, cn - sn)
                - np.float32(DIFFUSION) * w * dn,
                a, w, c, cn, sl, sn, dn,
            )

        cm2, cm1, c, cp1, cp2 = (conc(r + k) for k in (-2, -1, 0, 1, 2))
        pm, p, pn = (poro(r + k) for k in (-1, 0, 1))
        vm, v0, vn = (flow(r + k) for k in (-1, 0, 1))
        d0, d1, d2, d3 = less(cm1, cm2), less(c, cm1), less(cp1, c), less(cp2, cp1)
        sm, s0, sp = slopes(d0, d1), slopes(d1, d2), slopes(d2, d3)
        change = less(
            face(times(pm, p), vm, v0, cm1, c, sm, s0, d1), face(times(p, pn), v0, vn, c, cp1, s0, sp, d2)
        )
        for after, before, vel, open_ends in (
            (self.after, self.before, u[1], True), (self.above, self.below, u[0], False),
        ):
            cn = after(c)
            dn = less(cn, c)
            dm = less(c, before(c)) if open_ends else before(dn)
            s0 = slopes(dm, dn)
            flux = face(times(p, after(p)), vel, after(vel), c, cn, s0, after(s0), dn)
            change = each(lambda t, a, b: t + (a - b), change, before(flux), flux)
        rate = loss(s, c)
        cnew = each(
            lambda c, t, k, p: c + (t + k) / jnp.maximum(p, np.float32(FLOOR)), c, change, rate, p
        )
        return cnew, each(lambda s, k: s - np.float32(DEPLETION) * k, s, rate)


ZERO = np.float32(0.0)


def early_kernel(tiles, halves, ends, slabs, still0, still1, inner_u, ue0, ue1, flags, cs, u):
    rows = u.shape[1]
    row = Row(tiles, halves)
    first, last = ends_of(*ends)
    odd = upper(1)
    for k in range(3):
        for r in range(1, rows - 1):
            u[k, r] = inner_u[k, r]
    merge_rows(u, ue0, ue1, 3)

    def conc(r):
        if r < 0:
            return pick(first, [ZERO] * tiles, pick(odd, row.read(still0.at[5]), row.read(still1.at[5])))
        if r >= rows:
            beyond = pick(odd, row.read(still1.at[5]), row.read(still0.at[5]))
            return pick(last, row.read(slabs.at[0, rows - 1]), beyond)
        return row.read(slabs.at[0, r])

    def poro(r):
        return row.read(slabs.at[2, r])

    def flow(r):
        return row.read(u.at[1, r])

    for r in range(1, rows - 1):
        new = row.step(r, conc, poro, flow, (row.read(u.at[0, r]), row.read(u.at[2, r])), row.read(slabs.at[1, r]))
        for k in range(2):
            for c in range(tiles):
                cs[k, r - 1, :, cut(c)] = new[k][c]


def side_step(row, ends, up, which, conc_at, beyond_c, napl_at, slabs, still, u, flags, beyond_u):
    rows = u.shape[1]
    first, last = ends_of(*ends)

    def conc(r):
        if r < 0:
            return pick(first, [ZERO] * row.tiles, row.read(beyond_c(-1 - r)))
        if r >= rows:
            return pick(last, row.read(conc_at(rows - 1)), row.read(beyond_c(r - rows)))
        return row.read(conc_at(r))

    def poro(r):
        if r < 0:
            return pick(first, row.read(flags.at[0]), row.read(still.at[7]))
        if r >= rows:
            return pick(last, row.read(flags.at[1]), row.read(still.at[7]))
        return row.read(slabs.at[2, r])

    def flow(r):
        if r < 0:
            return pick(first, row.read(u.at[1, 0]), row.read(beyond_u))
        if r >= rows:
            return pick(last, row.read(u.at[1, rows - 1]), row.read(beyond_u))
        return row.read(u.at[1, r])

    return [
        row.step(r, conc, poro, flow, (row.read(u.at[0, r]), row.read(u.at[2, r])), row.read(napl_at(r)))
        for r in which
    ]


def rim_kernel(tiles, halves, ends, chain, slabs, still, u, flags, beyond_u, inner, after, cs, send):
    rows = u.shape[1]
    row = Row(tiles, halves)

    def side(up):
        x = rows - 1 if up else 0
        ((c1, s1),) = side_step(
            row, ends, up, (x,), lambda r: slabs.at[0, r], lambda k: still.at[5 + k], lambda r: slabs.at[1, r],
            slabs, still, u, flags, beyond_u,
        )
        for c in range(tiles):
            cs[0, :, cut(c)] = c1[c]
            cs[1, :, cut(c)] = s1[c]
            send[0, :, cut(c)] = c1[c]
        send[1] = inner[0, rows - 3 if up else 0]

    by_side(chain, side)


def middle_kernel(tiles, halves, slabs, u, inner, rim0, rim1, out):
    rows = u.shape[1]
    row = Row(tiles, halves)
    odd = upper(1)

    def conc(r):
        if r == 0:
            return pick(odd, row.read(rim0.at[0]), row.read(rim1.at[0]))
        if r == rows - 1:
            return pick(odd, row.read(rim1.at[0]), row.read(rim0.at[0]))
        return row.read(inner.at[0, r - 1])

    for r in range(2, rows - 2):
        new = row.step(
            r, conc, lambda r: row.read(slabs.at[2, r]), lambda r: row.read(u.at[1, r]),
            (row.read(u.at[0, r]), row.read(u.at[2, r])), row.read(inner.at[1, r - 1]),
        )
        for c in range(tiles):
            out[r - 2, :, cut(c)] = new[0][c]


def late_kernel(tiles, halves, ends, chain, slabs, still, u, flags, beyond_u, inner, rim, beyond_c, after, out):
    rows = u.shape[1]
    row = Row(tiles, halves)

    def side(up):
        def state(k, r):
            return rim.at[k] if r in (0, rows - 1) else inner.at[k, r - 1]

        new = side_step(
            row, ends, up, (rows - 1, rows - 2) if up else (0, 1), lambda r: state(0, r),
            lambda k: beyond_c.at[k], lambda r: state(1, r), slabs, still, u, flags, beyond_u,
        )
        for i in range(2):
            for c in range(tiles):
                out[i, :, cut(c)] = new[i][0][c]

    by_side(chain, side)


def deal_kernel(tiles, halves, parts, inner, rim0, rim1, late0, late1, mid, *refs):
    *blocks, whole = refs
    rows = inner.shape[1] + 2
    odd = upper(1)
    _, sub = iotas()
    for c in range(tiles):

        def ends_pick(a, b):
            return jnp.where(odd, a, b)

        lo = [ends_pick(late0[i, :, cut(c)], late1[i, :, cut(c)]) for i in range(2)]
        hi = [ends_pick(late1[i, :, cut(c)], late0[i, :, cut(c)]) for i in range(2)]
        conc = lo + [mid[r, :, cut(c)] for r in range(rows - 4)] + hi[::-1]
        left = []
        for r in range(rows):
            if r in (0, rows - 1):
                a, b = (rim0, rim1) if r == 0 else (rim1, rim0)
                cc, ss = (ends_pick(a[k, :, cut(c)], b[k, :, cut(c)]) for k in range(2))
            else:
                cc, ss = (inner[k, r - 1, :, cut(c)] for k in range(2))
            left.append(ss - np.float32(DEPLETION) * loss([ss], [cc])[0])
        run = whole.shape[3]
        for k, tile in enumerate((conc, left)):
            for i, t in enumerate(swap_tile(tile, sub)):
                column = (i % halves * tiles + c) * SUBS
                at = column % run
                whole[column // run, k, i // halves, at : at + SUBS, :] = t
    for k in range(parts):
        blocks[k][...] = whole[lax.axis_index("narrow") ^ k]


def gather_kernel(parts, *refs):
    blocks = refs[:parts]
    *outs, sems = refs[parts:]
    copies = []
    for k in range(parts):
        origin = lax.axis_index("narrow") ^ k
        for i, out in enumerate(outs):
            copies.append(pltpu.make_async_copy(blocks[k].at[i], out.at[:, origin], sems.at[i * parts + k]))
            copies[-1].start()
    for copy in copies:
        copy.wait()


def call(kernel, out_shape, args, scratch=(), hbm=(), free=(), hbm_out=(), name=None, flops=0, aliases=None):
    def spec(i, hbm, free=()):
        return pl.BlockSpec(memory_space=pltpu.HBM if i in hbm else pl.ANY if i in free else pltpu.VMEM)

    single = not isinstance(out_shape, tuple)
    shapes = (out_shape,) if single else out_shape
    out = pl.pallas_call(
        kernel,
        out_shape=shapes,
        in_specs=[spec(i, hbm, free) for i in range(len(args))],
        out_specs=tuple(spec(i, hbm_out) for i in range(len(shapes))),
        scratch_shapes=list(scratch),
        name=name,
        input_output_aliases=aliases or {},
        compiler_params=pltpu.CompilerParams(vmem_limit_bytes=VMEM_LIMIT),
        cost_estimate=pl.CostEstimate(flops=flops, bytes_accessed=flops // 10, transcendentals=0),
    )(*args)
    return out[0] if single else out


def local(populations, phase, porosity, napl, concentration, flags):
    layers, rows, width = phase.shape
    halves = SUBS // layers
    length = width // halves
    tiles = length // LANES
    parts = lax.axis_size("narrow")
    strips = lax.axis_size("wide") * parts
    both = ("wide", "narrow")
    pairs = (
        [(i, i ^ 1) for i in range(strips)],
        [(i, (i + 1 if i % 2 else i - 1) % strips) for i in range(strips)],
    )
    cells = rows * SUBS * length
    slab = (SUBS, length)
    ends = (parts, strips)
    run = width // LANES * SUBS // parts

    def hold(*shape, dtype=F32):
        return pltpu.VMEM(shape, dtype)

    def swap(chain, array):
        return lax.ppermute(array, both, pairs[chain])

    pop = to_view(populations)
    views = [to_view(a) for a in (phase, concentration, napl, porosity)]
    flat = views[0].shape
    given = [pltpu.with_memory_space_constraint(a, pltpu.HBM) for a in (pop, *views, flags)]
    popv, phv, cov, nav, pov, flv, row0, send = call(
        functools.partial(first_kernel, tiles),
        (
            hold(*pop.shape), hold(*flat, dtype=jnp.int32), hold(*flat), hold(*flat), hold(*flat),
            hold(*flags.shape, dtype=jnp.int32), hold(19, *slab), hold(8, *slab),
        ),
        given, scratch=(pltpu.SemaphoreType.DMA((6,)),), hbm=range(6), name="first", flops=50 * cells,
    )
    halo0 = still0 = swap(0, send)
    row1, send = call(
        functools.partial(second_kernel, tiles), (hold(19, *slab), hold(8, *slab)),
        (popv, phv, cov, pov, send), free=(4,), name="second", flops=30 * cells,
    )
    halo1 = still1 = swap(1, send)
    g, fac, start, slabs, open_ends = call(
        functools.partial(first_inner_kernel, tiles, halves),
        (
            hold(19, rows, *slab), hold(rows, *slab), hold(19, rows, *slab), hold(3, rows, *slab),
            hold(2, *slab),
        ),
        (popv, phv, cov, nav, pov, flv, row0, row1), name="first_inner", flops=300 * cells,
    )
    for _ in range(1, LBM_STEPS):
        row0, send = call(
            functools.partial(edge_kernel, tiles, halves, 0), (hold(19, *slab), hold(5, *slab)),
            (g, fac, halo0, send), free=(3,), name="edge0", flops=30 * cells,
        )
        halo0 = swap(0, send)
        row1, send = call(
            functools.partial(edge_kernel, tiles, halves, 1), (hold(19, *slab), hold(5, *slab)),
            (g, fac, halo1, send), free=(3,), name="edge1", flops=30 * cells,
        )
        halo1 = swap(1, send)
        g = call(
            functools.partial(inner_kernel, tiles, halves), hold(19, rows, *slab),
            (g, row0, row1, fac), name="inner", flops=250 * cells,
        )
    inner_u = call(
        functools.partial(inner_speed_kernel, tiles, halves), hold(3, rows, *slab), (g, fac),
        name="inner_speed", flops=100 * cells,
    )
    ue0, send = call(
        functools.partial(edge_speed_kernel, tiles, halves, 0), (hold(3, *slab), hold(*slab)),
        (g, fac, halo0, inner_u), free=(3,), name="edge_speed0", flops=20 * cells,
    )
    far0 = swap(0, send)
    ue1, send = call(
        functools.partial(edge_speed_kernel, tiles, halves, 1), (hold(3, *slab), hold(*slab)),
        (g, fac, halo1, send), free=(3,), name="edge_speed1", flops=20 * cells,
    )
    far1 = swap(1, send)
    inner, u = call(
        functools.partial(early_kernel, tiles, halves, ends),
        (hold(2, rows - 2, *slab), hold(3, rows, *slab)),
        (slabs, still0, still1, inner_u, ue0, ue1, open_ends), name="early", flops=100 * cells,
    )
    rim0, send = call(
        functools.partial(rim_kernel, tiles, halves, ends, 0), (hold(2, *slab), hold(2, *slab)),
        (slabs, still0, u, open_ends, far0, inner, send), free=(6,), name="rim0", flops=20 * cells,
    )
    next0 = swap(0, send)
    rim1, send = call(
        functools.partial(rim_kernel, tiles, halves, ends, 1), (hold(2, *slab), hold(2, *slab)),
        (slabs, still1, u, open_ends, far1, inner, send), free=(6,), name="rim1", flops=20 * cells,
    )
    next1 = swap(1, send)
    mid = call(
        functools.partial(middle_kernel, tiles, halves), hold(rows - 4, *slab),
        (slabs, u, inner, rim0, rim1), name="middle", flops=60 * cells,
    )
    late0 = call(
        functools.partial(late_kernel, tiles, halves, ends, 0), hold(2, *slab),
        (slabs, still0, u, open_ends, far0, inner, rim0, next0, mid), free=(8,), name="late0", flops=30 * cells,
    )
    late1 = call(
        functools.partial(late_kernel, tiles, halves, ends, 1), hold(2, *slab),
        (slabs, still1, u, open_ends, far1, inner, rim1, next1, late0), free=(8,), name="late1", flops=30 * cells,
    )
    block = (2, layers, run, LANES)
    blocks = call(
        functools.partial(deal_kernel, tiles, halves, parts), tuple(hold(*block) for _ in range(parts)),
        (inner, rim0, rim1, late0, late1, mid),
        scratch=(pltpu.VMEM((parts, *block), F32),), name="deal", flops=20 * cells,
    )
    blocks = list(blocks)

    def send_blocks(ks):
        for k in ks:
            blocks[k] = lax.ppermute(blocks[k], "narrow", [(i, i ^ k) for i in range(parts)])

    groups = [[int(k) for k in ks] for ks in np.array_split(np.arange(parts - 1, 0, -1), 3)]
    send_blocks(groups[0])
    out = None
    for ks, dirs in ((groups[1], range(0, 10)), (groups[2], range(10, 19))):
        args = [g, fac, halo0, halo1, start, *(blocks[k] for k in ks), blocks[0]]
        n = len(args)
        if out is not None:
            args.append(out)
        out, *passed = call(
            functools.partial(final_kernel, tiles, halves, dirs, len(ks), int(out is not None)),
            (jax.ShapeDtypeStruct((19, *flat), F32), *(hold(*block) for _ in ks)),
            args,
            scratch=(pltpu.VMEM((len(dirs), *flat), F32), pltpu.SemaphoreType.DMA((len(dirs),))),
            hbm=(n,), free=(n - 1,), hbm_out=(0,), name="final", flops=200 * cells,
            aliases={n: 0} if out is not None else None,
        )
        for k, b in zip(ks, passed):
            blocks[k] = b
        send_blocks(ks)
    tile = (layers, parts, run, LANES)
    conc_out, napl_out = call(
        functools.partial(gather_kernel, parts),
        (jax.ShapeDtypeStruct(tile, F32), jax.ShapeDtypeStruct(tile, F32)),
        blocks, scratch=(pltpu.SemaphoreType.DMA((2 * parts,)),), hbm_out=(0, 1), name="gather", flops=10 * cells,
    )
    shape = (layers, rows * parts, width // parts)

    def tile_of(a):
        return from_view(a.reshape(layers * parts * run, LANES), shape)

    return from_view(out, populations.shape), tile_of(conc_out), tile_of(napl_out)


def solution(mesh):
    strip = P(None, ("wide", "narrow"), None)
    in_specs = (P(None, None, ("wide", "narrow"), None), strip, strip, strip, strip, P())
    tile = P(None, "wide", "narrow")
    out_specs = (P(None, None, ("wide", "narrow"), None), tile, tile)
    return jax.shard_map(local, mesh=mesh, in_specs=in_specs, out_specs=out_specs, check_vma=False)
```

```python
import functools

import jax
import jax.numpy as jnp
import numpy as np
from jax import lax
from jax.experimental import pallas as pl
from jax.experimental.pallas import tpu as pltpu
from jax.sharding import PartitionSpec as P

LBM_STEPS = 4
F32 = jnp.float32

DIRS = [
    (0, 0, 0), (1, 0, 0), (-1, 0, 0), (0, 1, 0), (0, -1, 0), (0, 0, 1), (0, 0, -1),
    (1, 1, 0), (-1, -1, 0), (1, -1, 0), (-1, 1, 0), (1, 0, 1), (-1, 0, -1), (1, 0, -1),
    (-1, 0, 1), (0, 1, 1), (0, -1, -1), (0, 1, -1), (0, -1, 1),
]
OPP = [0, 2, 1, 4, 3, 6, 5, 8, 7, 10, 9, 12, 11, 14, 13, 16, 15, 18, 17]
UP = [1, 7, 9, 11, 13]
DOWN = [2, 8, 10, 12, 14]
DIFFUSION = 0.15
TRANSFER = 0.3
DEPLETION = 0.5
FLOOR = 0.3
SUBS = 8
LANES = 128
VMEM_LIMIT = 16 * 1024 * 1024


def to_view(array):
    *lead, rows, width = array.shape
    n = len(lead)
    t = array.reshape(*lead, rows // SUBS, SUBS, width // LANES, LANES)
    t = t.transpose(*range(n), n, n + 2, n + 1, n + 3)
    return t.reshape(*lead[:-1], lead[-1] * rows * width // LANES, LANES)


def from_view(view, shape):
    *lead, rows, width = shape
    n = len(lead)
    t = view.reshape(*lead, rows // SUBS, width // LANES, SUBS, LANES)
    t = t.transpose(*range(n), n, n + 2, n + 1, n + 3)
    return t.reshape(shape)


def iotas():
    lane = lax.broadcasted_iota(jnp.int32, (SUBS, LANES), 1)
    sub = lax.broadcasted_iota(jnp.int32, (SUBS, LANES), 0)
    return lane, sub


def cut(c):
    return slice(c * LANES, (c + 1) * LANES)


def strided(tiles, c, x):
    return pl.ds(c * SUBS + x, SUBS, stride=tiles * SUBS)


def collide(f, fac):
    s = [f[2 * p + 1] + f[2 * p + 2] for p in range(9)]
    d = [f[2 * p + 1] - f[2 * p + 2] for p in range(9)]
    rho = f[0] + (((s[0] + s[1]) + (s[2] + s[3])) + ((s[4] + s[5]) + (s[6] + s[7])) + s[8])
    jx = d[0] + ((d[3] + d[4]) + (d[5] + d[6]))
    jy = d[1] + ((d[3] - d[4]) + (d[7] + d[8]))
    jz = d[2] + ((d[5] - d[6]) + (d[7] - d[8]))
    inv = fac / rho
    vx, vy, vz = jx * inv, jy * inv, jz * inv
    w1 = rho * np.float32(1.25 / 18)
    w2 = rho * np.float32(1.25 / 36)
    w4 = rho * np.float32(1.25 / 72)
    a1 = w1 - w1 * ((vx * vx + vy * vy + vz * vz) * np.float32(1.0 / 6))
    a2 = a1 * np.float32(0.5)
    post = [a1 * np.float32(6.0) - f[0] * np.float32(0.25)]
    axes = [vx, vy, vz, vx + vy, vx - vy, vx + vz, vx - vz, vy + vz, vy - vz]
    for p, v in enumerate(axes):
        wa, wh, base = (w1, w2, a1) if p < 3 else (w2, w4, a2)
        even = (base + (wh * v) * v) - s[p] * np.float32(0.125)
        odd = wa * v - d[p] * np.float32(0.125)
        post += [even + odd, even - odd]
    return post


def pull(load, q, c, tiles, halves, lane, sub):
    _, cross, layer = DIRS[q]
    v = load(q, c)
    if cross == 1:
        if c > 0:
            side = load(q, c - 1)
        else:
            side = jnp.where(sub % halves == 0, jnp.nan, pltpu.roll(load(q, tiles - 1), 1, 0))
        v = pltpu.roll(jnp.where(lane == LANES - 1, side, v), 1, 1)
    elif cross == -1:
        if c < tiles - 1:
            side = load(q, c + 1)
        else:
            side = jnp.where(sub % halves == halves - 1, jnp.nan, pltpu.roll(load(q, 0), SUBS - 1, 0))
        v = pltpu.roll(jnp.where(lane == 0, side, v), LANES - 1, 1)
    if layer:
        v = pltpu.roll(v, (layer * halves) % SUBS, 0)
    return v


def stream(g, lo, hi, x, c, tiles, halves, lane, sub, place):
    def load(q, cc):
        flow = DIRS[q][0]
        if flow == 1 and place == "first":
            return lo[UP.index(q), :, cut(cc)]
        if flow == -1 and place == "last":
            return hi[DOWN.index(q), :, cut(cc)]
        return g[q, x - flow, :, cut(cc)]

    f = [g[0, x, :, cut(c)]]
    for q in range(1, 19):
        v = pull(load, q, c, tiles, halves, lane, sub)
        f.append(jnp.where(v != v, g[OPP[q], x, :, cut(c)], v))
    return f


def drag(ph):
    return jnp.where(ph == 2, jnp.nan, jnp.where(ph == 1, np.float32(1.5), np.float32(3.0)))


def swap_tile(v, sub):
    v = list(v)
    for k in (4, 2, 1):
        low = sub & k == 0
        for i in range(SUBS):
            if not i & k:
                a, b = v[i], v[i + k]
                v[i] = jnp.where(low, a, pltpu.roll(b, k, 0))
                v[i + k] = jnp.where(low, pltpu.roll(a, SUBS - k, 0), b)
    return v


def upper(chain):
    odd = lax.rem(lax.axis_index("narrow"), 2) == 1
    return odd if chain else jnp.logical_not(odd)


def by_side(chain, side):
    pl.when(upper(chain))(lambda: side(True))
    pl.when(jnp.logical_not(upper(chain)))(lambda: side(False))


def pick(flag, a, b):
    return [jnp.where(flag, x, y) for x, y in zip(a, b)]


def start_face(tiles, chain, pop, phase, conc, poro, row, send):
    up = upper(chain)
    x = jnp.where(up, SUBS - 1, 0)
    beside = jnp.where(up, SUBS - 2, 1)
    for c in range(tiles):
        at = strided(tiles, c, x)
        post = collide([pop[q, at, :] for q in range(19)], drag(phase[at, :]))
        for q in range(19):
            row[q, :, cut(c)] = post[q]
        for i in range(5):
            send[i, :, cut(c)] = jnp.where(up, post[UP[i]], post[DOWN[i]])
        send[5, :, cut(c)] = conc[at, :]
        send[6, :, cut(c)] = conc[strided(tiles, c, beside), :]
        send[7, :, cut(c)] = poro[at, :]


def first_kernel(
    tiles, pop_h, phase_h, conc_h, napl_h, poro_h, flags_h,
    pop, phase, conc, napl, poro, flags, row, send, sems,
):
    small = [
        pltpu.make_async_copy(a, b, sems.at[i])
        for i, (a, b) in enumerate(
            ((phase_h, phase), (conc_h, conc), (poro_h, poro), (napl_h, napl), (flags_h, flags))
        )
    ]
    large = pltpu.make_async_copy(pop_h, pop, sems.at[len(small)])
    large.start()
    for copy in small:
        copy.start()
    for copy in small:
        copy.wait()
    large.wait()
    start_face(tiles, 0, pop, phase, conc, poro, row, send)


def second_kernel(tiles, pop, phase, conc, poro, after, row, send):
    start_face(tiles, 1, pop, phase, conc, poro, row, send)


def merge_rows(out, row0, row1, count):
    rows = out.shape[1]

    def side(up):
        for k in range(count):
            out[k, 0] = (row0 if up else row1)[k]
            out[k, rows - 1] = (row1 if up else row0)[k]

    by_side(1, side)


def first_inner_kernel(
    tiles, halves, pop, phase, conc, napl, poro, flags, row0, row1, g, fac, start, slabs, open_ends
):
    rows = g.shape[1]
    length = tiles * LANES
    _, sub = iotas()

    def to_slabs(read, write):
        for c in range(tiles):
            v = [read(pl.ds((i * tiles + c) * SUBS, SUBS)) for i in range(SUBS)]
            for x, t in enumerate(swap_tile(v, sub)):
                write(x, cut(c), t)

    def store(ref, k):
        def write(x, at, t):
            ref[k, x, :, at] = t

        return write

    def store_fac(x, at, t):
        fac[x, :, at] = t

    to_slabs(lambda at: drag(phase[at, :]), store_fac)

    def direction(q, _):
        to_slabs(lambda at: pop[q, at, :], store(start, q))
        return 0

    lax.fori_loop(0, 19, direction, 0)

    def row(x, _):
        for c in range(tiles):
            post = collide([start[q, x, :, cut(c)] for q in range(19)], fac[x, :, cut(c)])
            for q in range(19):
                g[q, x, :, cut(c)] = post[q]
        return 0

    lax.fori_loop(1, rows - 1, row, 0)
    merge_rows(g, row0, row1, 19)
    for k, ref in enumerate((conc, napl, poro)):
        to_slabs(lambda at, ref=ref: ref[at, :], store(slabs, k))
    for k in range(2):
        for z in range(SUBS // halves):
            for h in range(halves):
                line = flags[k, z : z + 1, h * length : (h + 1) * length]
                open_ends[k, z * halves + h : z * halves + h + 1, :] = line.astype(F32)


def edge_kernel(tiles, halves, chain, g, fac, halo, after, row, send):
    rows = g.shape[1]
    lane, sub = iotas()

    def side(up):
        x = rows - 1 if up else 0
        lo, hi, place = (None, halo, "last") if up else (halo, None, "first")
        for c in range(tiles):
            post = collide(stream(g, lo, hi, x, c, tiles, halves, lane, sub, place), fac[x, :, cut(c)])
            for q in range(19):
                row[q, :, cut(c)] = post[q]
            for i, q in enumerate(UP if up else DOWN):
                send[i, :, cut(c)] = post[q]

    by_side(chain, side)


def inner_kernel(tiles, halves, g, row0, row1, fac, out):
    rows = g.shape[1]
    lane, sub = iotas()

    def row(x, _):
        for c in range(tiles):
            f = stream(g, None, None, x, c, tiles, halves, lane, sub, "mid")
            post = collide(f, fac[x, :, cut(c)])
            for q in range(19):
                out[q, x, :, cut(c)] = post[q]
        return 0

    lax.fori_loop(1, rows - 1, row, 0)
    merge_rows(out, row0, row1, 19)


def speed(f, fc):
    s = [f[2 * p + 1] + f[2 * p + 2] for p in range(9)]
    d = [f[2 * p + 1] - f[2 * p + 2] for p in range(9)]
    rho = f[0] + (((s[0] + s[1]) + (s[2] + s[3])) + ((s[4] + s[5]) + (s[6] + s[7])) + s[8])
    jx = d[0] + ((d[3] + d[4]) + (d[5] + d[6]))
    jy = d[1] + ((d[3] - d[4]) + (d[7] + d[8]))
    jz = d[2] + ((d[5] - d[6]) + (d[7] - d[8]))
    inv = np.float32(1.0) / rho
    return [jnp.where(fc != fc, np.float32(0.0), j * inv) for j in (jz, jx, jy)]


def inner_speed_kernel(tiles, halves, g, fac, u):
    rows = g.shape[1]
    lane, sub = iotas()

    def row(x, _):
        for c in range(tiles):
            f = stream(g, None, None, x, c, tiles, halves, lane, sub, "mid")
            for i, v in enumerate(speed(f, fac[x, :, cut(c)])):
                u[i, x - 1, :, cut(c)] = v
        return 0

    lax.fori_loop(1, rows - 1, row, 0)


def final_kernel(tiles, halves, g, fac, halo0, halo1, start, after, out, buf, sems):
    rows = g.shape[1]
    lane, sub = iotas()
    odd = upper(1)

    def row_of(q, x):
        at = x - DIRS[q][0]
        if at < 0:
            return lambda qq, cc: jnp.where(
                odd, halo0[UP.index(qq), :, cut(cc)], halo1[UP.index(qq), :, cut(cc)]
            )
        if at >= rows:
            return lambda qq, cc: jnp.where(
                odd, halo1[DOWN.index(qq), :, cut(cc)], halo0[DOWN.index(qq), :, cut(cc)]
            )
        return lambda qq, cc: g[qq, at, :, cut(cc)]

    copies = []
    for q in range(19):
        for c in range(tiles):
            new = []
            for x in range(rows):
                fc = fac[x, :, cut(c)]
                if q == 0:
                    v = g[0, x, :, cut(c)]
                else:
                    v = pull(row_of(q, x), q, c, tiles, halves, lane, sub)
                    v = jnp.where(v != v, g[OPP[q], x, :, cut(c)], v)
                new.append(jnp.where(fc != fc, start[q, x, :, cut(c)], v))
            for i, t in enumerate(swap_tile(new, sub)):
                first = (i * tiles + c) * SUBS
                buf[q, first : first + SUBS, :] = t
        copy = pltpu.make_async_copy(buf.at[q], out.at[q], sems.at[q])
        copy.start()
        copies.append(copy)
    for copy in copies:
        copy.wait()


def slope(p, q):
    return np.float32(0.5) * (
        jnp.maximum(jnp.minimum(p, q), np.float32(0.0)) + jnp.minimum(jnp.maximum(p, q), np.float32(0.0))
    )


def loss(s, c):
    return [np.float32(TRANSFER) * a * (np.float32(1.0) - b) for a, b in zip(s, c)]


def ends_of(parts, strips):
    place = lax.axis_index("wide") * parts + lax.axis_index("narrow")
    return place == 0, place == strips - 1


ZERO = np.float32(0.0)


def each(f, *lists):
    return [f(*t) for t in zip(*lists)]


def less(a, b):
    return each(lambda x, y: x - y, a, b)


def times(a, b):
    return each(lambda x, y: x * y, a, b)


def face(w, va, vb, c, cn, sl, sn, dn):
    a = each(lambda w, x, y: w * np.float32(0.5) * (x + y), w, va, vb)
    return each(
        lambda a, w, c, cn, sl, sn, dn: a * jnp.where(a > 0, c + sl, cn - sn) - np.float32(DIFFUSION) * w * dn,
        a, w, c, cn, sl, sn, dn,
    )


def floored(p):
    return [jnp.maximum(t, np.float32(FLOOR)) for t in p]


class Step:
    def __init__(self, tiles, halves, conc, poro, flow, cross, napl):
        self.tiles, self.halves = tiles, halves
        self.lane, self.sub = iotas()
        self.conc, self.poro, self.flow = (self.keep(f) for f in (conc, poro, flow))
        self.cross, self.napl = cross, napl
        self.gap = self.keep(lambda r: less(self.conc(r + 1), self.conc(r)))
        self.lean = self.keep(lambda r: each(slope, self.gap(r - 1), self.gap(r)))

    @staticmethod
    def keep(f):
        seen = {}

        def get(r):
            if r not in seen:
                seen[r] = f(r)
            return seen[r]

        return get

    def after(self, v):
        out = []
        for c in range(self.tiles):
            if c < self.tiles - 1:
                side = v[c + 1]
            else:
                edge = self.sub % self.halves == self.halves - 1
                side = jnp.where(edge, ZERO, pltpu.roll(v[0], SUBS - 1, 0))
            out.append(pltpu.roll(jnp.where(self.lane == 0, side, v[c]), LANES - 1, 1))
        return out

    def before(self, v):
        out = []
        for c in range(self.tiles):
            if c > 0:
                side = v[c - 1]
            else:
                edge = self.sub % self.halves == 0
                side = jnp.where(edge, ZERO, pltpu.roll(v[self.tiles - 1], 1, 0))
            out.append(pltpu.roll(jnp.where(self.lane == LANES - 1, side, v[c]), 1, 1))
        return out

    def above(self, v):
        return [pltpu.roll(t, SUBS - self.halves, 0) for t in v]

    def below(self, v):
        return [pltpu.roll(t, self.halves, 0) for t in v]

    def flow_face(self, r):
        return face(
            times(self.poro(r), self.poro(r + 1)), self.flow(r), self.flow(r + 1), self.conc(r), self.conc(r + 1),
            self.lean(r), self.lean(r + 1), self.gap(r),
        )

    def run(self, r, low=True, high=True):
        c, p, s = self.conc(r), self.poro(r), self.napl(r)
        change = None
        if low:
            change = self.flow_face(r - 1)
        if high:
            out = self.flow_face(r)
            change = [-t for t in out] if change is None else less(change, out)
        vel = self.cross(r)
        for after, before, v, open_ends in (
            (self.after, self.before, vel[0], True), (self.above, self.below, vel[1], False),
        ):
            cn = after(c)
            dn = less(cn, c)
            dm = less(c, before(c)) if open_ends else before(dn)
            s0 = each(slope, dm, dn)
            flux = face(times(p, after(p)), v, after(v), c, cn, s0, after(s0), dn)
            change = each(lambda t, a, b: t + (a - b), change, before(flux), flux)
        rate = loss(s, c)
        cnew = each(lambda c, t, k, p: c + (t + k) / p, c, change, rate, floored(p))
        return cnew, each(lambda s, k: s - np.float32(DEPLETION) * k, s, rate)


def read(slab):
    return [slab[:, cut(c)] for c in range(slab.shape[1] // LANES)]


def write(slab, tiles):
    for c, t in enumerate(tiles):
        slab[:, cut(c)] = t


def early_kernel(tiles, halves, slabs, u, cs):
    rows = slabs.shape[1]
    step = Step(
        tiles, halves, lambda r: read(slabs.at[0, r]), lambda r: read(slabs.at[2, r]),
        lambda r: read(u.at[1, r - 1]), lambda r: (read(u.at[2, r - 1]), read(u.at[0, r - 1])),
        lambda r: read(slabs.at[1, r]),
    )
    for r in range(2, rows - 2):
        for k, v in enumerate(step.run(r)):
            write(cs.at[k, r - 2], v)


def static_readers(ends, up, slabs, still, flags):
    rows = slabs.shape[1]
    first, last = ends_of(*ends)

    def conc(r):
        if r < 0:
            return [jnp.where(first, ZERO, t) for t in read(still.at[4 - r])]
        if r >= rows:
            return pick(last, read(slabs.at[0, rows - 1]), read(still.at[5 + r - rows]))
        return read(slabs.at[0, r])

    def poro(r):
        if 0 <= r < rows:
            return read(slabs.at[2, r])
        return pick(last if up else first, read(flags.at[1 if up else 0]), read(still.at[7]))

    return conc, poro


def rim_kernel(tiles, halves, ends, chain, g, fac, halo, u, slabs, still, flags, after, ue, cs, send):
    rows = g.shape[1]
    lane, sub = iotas()

    def side(up):
        x, beside = (rows - 1, rows - 2) if up else (0, 1)
        lo, hi, place = (None, halo, "last") if up else (halo, None, "first")
        for c in range(tiles):
            f = stream(g, lo, hi, x, c, tiles, halves, lane, sub, place)
            for i, v in enumerate(speed(f, fac[x, :, cut(c)])):
                ue[i, :, cut(c)] = v
        conc, poro = static_readers(ends, up, slabs, still, flags)

        def vel(k, r):
            return read(ue.at[k] if r == x else u.at[k, r - 1])

        step = Step(
            tiles, halves, conc, poro, lambda r: vel(1, r), lambda r: (vel(2, r), vel(0, r)),
            lambda r: read(slabs.at[1, r]),
        )
        edge = step.run(x, low=up, high=not up)
        inward = step.run(beside)
        for i, new in enumerate((edge, inward)):
            for k in range(2):
                write(cs.at[i, k], new[k])
            write(send.at[1 + i], new[0])
        send[0] = ue[1]

    by_side(chain, side)


def state_reader(rows, edge, inner, rims):
    def state(k, r):
        if r in (0, rows - 1):
            return edge(k, r)
        if r in (1, rows - 2):
            return rims(k, r)
        return read(inner.at[k, r - 2])

    return state


def middle_kernel(tiles, halves, slabs, u, inner, rim0, rim1, out):
    rows = slabs.shape[1]
    odd = upper(1)

    def rims(k, r):
        a, b = (rim0, rim1) if r == 1 else (rim1, rim0)
        return pick(odd, read(a.at[1, k]), read(b.at[1, k]))

    state = state_reader(rows, None, inner, rims)
    step = Step(
        tiles, halves, lambda r: state(0, r), lambda r: read(slabs.at[2, r]), lambda r: read(u.at[1, r - 1]),
        lambda r: (read(u.at[2, r - 1]), read(u.at[0, r - 1])), lambda r: state(1, r),
    )
    for r in range(3, rows - 3):
        write(out.at[r - 3], step.run(r)[0])


def late_kernel(
    tiles, halves, ends, chain, slabs, u, ue, inner, rim, still, flags, there, after, out
):
    rows = slabs.shape[1]
    first, last = ends_of(*ends)

    def side(up):
        x = rows - 1 if up else 0
        beyond = rows if up else -1
        ghost = last if up else first
        conc, poro = static_readers(ends, up, slabs, still, flags)

        def vel(k, r):
            if r == beyond:
                return pick(ghost, read(ue.at[1]), read(there.at[0]))
            return read(ue.at[k] if r == x else u.at[k, r - 1])

        def cross(r):
            return vel(2, r), vel(0, r)

        one = Step(tiles, halves, conc, poro, lambda r: vel(1, r), cross, None)
        flux = one.flow_face(x if up else -1)
        sign = np.float32(-1.0 if up else 1.0)
        edge = each(lambda c, f, p: c + sign * f / p, read(rim.at[0, 0]), flux, floored(poro(x)))
        outer = each(lambda c, f, p: c - sign * f / p, read(there.at[1]), flux, floored(poro(beyond)))
        second = read(there.at[2])
        if up:
            outer, second = pick(ghost, edge, outer), pick(ghost, edge, second)
        else:
            outer, second = ([jnp.where(ghost, ZERO, t) for t in v] for v in (outer, second))
        state = state_reader(
            rows, lambda k, r: read(rim.at[0, k]) if k else edge, inner, lambda k, r: read(rim.at[1, k])
        )

        def after_one(r):
            if r < 0 or r >= rows:
                return outer if r == beyond else second
            return state(0, r)

        two = Step(tiles, halves, after_one, poro, lambda r: vel(1, r), cross, lambda r: state(1, r))
        for i in range(3):
            new = two.run(rows - 1 - i if up else i)
            write(out.at[i], new[0])
            if i == 0:
                write(out.at[3], new[1])

    by_side(chain, side)


def place_of(parts):
    me = lax.axis_index("narrow")
    odd = lax.rem(lax.axis_index("wide"), 2) == 1
    late = jnp.where(odd, parts - 1, 0)
    return late, me == late, jnp.where(odd, me, me - 1), jnp.where(odd, 0, 1)


def deal_kernel(tiles, halves, parts, inner, rim0, rim1, late0, late1, mid, *refs):
    *blocks, whole = refs
    rows = inner.shape[1] + 4
    odd = upper(1)
    _, sub = iotas()
    for c in range(tiles):

        def ends_pick(a, b):
            return jnp.where(odd, a, b)

        lo = [ends_pick(late0[i, :, cut(c)], late1[i, :, cut(c)]) for i in range(4)]
        hi = [ends_pick(late1[i, :, cut(c)], late0[i, :, cut(c)]) for i in range(4)]
        conc = lo[:3] + [mid[r, :, cut(c)] for r in range(rows - 6)] + hi[2::-1]
        left = [lo[3]]
        for r in range(1, rows - 1):
            if r in (1, rows - 2):
                a, b = (rim0, rim1) if r == 1 else (rim1, rim0)
                cc, ss = (ends_pick(a[1, k, :, cut(c)], b[1, k, :, cut(c)]) for k in range(2))
            else:
                cc, ss = (inner[k, r - 2, :, cut(c)] for k in range(2))
            left.append(ss - np.float32(DEPLETION) * loss([ss], [cc])[0])
        left.append(hi[3])
        run = whole.shape[3]
        for k, tile in enumerate((conc, left)):
            for i, t in enumerate(swap_tile(tile, sub)):
                column = (i % halves * tiles + c) * SUBS
                at = column % run
                whole[column // run, k, i // halves, at : at + SUBS, :] = t
    late, is_late, place, base = place_of(parts)
    others = parts - 1
    blocks[0][...] = whole[lax.axis_index("narrow")]
    for k in range(1, others):
        blocks[k][...] = whole[base + lax.rem(place + k + others, others)]
    for k in range(others):
        blocks[others + k][...] = whole[jnp.where(is_late, base + k, late)]


def gather_kernel(parts, *refs):
    *blocks, conc, napl, sems = refs
    late, is_late, place, base = place_of(parts)
    others = parts - 1

    def copies(k, origin):
        return [
            pltpu.make_async_copy(blocks[k].at[i], out.at[:, origin], sems.at[i, k])
            for i, out in enumerate((conc, napl))
        ]

    moves = [(None, copies(0, lax.axis_index("narrow")))]
    for k in range(1, others):
        moves.append((jnp.logical_not(is_late), copies(k, base + lax.rem(place - k + 2 * others, others))))
    for k in range(others):
        moves.append((is_late | (place == k), copies(others + k, jnp.where(is_late, base + k, late))))
    for act in ("start", "wait"):
        for when, pair in moves:

            def go(pair=pair):
                for copy in pair:
                    getattr(copy, act)()

            if when is None:
                go()
            else:
                pl.when(when)(go)


def call(kernel, out_shape, args, scratch=(), hbm=(), free=(), hbm_out=(), name=None, flops=0, aliases=None):
    def spec(i, hbm, free=()):
        return pl.BlockSpec(memory_space=pltpu.HBM if i in hbm else pl.ANY if i in free else pltpu.VMEM)

    single = not isinstance(out_shape, tuple)
    shapes = (out_shape,) if single else out_shape
    out = pl.pallas_call(
        kernel,
        out_shape=shapes,
        in_specs=[spec(i, hbm, free) for i in range(len(args))],
        out_specs=tuple(spec(i, hbm_out) for i in range(len(shapes))),
        scratch_shapes=list(scratch),
        name=name,
        input_output_aliases=aliases or {},
        compiler_params=pltpu.CompilerParams(vmem_limit_bytes=VMEM_LIMIT),
        cost_estimate=pl.CostEstimate(flops=flops, bytes_accessed=flops // 10, transcendentals=0),
    )(*args)
    return out[0] if single else out


def local(populations, phase, porosity, napl, concentration, flags):
    layers, rows, width = phase.shape
    halves = SUBS // layers
    length = width // halves
    tiles = length // LANES
    parts = lax.axis_size("narrow")
    strips = lax.axis_size("wide") * parts
    both = ("wide", "narrow")
    pairs = (
        [(i, i ^ 1) for i in range(strips)],
        [(i, (i + 1 if i % 2 else i - 1) % strips) for i in range(strips)],
    )
    cells = rows * SUBS * length
    slab = (SUBS, length)
    ends = (parts, strips)
    run = width // LANES * SUBS // parts

    def hold(*shape, dtype=F32):
        return pltpu.VMEM(shape, dtype)

    def swap(chain, array):
        return lax.ppermute(array, both, pairs[chain])

    pop = to_view(populations)
    views = [to_view(a) for a in (phase, concentration, napl, porosity)]
    flat = views[0].shape
    given = [pltpu.with_memory_space_constraint(a, pltpu.HBM) for a in (pop, *views, flags)]
    popv, phv, cov, nav, pov, flv, row0, send = call(
        functools.partial(first_kernel, tiles),
        (
            hold(*pop.shape), hold(*flat, dtype=jnp.int32), hold(*flat), hold(*flat), hold(*flat),
            hold(*flags.shape, dtype=jnp.int32), hold(19, *slab), hold(8, *slab),
        ),
        given, scratch=(pltpu.SemaphoreType.DMA((6,)),), hbm=range(6), name="first", flops=50 * cells,
    )
    halo0 = still0 = swap(0, send)
    row1, send = call(
        functools.partial(second_kernel, tiles), (hold(19, *slab), hold(8, *slab)),
        (popv, phv, cov, pov, send), free=(4,), name="second", flops=30 * cells,
    )
    halo1 = still1 = swap(1, send)
    g, fac, start, slabs, open_ends = call(
        functools.partial(first_inner_kernel, tiles, halves),
        (
            hold(19, rows, *slab), hold(rows, *slab), hold(19, rows, *slab), hold(3, rows, *slab),
            hold(2, *slab),
        ),
        (popv, phv, cov, nav, pov, flv, row0, row1), name="first_inner", flops=300 * cells,
    )
    for _ in range(1, LBM_STEPS):
        row0, send = call(
            functools.partial(edge_kernel, tiles, halves, 0), (hold(19, *slab), hold(5, *slab)),
            (g, fac, halo0, send), free=(3,), name="edge0", flops=30 * cells,
        )
        halo0 = swap(0, send)
        row1, send = call(
            functools.partial(edge_kernel, tiles, halves, 1), (hold(19, *slab), hold(5, *slab)),
            (g, fac, halo1, send), free=(3,), name="edge1", flops=30 * cells,
        )
        halo1 = swap(1, send)
        g = call(
            functools.partial(inner_kernel, tiles, halves), hold(19, rows, *slab),
            (g, row0, row1, fac), name="inner", flops=250 * cells,
        )
    u = call(
        functools.partial(inner_speed_kernel, tiles, halves), hold(3, rows - 2, *slab), (g, fac),
        name="inner_speed", flops=100 * cells,
    )
    inner = call(
        functools.partial(early_kernel, tiles, halves), hold(2, rows - 4, *slab), (slabs, u),
        name="early", flops=60 * cells,
    )
    ue0, rim0, send = call(
        functools.partial(rim_kernel, tiles, halves, ends, 0), (hold(3, *slab), hold(2, 2, *slab), hold(3, *slab)),
        (g, fac, halo0, u, slabs, still0, open_ends, inner), free=(7,), name="rim0", flops=40 * cells,
    )
    there0 = swap(0, send)
    ue1, rim1, send = call(
        functools.partial(rim_kernel, tiles, halves, ends, 1), (hold(3, *slab), hold(2, 2, *slab), hold(3, *slab)),
        (g, fac, halo1, u, slabs, still1, open_ends, send), free=(7,), name="rim1", flops=40 * cells,
    )
    there1 = swap(1, send)
    mid = call(
        functools.partial(middle_kernel, tiles, halves), hold(rows - 6, *slab), (slabs, u, inner, rim0, rim1),
        name="middle", flops=40 * cells,
    )
    late0 = call(
        functools.partial(late_kernel, tiles, halves, ends, 0), hold(4, *slab),
        (slabs, u, ue0, inner, rim0, still0, open_ends, there0, mid), free=(8,), name="late0", flops=30 * cells,
    )
    late1 = call(
        functools.partial(late_kernel, tiles, halves, ends, 1), hold(4, *slab),
        (slabs, u, ue1, inner, rim1, still1, open_ends, there1, late0), free=(8,), name="late1", flops=30 * cells,
    )
    block = (2, layers, run, LANES)
    others = parts - 1
    blocks = call(
        functools.partial(deal_kernel, tiles, halves, parts), tuple(hold(*block) for _ in range(2 * others)),
        (inner, rim0, rim1, late0, late1, mid),
        scratch=(pltpu.VMEM((parts, *block), F32),), name="deal", flops=20 * cells,
    )
    came = [blocks[0]]
    rings, meets = [[] for _ in range(others)], [[] for _ in range(others)]
    for w in range(strips // parts):
        late, base = (parts - 1, 0) if w % 2 else (0, 1)
        for a in range(others):
            at = w * parts + base + a
            for k in range(1, others):
                rings[k].append((at, w * parts + base + (a + k) % others))
            meets[a] += [(at, w * parts + late), (w * parts + late, at)]
    for k in range(1, others):
        came.append(lax.ppermute(blocks[k], both, rings[k]))
    for k in range(others):
        came.append(lax.ppermute(blocks[others + k], both, meets[k]))
    out = call(
        functools.partial(final_kernel, tiles, halves), jax.ShapeDtypeStruct((19, *flat), F32),
        (g, fac, halo0, halo1, start, blocks[0]),
        scratch=(pltpu.VMEM((19, *flat), F32), pltpu.SemaphoreType.DMA((19,))),
        free=(5,), hbm_out=(0,), name="final", flops=400 * cells,
    )
    tile = (layers, parts, run, LANES)
    conc_out, napl_out = call(
        functools.partial(gather_kernel, parts),
        (jax.ShapeDtypeStruct(tile, F32), jax.ShapeDtypeStruct(tile, F32)),
        came, scratch=(pltpu.SemaphoreType.DMA((2, 2 * others)),), hbm_out=(0, 1), name="gather", flops=10 * cells,
    )
    shape = (layers, rows * parts, width // parts)

    def tile_of(a):
        return from_view(a.reshape(layers * parts * run, LANES), shape)

    return from_view(out, populations.shape), tile_of(conc_out), tile_of(napl_out)


def solution(mesh):
    strip = P(None, ("wide", "narrow"), None)
    in_specs = (P(None, None, ("wide", "narrow"), None), strip, strip, strip, strip, P())
    tile = P(None, "wide", "narrow")
    out_specs = (P(None, None, ("wide", "narrow"), None), tile, tile)
    return jax.shard_map(local, mesh=mesh, in_specs=in_specs, out_specs=out_specs, check_vma=False)
```

```python
import functools

import jax
import jax.numpy as jnp
import numpy as np
from jax import lax
from jax.experimental import pallas as pl
from jax.experimental.pallas import tpu as pltpu
from jax.sharding import PartitionSpec as P

LBM_STEPS = 4
F32 = jnp.float32

DIRS = [
    (0, 0, 0), (1, 0, 0), (-1, 0, 0), (0, 1, 0), (0, -1, 0), (0, 0, 1), (0, 0, -1),
    (1, 1, 0), (-1, -1, 0), (1, -1, 0), (-1, 1, 0), (1, 0, 1), (-1, 0, -1), (1, 0, -1),
    (-1, 0, 1), (0, 1, 1), (0, -1, -1), (0, 1, -1), (0, -1, 1),
]
OPP = [0, 2, 1, 4, 3, 6, 5, 8, 7, 10, 9, 12, 11, 14, 13, 16, 15, 18, 17]
UP = [1, 7, 9, 11, 13]
DOWN = [2, 8, 10, 12, 14]
DIFFUSION = 0.15
TRANSFER = 0.3
DEPLETION = 0.5
FLOOR = 0.3
SUBS = 8
LANES = 128
VMEM_LIMIT = 16 * 1024 * 1024


def to_view(array):
    *lead, rows, width = array.shape
    n = len(lead)
    t = array.reshape(*lead, rows // SUBS, SUBS, width // LANES, LANES)
    t = t.transpose(*range(n), n, n + 2, n + 1, n + 3)
    return t.reshape(*lead[:-1], lead[-1] * rows * width // LANES, LANES)


def from_view(view, shape):
    *lead, rows, width = shape
    n = len(lead)
    t = view.reshape(*lead, rows // SUBS, width // LANES, SUBS, LANES)
    t = t.transpose(*range(n), n, n + 2, n + 1, n + 3)
    return t.reshape(shape)


def iotas():
    lane = lax.broadcasted_iota(jnp.int32, (SUBS, LANES), 1)
    sub = lax.broadcasted_iota(jnp.int32, (SUBS, LANES), 0)
    return lane, sub


def cut(c):
    return slice(c * LANES, (c + 1) * LANES)


def strided(tiles, c, x):
    return pl.ds(c * SUBS + x, SUBS, stride=tiles * SUBS)


def collide(f, fac):
    s = [f[2 * p + 1] + f[2 * p + 2] for p in range(9)]
    d = [f[2 * p + 1] - f[2 * p + 2] for p in range(9)]
    rho = f[0] + (((s[0] + s[1]) + (s[2] + s[3])) + ((s[4] + s[5]) + (s[6] + s[7])) + s[8])
    jx = d[0] + ((d[3] + d[4]) + (d[5] + d[6]))
    jy = d[1] + ((d[3] - d[4]) + (d[7] + d[8]))
    jz = d[2] + ((d[5] - d[6]) + (d[7] - d[8]))
    inv = fac / rho
    vx, vy, vz = jx * inv, jy * inv, jz * inv
    w1 = rho * np.float32(1.25 / 18)
    w2 = rho * np.float32(1.25 / 36)
    w4 = rho * np.float32(1.25 / 72)
    a1 = w1 - w1 * ((vx * vx + vy * vy + vz * vz) * np.float32(1.0 / 6))
    a2 = a1 * np.float32(0.5)
    post = [a1 * np.float32(6.0) - f[0] * np.float32(0.25)]
    axes = [vx, vy, vz, vx + vy, vx - vy, vx + vz, vx - vz, vy + vz, vy - vz]
    for p, v in enumerate(axes):
        wa, wh, base = (w1, w2, a1) if p < 3 else (w2, w4, a2)
        even = (base + (wh * v) * v) - s[p] * np.float32(0.125)
        odd = wa * v - d[p] * np.float32(0.125)
        post += [even + odd, even - odd]
    return post


def pull(load, q, c, tiles, halves, lane, sub):
    _, cross, layer = DIRS[q]
    v = load(q, c)
    if cross == 1:
        if c > 0:
            side = load(q, c - 1)
        else:
            side = jnp.where(sub % halves == 0, jnp.nan, pltpu.roll(load(q, tiles - 1), 1, 0))
        v = pltpu.roll(jnp.where(lane == LANES - 1, side, v), 1, 1)
    elif cross == -1:
        if c < tiles - 1:
            side = load(q, c + 1)
        else:
            side = jnp.where(sub % halves == halves - 1, jnp.nan, pltpu.roll(load(q, 0), SUBS - 1, 0))
        v = pltpu.roll(jnp.where(lane == 0, side, v), LANES - 1, 1)
    if layer:
        v = pltpu.roll(v, (layer * halves) % SUBS, 0)
    return v


def stream(g, lo, hi, x, c, tiles, halves, lane, sub, place):
    def load(q, cc):
        flow = DIRS[q][0]
        if flow == 1 and place == "first":
            return lo[UP.index(q), :, cut(cc)]
        if flow == -1 and place == "last":
            return hi[DOWN.index(q), :, cut(cc)]
        return g[q, x - flow, :, cut(cc)]

    f = [g[0, x, :, cut(c)]]
    for q in range(1, 19):
        v = pull(load, q, c, tiles, halves, lane, sub)
        f.append(jnp.where(v != v, g[OPP[q], x, :, cut(c)], v))
    return f


def drag(ph):
    return jnp.where(ph == 2, jnp.nan, jnp.where(ph == 1, np.float32(1.5), np.float32(3.0)))


def swap_tile(v, sub):
    v = list(v)
    for k in (4, 2, 1):
        low = sub & k == 0
        for i in range(SUBS):
            if not i & k:
                a, b = v[i], v[i + k]
                v[i] = jnp.where(low, a, pltpu.roll(b, k, 0))
                v[i + k] = jnp.where(low, pltpu.roll(a, SUBS - k, 0), b)
    return v


def upper(chain):
    odd = lax.rem(lax.axis_index("narrow"), 2) == 1
    return odd if chain else jnp.logical_not(odd)


def by_side(chain, side):
    pl.when(upper(chain))(lambda: side(True))
    pl.when(jnp.logical_not(upper(chain)))(lambda: side(False))


def pick(flag, a, b):
    return [jnp.where(flag, x, y) for x, y in zip(a, b)]


def start_row(tiles, pop, phase, x, row, c):
    at = strided(tiles, c, x)
    fc = drag(phase[at, :])
    post = collide([pop[q, at, :] for q in range(19)], fc)
    for q in range(19):
        row[q, :, cut(c)] = post[q]
    return post, fc


def start_static(tiles, up, conc, poro, send, n):
    x, beside = jnp.where(up, SUBS - 1, 0), jnp.where(up, SUBS - 2, 1)
    for c in range(tiles):
        send[n, :, cut(c)] = conc[strided(tiles, c, x), :]
        send[n + 1, :, cut(c)] = conc[strided(tiles, c, beside), :]
        send[n + 2, :, cut(c)] = poro[strided(tiles, c, x), :]


def look_ahead(tiles, halves, up, edge, beside, send):
    lane, sub = iotas()
    toward, back = (UP, DOWN) if up else (DOWN, UP)
    for c in range(tiles):
        sums = [None] * 4
        for q in range(19):
            if q in back:
                continue
            if q == 0:
                f = edge(0, c)
            else:
                f = pull(beside if q in toward else edge, q, c, tiles, halves, lane, sub)
                f = jnp.where(f != f, edge(OPP[q], c), f)
            for k, e in enumerate((1, *DIRS[q])):
                if e:
                    t = f if e > 0 else -f
                    sums[k] = t if sums[k] is None else sums[k] + t
            if q in toward:
                i = toward.index(q)
                send[i, :, cut(c)] = edge(q, c)
                send[5 + i, :, cut(c)] = f
        for k in range(4):
            send[10 + k, :, cut(c)] = sums[k]


def first_kernel(
    tiles, halves, pop_h, phase_h, conc_h, napl_h, poro_h, flags_h,
    pop, phase, conc, napl, poro, flags, row, send, beside, sems,
):
    small = [
        pltpu.make_async_copy(a, b, sems.at[tiles + i])
        for i, (a, b) in enumerate(
            ((phase_h, phase), (conc_h, conc), (poro_h, poro), (napl_h, napl), (flags_h, flags))
        )
    ]
    large = [pltpu.make_async_copy(pop_h.at[:, :, c], pop.at[:, :, c], sems.at[c]) for c in range(tiles)]
    small[0].start()
    for copy in large + small[1:]:
        copy.start()
    flat = pop.reshape(pop.shape[0], SUBS * tiles * SUBS, LANES)
    up = upper(1)
    x, inwards = jnp.where(up, SUBS - 1, 0), jnp.where(up, SUBS - 2, 1)
    small[0].wait()
    for c in range(tiles):
        large[c].wait()
        _, fc = start_row(tiles, flat, phase, x, row, c)
        send[14, :, cut(c)] = fc
        start_row(tiles, flat, phase, inwards, beside, c)

    def side(up):
        look_ahead(
            tiles, halves, up, lambda q, c: row[q, :, cut(c)], lambda q, c: beside[q, :, cut(c)], send
        )

    by_side(1, side)
    for copy in small[1:]:
        copy.wait()
    start_static(tiles, up, conc, poro, send, 15)


def second_kernel(tiles, pop, phase, conc, poro, after, row, send):
    up = upper(0)
    x = jnp.where(up, SUBS - 1, 0)
    for c in range(tiles):
        post, _ = start_row(tiles, pop, phase, x, row, c)
        for i in range(5):
            send[i, :, cut(c)] = jnp.where(up, post[UP[i]], post[DOWN[i]])
    start_static(tiles, up, conc, poro, send, 5)


def merge_rows(out, row0, row1, count):
    rows = out.shape[1]

    def side(up):
        for k in range(count):
            out[k, 0] = (row0 if up else row1)[k]
            out[k, rows - 1] = (row1 if up else row0)[k]

    by_side(1, side)


def first_inner_kernel(
    tiles, halves, pop, phase, conc, napl, poro, flags, row0, row1, g, fac, start, slabs, open_ends
):
    rows = g.shape[1]
    length = tiles * LANES
    _, sub = iotas()

    def to_slabs(read, write):
        for c in range(tiles):
            v = [read(pl.ds((i * tiles + c) * SUBS, SUBS)) for i in range(SUBS)]
            for x, t in enumerate(swap_tile(v, sub)):
                write(x, cut(c), t)

    def store(ref, k):
        def write(x, at, t):
            ref[k, x, :, at] = t

        return write

    def store_fac(x, at, t):
        fac[x, :, at] = t

    to_slabs(lambda at: drag(phase[at, :]), store_fac)

    def direction(q, _):
        to_slabs(lambda at: pop[q, at, :], store(start, q))
        return 0

    lax.fori_loop(0, 19, direction, 0)

    def row(x, _):
        for c in range(tiles):
            post = collide([start[q, x, :, cut(c)] for q in range(19)], fac[x, :, cut(c)])
            for q in range(19):
                g[q, x, :, cut(c)] = post[q]
        return 0

    lax.fori_loop(1, rows - 1, row, 0)
    merge_rows(g, row0, row1, 19)
    for k, ref in enumerate((conc, napl, poro)):
        to_slabs(lambda at, ref=ref: ref[at, :], store(slabs, k))
    for k in range(2):
        for z in range(SUBS // halves):
            for h in range(halves):
                line = flags[k, z : z + 1, h * length : (h + 1) * length]
                open_ends[k, z * halves + h : z * halves + h + 1, :] = line.astype(F32)


def edge_kernel(tiles, halves, chain, g, fac, halo, after, row, send):
    rows = g.shape[1]
    lane, sub = iotas()

    def side(up):
        x = rows - 1 if up else 0
        lo, hi, place = (None, halo, "last") if up else (halo, None, "first")
        for c in range(tiles):
            post = collide(stream(g, lo, hi, x, c, tiles, halves, lane, sub, place), fac[x, :, cut(c)])
            for q in range(19):
                row[q, :, cut(c)] = post[q]
            for i, q in enumerate(UP if up else DOWN):
                send[i, :, cut(c)] = post[q]

    by_side(chain, side)


def inner_kernel(tiles, halves, g, fac, after, out):
    rows = g.shape[1]
    lane, sub = iotas()

    def row(x, _):
        for c in range(tiles):
            f = stream(g, None, None, x, c, tiles, halves, lane, sub, "mid")
            post = collide(f, fac[x, :, cut(c)])
            for q in range(19):
                out[q, x, :, cut(c)] = post[q]
        return 0

    lax.fori_loop(1, rows - 1, row, 0)


def put_kernel(inner, row0, row1, out):
    merge_rows(out, row0, row1, 19)


def arrive_kernel(tiles, halves, g, fac, halo, still, row0, after, inner, out, ghost):
    rows = g.shape[1]
    lane, sub = iotas()

    def side(up):
        x = rows - 1 if up else 0
        lo, hi, place = (None, halo, "last") if up else (halo, None, "first")
        toward, back = (DOWN, UP) if up else (UP, DOWN)
        for q in range(19):
            out[q, rows - 1 - x] = row0[q]
        for c in range(tiles):
            post = collide(stream(g, lo, hi, x, c, tiles, halves, lane, sub, place), fac[x, :, cut(c)])
            for q in range(19):
                out[q, x, :, cut(c)] = post[q]
            sums = [halo[10 + k, :, cut(c)] for k in range(4)]
            for i, q in enumerate(back):
                f = pull(lambda q, cc: g[q, x, :, cut(cc)], q, c, tiles, halves, lane, sub)
                f = jnp.where(f != f, halo[i, :, cut(c)], f)
                for k, e in enumerate((1, *DIRS[q])):
                    if e:
                        sums[k] = sums[k] + f if e > 0 else sums[k] - f
            rho = sums[0]
            inv = still[14, :, cut(c)] / rho
            v = [j * inv for j in sums[1:]]
            base = np.float32(1.0) - (v[0] * v[0] + v[1] * v[1] + v[2] * v[2]) * np.float32(1.0 / 6)
            for i, q in enumerate(toward):
                along = None
                for e, t in zip(DIRS[q], v):
                    if e:
                        t = t if e > 0 else -t
                        along = t if along is None else along + t
                weight = np.float32(1.25 / 18 if sum(map(abs, DIRS[q])) == 1 else 1.25 / 36)
                feq = (rho * weight) * (base + along * (along * np.float32(0.5) + np.float32(1.0)))
                ghost[i, :, cut(c)] = feq - halo[5 + i, :, cut(c)] * np.float32(0.25)

    by_side(1, side)


def far_kernel(tiles, halves, g, fac, halo, row, send, beside):
    rows = g.shape[1]
    lane, sub = iotas()

    def side(up):
        x, inwards = (rows - 1, rows - 2) if up else (0, 1)
        lo, hi, place = (None, halo, "last") if up else (halo, None, "first")
        for c in range(tiles):
            for at, ref, where in ((x, row, place), (inwards, beside, "mid")):
                f = stream(g, lo, hi, at, c, tiles, halves, lane, sub, where)
                post = collide(f, fac[at, :, cut(c)])
                for q in range(19):
                    ref[q, :, cut(c)] = post[q]
        look_ahead(
            tiles, halves, up, lambda q, c: row[q, :, cut(c)], lambda q, c: beside[q, :, cut(c)], send
        )

    by_side(1, side)


def speed(f, fc):
    s = [f[2 * p + 1] + f[2 * p + 2] for p in range(9)]
    d = [f[2 * p + 1] - f[2 * p + 2] for p in range(9)]
    rho = f[0] + (((s[0] + s[1]) + (s[2] + s[3])) + ((s[4] + s[5]) + (s[6] + s[7])) + s[8])
    jx = d[0] + ((d[3] + d[4]) + (d[5] + d[6]))
    jy = d[1] + ((d[3] - d[4]) + (d[7] + d[8]))
    jz = d[2] + ((d[5] - d[6]) + (d[7] - d[8]))
    inv = np.float32(1.0) / rho
    return [jnp.where(fc != fc, np.float32(0.0), j * inv) for j in (jz, jx, jy)]


def inner_speed_kernel(tiles, halves, g, fac, after, u):
    rows = g.shape[1]
    lane, sub = iotas()

    def row(x, _):
        for c in range(tiles):
            f = stream(g, None, None, x, c, tiles, halves, lane, sub, "mid")
            for i, v in enumerate(speed(f, fac[x, :, cut(c)])):
                u[i, x - 2, :, cut(c)] = v
        return 0

    lax.fori_loop(2, rows - 2, row, 0)


def final_kernel(tiles, halves, g, fac, halo0, halo1, start, after, out, token, buf, sems):
    rows = g.shape[1]
    lane, sub = iotas()
    odd = upper(1)
    token[...] = jnp.zeros(token.shape, F32)

    def row_of(q, x):
        at = x - DIRS[q][0]
        if at < 0:
            return lambda qq, cc: jnp.where(
                odd, halo0[UP.index(qq), :, cut(cc)], halo1[UP.index(qq), :, cut(cc)]
            )
        if at >= rows:
            return lambda qq, cc: jnp.where(
                odd, halo1[DOWN.index(qq), :, cut(cc)], halo0[DOWN.index(qq), :, cut(cc)]
            )
        return lambda qq, cc: g[qq, at, :, cut(cc)]

    copies = []
    for q in range(19):
        for c in range(tiles):
            new = []
            for x in range(rows):
                fc = fac[x, :, cut(c)]
                if q == 0:
                    v = g[0, x, :, cut(c)]
                else:
                    v = pull(row_of(q, x), q, c, tiles, halves, lane, sub)
                    v = jnp.where(v != v, g[OPP[q], x, :, cut(c)], v)
                new.append(jnp.where(fc != fc, start[q, x, :, cut(c)], v))
            for i, t in enumerate(swap_tile(new, sub)):
                first = (i * tiles + c) * SUBS
                buf[q, first : first + SUBS, :] = t
        copy = pltpu.make_async_copy(buf.at[q], out.at[q], sems.at[q])
        copy.start()
        copies.append(copy)
    for copy in copies:
        copy.wait()


def slope(p, q):
    return np.float32(0.5) * (
        jnp.maximum(jnp.minimum(p, q), np.float32(0.0)) + jnp.minimum(jnp.maximum(p, q), np.float32(0.0))
    )


def loss(s, c):
    return [np.float32(TRANSFER) * a * (np.float32(1.0) - b) for a, b in zip(s, c)]


def ends_of(parts, strips):
    place = lax.axis_index("wide") * parts + lax.axis_index("narrow")
    return place == 0, place == strips - 1


ZERO = np.float32(0.0)


def each(f, *lists):
    return [f(*t) for t in zip(*lists)]


def less(a, b):
    return each(lambda x, y: x - y, a, b)


def times(a, b):
    return each(lambda x, y: x * y, a, b)


def face(w, va, vb, c, cn, sl, sn, dn):
    a = each(lambda w, x, y: w * np.float32(0.5) * (x + y), w, va, vb)
    return each(
        lambda a, w, c, cn, sl, sn, dn: a * jnp.where(a > 0, c + sl, cn - sn) - np.float32(DIFFUSION) * w * dn,
        a, w, c, cn, sl, sn, dn,
    )


def floored(p):
    return [jnp.maximum(t, np.float32(FLOOR)) for t in p]


class Step:
    def __init__(self, tiles, halves, conc, poro, flow, cross, napl):
        self.tiles, self.halves = tiles, halves
        self.lane, self.sub = iotas()
        self.conc, self.poro, self.flow = (self.keep(f) for f in (conc, poro, flow))
        self.cross, self.napl = cross, napl
        self.gap = self.keep(lambda r: less(self.conc(r + 1), self.conc(r)))
        self.lean = self.keep(lambda r: each(slope, self.gap(r - 1), self.gap(r)))

    @staticmethod
    def keep(f):
        seen = {}

        def get(r):
            if r not in seen:
                seen[r] = f(r)
            return seen[r]

        return get

    def after(self, v):
        out = []
        for c in range(self.tiles):
            if c < self.tiles - 1:
                side = v[c + 1]
            else:
                edge = self.sub % self.halves == self.halves - 1
                side = jnp.where(edge, ZERO, pltpu.roll(v[0], SUBS - 1, 0))
            out.append(pltpu.roll(jnp.where(self.lane == 0, side, v[c]), LANES - 1, 1))
        return out

    def before(self, v):
        out = []
        for c in range(self.tiles):
            if c > 0:
                side = v[c - 1]
            else:
                edge = self.sub % self.halves == 0
                side = jnp.where(edge, ZERO, pltpu.roll(v[self.tiles - 1], 1, 0))
            out.append(pltpu.roll(jnp.where(self.lane == LANES - 1, side, v[c]), 1, 1))
        return out

    def above(self, v):
        return [pltpu.roll(t, SUBS - self.halves, 0) for t in v]

    def below(self, v):
        return [pltpu.roll(t, self.halves, 0) for t in v]

    def flow_face(self, r):
        return face(
            times(self.poro(r), self.poro(r + 1)), self.flow(r), self.flow(r + 1), self.conc(r), self.conc(r + 1),
            self.lean(r), self.lean(r + 1), self.gap(r),
        )

    def run(self, r, low=True, high=True):
        c, p, s = self.conc(r), self.poro(r), self.napl(r)
        change = None
        if low:
            change = self.flow_face(r - 1)
        if high:
            out = self.flow_face(r)
            change = [-t for t in out] if change is None else less(change, out)
        vel = self.cross(r)
        for after, before, v, open_ends in (
            (self.after, self.before, vel[0], True), (self.above, self.below, vel[1], False),
        ):
            cn = after(c)
            dn = less(cn, c)
            dm = less(c, before(c)) if open_ends else before(dn)
            s0 = each(slope, dm, dn)
            flux = face(times(p, after(p)), v, after(v), c, cn, s0, after(s0), dn)
            change = each(lambda t, a, b: t + (a - b), change, before(flux), flux)
        rate = loss(s, c)
        cnew = each(lambda c, t, k, p: c + (t + k) / p, c, change, rate, floored(p))
        return cnew, each(lambda s, k: s - np.float32(DEPLETION) * k, s, rate)


def read(slab):
    return [slab[:, cut(c)] for c in range(slab.shape[1] // LANES)]


def write(slab, tiles):
    for c, t in enumerate(tiles):
        slab[:, cut(c)] = t


def early_kernel(tiles, halves, slabs, u, ue0, ue1, cs):
    rows = slabs.shape[1]
    odd = upper(1)

    def flow(r):
        if r == 1:
            return pick(odd, read(ue0.at[1, 1]), read(ue1.at[1, 1]))
        if r == rows - 2:
            return pick(odd, read(ue1.at[1, 1]), read(ue0.at[1, 1]))
        return read(u.at[1, r - 2])

    step = Step(
        tiles, halves, lambda r: read(slabs.at[0, r]), lambda r: read(slabs.at[2, r]), flow,
        lambda r: (read(u.at[2, r - 2]), read(u.at[0, r - 2])), lambda r: read(slabs.at[1, r]),
    )
    for r in range(2, rows - 2):
        for k, v in enumerate(step.run(r)):
            write(cs.at[k, r - 2], v)


def static_readers(ends, up, slabs, still, base, flags):
    rows = slabs.shape[1]
    first, last = ends_of(*ends)

    def conc(r):
        if r < 0:
            return [jnp.where(first, ZERO, t) for t in read(still.at[base - 1 - r])]
        if r >= rows:
            return pick(last, read(slabs.at[0, rows - 1]), read(still.at[base + r - rows]))
        return read(slabs.at[0, r])

    def poro(r):
        if 0 <= r < rows:
            return read(slabs.at[2, r])
        return pick(last if up else first, read(flags.at[1 if up else 0]), read(still.at[base + 2]))

    return conc, poro


def rim_kernel(tiles, halves, ends, chain, base, g, fac, halo, u, slabs, still, flags, after, ue, cs, send):
    rows = g.shape[1]
    lane, sub = iotas()

    def side(up):
        x, beside = (rows - 1, rows - 2) if up else (0, 1)
        lo, hi, place = (None, halo, "last") if up else (halo, None, "first")
        for n, (at, where) in enumerate(((x, place), (beside, "mid"))):
            for c in range(tiles):
                f = stream(g, lo, hi, at, c, tiles, halves, lane, sub, where)
                for i, v in enumerate(speed(f, fac[at, :, cut(c)])):
                    ue[n, i, :, cut(c)] = v
        conc, poro = static_readers(ends, up, slabs, still, base, flags)

        def vel(k, r):
            return read(ue.at[0 if r == x else 1, k] if r in (x, beside) else u.at[k, r - 2])

        step = Step(
            tiles, halves, conc, poro, lambda r: vel(1, r), lambda r: (vel(2, r), vel(0, r)),
            lambda r: read(slabs.at[1, r]),
        )
        edge = step.run(x, low=up, high=not up)
        inward = step.run(beside)
        for i, new in enumerate((edge, inward)):
            for k in range(2):
                write(cs.at[i, k], new[k])
            write(send.at[1 + i], new[0])
        send[0] = ue[0, 1]

    by_side(chain, side)


def state_reader(rows, edge, inner, rims):
    def state(k, r):
        if r in (0, rows - 1):
            return edge(k, r)
        if r in (1, rows - 2):
            return rims(k, r)
        return read(inner.at[k, r - 2])

    return state


def middle_kernel(tiles, halves, slabs, u, inner, rim0, rim1, out):
    rows = slabs.shape[1]
    odd = upper(1)

    def rims(k, r):
        a, b = (rim0, rim1) if r == 1 else (rim1, rim0)
        return pick(odd, read(a.at[1, k]), read(b.at[1, k]))

    state = state_reader(rows, None, inner, rims)
    step = Step(
        tiles, halves, lambda r: state(0, r), lambda r: read(slabs.at[2, r]), lambda r: read(u.at[1, r - 2]),
        lambda r: (read(u.at[2, r - 2]), read(u.at[0, r - 2])), lambda r: state(1, r),
    )
    for r in range(3, rows - 3):
        write(out.at[r - 3], step.run(r)[0])


def late_kernel(
    tiles, halves, ends, chain, base, slabs, u, ue, inner, rim, still, flags, there, after, out
):
    rows = slabs.shape[1]
    first, last = ends_of(*ends)

    def side(up):
        x = rows - 1 if up else 0
        beyond = rows if up else -1
        ghost = last if up else first
        conc, poro = static_readers(ends, up, slabs, still, base, flags)

        def vel(k, r):
            if r == beyond:
                return pick(ghost, read(ue.at[0, 1]), read(there.at[0]))
            if r in (x, x - 1 if up else x + 1):
                return read(ue.at[0 if r == x else 1, k])
            return read(u.at[k, r - 2])

        def cross(r):
            return vel(2, r), vel(0, r)

        one = Step(tiles, halves, conc, poro, lambda r: vel(1, r), cross, None)
        flux = one.flow_face(x if up else -1)
        sign = np.float32(-1.0 if up else 1.0)
        edge = each(lambda c, f, p: c + sign * f / p, read(rim.at[0, 0]), flux, floored(poro(x)))
        outer = each(lambda c, f, p: c - sign * f / p, read(there.at[1]), flux, floored(poro(beyond)))
        second = read(there.at[2])
        if up:
            outer, second = pick(ghost, edge, outer), pick(ghost, edge, second)
        else:
            outer, second = ([jnp.where(ghost, ZERO, t) for t in v] for v in (outer, second))
        state = state_reader(
            rows, lambda k, r: read(rim.at[0, k]) if k else edge, inner, lambda k, r: read(rim.at[1, k])
        )

        def after_one(r):
            if r < 0 or r >= rows:
                return outer if r == beyond else second
            return state(0, r)

        two = Step(tiles, halves, after_one, poro, lambda r: vel(1, r), cross, lambda r: state(1, r))
        for i in range(3):
            new = two.run(rows - 1 - i if up else i)
            write(out.at[i], new[0])
            if i == 0:
                write(out.at[3], new[1])

    by_side(chain, side)


def deal_kernel(tiles, halves, parts, inner, rim0, rim1, late0, late1, mid, *refs):
    *blocks, whole = refs
    rows = inner.shape[1] + 4
    odd = upper(1)
    _, sub = iotas()
    for c in range(tiles):

        def ends_pick(a, b):
            return jnp.where(odd, a, b)

        lo = [ends_pick(late0[i, :, cut(c)], late1[i, :, cut(c)]) for i in range(4)]
        hi = [ends_pick(late1[i, :, cut(c)], late0[i, :, cut(c)]) for i in range(4)]
        conc = lo[:3] + [mid[r, :, cut(c)] for r in range(rows - 6)] + hi[2::-1]
        left = [lo[3]]
        for r in range(1, rows - 1):
            if r in (1, rows - 2):
                a, b = (rim0, rim1) if r == 1 else (rim1, rim0)
                cc, ss = (ends_pick(a[1, k, :, cut(c)], b[1, k, :, cut(c)]) for k in range(2))
            else:
                cc, ss = (inner[k, r - 2, :, cut(c)] for k in range(2))
            left.append(ss - np.float32(DEPLETION) * loss([ss], [cc])[0])
        left.append(hi[3])
        run = whole.shape[3]
        for k, tile in enumerate((conc, left)):
            for i, t in enumerate(swap_tile(tile, sub)):
                column = (i % halves * tiles + c) * SUBS
                at = column % run
                whole[column // run, k, i // halves, at : at + SUBS, :] = t
    for k in range(parts):
        blocks[k][...] = whole[lax.axis_index("narrow") ^ k]


def gather_kernel(parts, order, *refs):
    blocks = refs[:parts]
    *outs, sems = refs[parts:]
    copies = []
    for k, block in zip(order, blocks):
        origin = lax.axis_index("narrow") ^ k
        for i, out in enumerate(outs):
            copies.append(pltpu.make_async_copy(block.at[i], out.at[:, origin], sems.at[i, k]))
            copies[-1].start()
    for copy in copies:
        copy.wait()


def call(kernel, out_shape, args, scratch=(), hbm=(), free=(), hbm_out=(), name=None, flops=0, aliases=None):
    def spec(i, hbm, free=()):
        return pl.BlockSpec(memory_space=pltpu.HBM if i in hbm else pl.ANY if i in free else pltpu.VMEM)

    single = not isinstance(out_shape, tuple)
    shapes = (out_shape,) if single else out_shape
    out = pl.pallas_call(
        kernel,
        out_shape=shapes,
        in_specs=[spec(i, hbm, free) for i in range(len(args))],
        out_specs=tuple(spec(i, hbm_out) for i in range(len(shapes))),
        scratch_shapes=list(scratch),
        name=name,
        input_output_aliases=aliases or {},
        compiler_params=pltpu.CompilerParams(vmem_limit_bytes=VMEM_LIMIT),
        cost_estimate=pl.CostEstimate(flops=flops, bytes_accessed=flops // 10, transcendentals=0),
    )(*args)
    return out[0] if single else out


def local(populations, phase, porosity, napl, concentration, flags):
    layers, rows, width = phase.shape
    halves = SUBS // layers
    length = width // halves
    tiles = length // LANES
    parts = lax.axis_size("narrow")
    strips = lax.axis_size("wide") * parts
    both = ("wide", "narrow")
    pairs = (
        [(i, i ^ 1) for i in range(strips)],
        [(i, (i + 1 if i % 2 else i - 1) % strips) for i in range(strips)],
    )
    cells = rows * SUBS * length
    slab = (SUBS, length)
    ends = (parts, strips)
    run = width // LANES * SUBS // parts

    def hold(*shape, dtype=F32):
        return pltpu.VMEM(shape, dtype)

    def swap(chain, array):
        return lax.ppermute(array, both, pairs[chain])

    pop = to_view(populations)
    views = [to_view(a) for a in (phase, concentration, napl, porosity)]
    flat = views[0].shape
    chunks = pop.reshape(19, SUBS, tiles, SUBS, LANES)
    given = [pltpu.with_memory_space_constraint(a, pltpu.HBM) for a in (chunks, *views, flags)]
    popv, phv, cov, nav, pov, flv, row1, send = call(
        functools.partial(first_kernel, tiles, halves),
        (
            hold(*chunks.shape), hold(*flat, dtype=jnp.int32), hold(*flat), hold(*flat), hold(*flat),
            hold(*flags.shape, dtype=jnp.int32), hold(19, *slab), hold(18, *slab),
        ),
        given, scratch=(pltpu.VMEM((19, *slab), F32), pltpu.SemaphoreType.DMA((tiles + 5,))),
        hbm=range(6), name="first", flops=50 * cells,
    )
    popv = popv.reshape(pop.shape)
    halo1 = still1 = swap(1, send)
    row0, send = call(
        functools.partial(second_kernel, tiles), (hold(19, *slab), hold(8, *slab)),
        (popv, phv, cov, pov, send), free=(4,), name="second", flops=30 * cells,
    )
    halo0 = still0 = swap(0, send)
    g, fac, start, slabs, open_ends = call(
        functools.partial(first_inner_kernel, tiles, halves),
        (
            hold(19, rows, *slab), hold(rows, *slab), hold(19, rows, *slab), hold(3, rows, *slab),
            hold(2, *slab),
        ),
        (popv, phv, cov, nav, pov, flv, row0, row1), name="first_inner", flops=300 * cells,
    )
    after = slabs
    for step in range(1, LBM_STEPS):
        if step % 2 == 0:
            row1, send1 = call(
                functools.partial(far_kernel, tiles, halves), (hold(19, *slab), hold(14, *slab)),
                (g, fac, ghost), scratch=(pltpu.VMEM((19, *slab), F32),), name="far", flops=60 * cells,
            )
            halo1 = swap(1, send1)
            after = send1
        new = call(
            functools.partial(inner_kernel, tiles, halves), hold(19, rows, *slab), (g, fac, after),
            free=(2,), name="inner", flops=250 * cells,
        )
        if step == LBM_STEPS - 1:
            u = call(
                functools.partial(inner_speed_kernel, tiles, halves), hold(3, rows - 4, *slab), (new, fac, after),
                free=(2,), name="inner_speed", flops=100 * cells,
            )
        row0, send = call(
            functools.partial(edge_kernel, tiles, halves, 0), (hold(19, *slab), hold(5, *slab)),
            (g, fac, halo0, new), free=(3,), name="edge0", flops=30 * cells,
        )
        halo0 = swap(0, send)
        if step % 2 == 0:
            g = call(
                put_kernel, hold(19, rows, *slab), (new, row0, row1), name="put", flops=10 * cells,
                aliases={0: 0},
            )
            after = g
        else:
            g, ghost = call(
                functools.partial(arrive_kernel, tiles, halves), (hold(19, rows, *slab), hold(5, *slab)),
                (g, fac, halo1, still1, row0, u if step == LBM_STEPS - 1 else send, new), free=(5,),
                name="arrive", flops=60 * cells, aliases={6: 0},
            )
            after = ghost
    ue1, rim1, send = call(
        functools.partial(rim_kernel, tiles, halves, ends, 1, 15),
        (hold(2, 3, *slab), hold(2, 2, *slab), hold(3, *slab)),
        (g, fac, ghost, u, slabs, still1, open_ends, u), free=(7,), name="rim1", flops=50 * cells,
    )
    there1 = swap(1, send)
    ue0, rim0, send = call(
        functools.partial(rim_kernel, tiles, halves, ends, 0, 5),
        (hold(2, 3, *slab), hold(2, 2, *slab), hold(3, *slab)),
        (g, fac, halo0, u, slabs, still0, open_ends, send), free=(7,), name="rim0", flops=50 * cells,
    )
    there0 = swap(0, send)
    inner = call(
        functools.partial(early_kernel, tiles, halves), hold(2, rows - 4, *slab), (slabs, u, ue0, ue1),
        name="early", flops=60 * cells,
    )
    mid = call(
        functools.partial(middle_kernel, tiles, halves), hold(rows - 6, *slab), (slabs, u, inner, rim0, rim1),
        name="middle", flops=40 * cells,
    )
    late0 = call(
        functools.partial(late_kernel, tiles, halves, ends, 0, 5), hold(4, *slab),
        (slabs, u, ue0, inner, rim0, still0, open_ends, there0, mid), free=(8,), name="late0", flops=30 * cells,
    )
    out, token = call(
        functools.partial(final_kernel, tiles, halves),
        (jax.ShapeDtypeStruct((19, *flat), F32), hold(SUBS, LANES)),
        (g, fac, halo0, ghost, start, late0),
        scratch=(pltpu.VMEM((19, *flat), F32), pltpu.SemaphoreType.DMA((19,))),
        free=(5,), hbm_out=(0,), name="final", flops=400 * cells,
    )
    late1 = call(
        functools.partial(late_kernel, tiles, halves, ends, 1, 15), hold(4, *slab),
        (slabs, u, ue1, inner, rim1, still1, open_ends, there1, token), free=(8,), name="late1", flops=30 * cells,
    )
    block = (2, layers, run, LANES)
    blocks = call(
        functools.partial(deal_kernel, tiles, halves, parts), tuple(hold(*block) for _ in range(parts)),
        (inner, rim0, rim1, late0, late1, mid),
        scratch=(pltpu.VMEM((parts, *block), F32),), name="deal", flops=20 * cells,
    )
    order = [0, *range(2, parts), 1]
    came = [blocks[0]]
    for k in order[1:]:
        came.append(lax.ppermute(blocks[k], "narrow", [(i, i ^ k) for i in range(parts)]))
    tile = (layers, parts, run, LANES)
    conc_out, napl_out = call(
        functools.partial(gather_kernel, parts, order),
        (jax.ShapeDtypeStruct(tile, F32), jax.ShapeDtypeStruct(tile, F32)),
        came, scratch=(pltpu.SemaphoreType.DMA((2, parts)),), hbm_out=(0, 1), name="gather", flops=10 * cells,
    )
    shape = (layers, rows * parts, width // parts)

    def tile_of(a):
        return from_view(a.reshape(layers * parts * run, LANES), shape)

    return from_view(out, populations.shape), tile_of(conc_out), tile_of(napl_out)


def solution(mesh):
    strip = P(None, ("wide", "narrow"), None)
    in_specs = (P(None, None, ("wide", "narrow"), None), strip, strip, strip, strip, P())
    tile = P(None, "wide", "narrow")
    out_specs = (P(None, None, ("wide", "narrow"), None), tile, tile)
    return jax.shard_map(local, mesh=mesh, in_specs=in_specs, out_specs=out_specs, check_vma=False)
```

```python
import functools

import jax
import jax.numpy as jnp
import numpy as np
from jax import lax
from jax.experimental import pallas as pl
from jax.experimental.pallas import tpu as pltpu
from jax.sharding import PartitionSpec as P

LBM_STEPS = 4
F32 = jnp.float32

DIRS = [
    (0, 0, 0), (1, 0, 0), (-1, 0, 0), (0, 1, 0), (0, -1, 0), (0, 0, 1), (0, 0, -1),
    (1, 1, 0), (-1, -1, 0), (1, -1, 0), (-1, 1, 0), (1, 0, 1), (-1, 0, -1), (1, 0, -1),
    (-1, 0, 1), (0, 1, 1), (0, -1, -1), (0, 1, -1), (0, -1, 1),
]
OPP = [0, 2, 1, 4, 3, 6, 5, 8, 7, 10, 9, 12, 11, 14, 13, 16, 15, 18, 17]
UP = [1, 7, 9, 11, 13]
DOWN = [2, 8, 10, 12, 14]
DIFFUSION = 0.15
TRANSFER = 0.3
DEPLETION = 0.5
FLOOR = 0.3
SUBS = 8
LANES = 128
VMEM_LIMIT = 16 * 1024 * 1024


def to_view(array):
    *lead, rows, width = array.shape
    n = len(lead)
    t = array.reshape(*lead, rows // SUBS, SUBS, width // LANES, LANES)
    t = t.transpose(*range(n), n, n + 2, n + 1, n + 3)
    return t.reshape(*lead[:-1], lead[-1] * rows * width // LANES, LANES)


def from_view(view, shape):
    *lead, rows, width = shape
    n = len(lead)
    t = view.reshape(*lead, rows // SUBS, width // LANES, SUBS, LANES)
    t = t.transpose(*range(n), n, n + 2, n + 1, n + 3)
    return t.reshape(shape)


def iotas():
    lane = lax.broadcasted_iota(jnp.int32, (SUBS, LANES), 1)
    sub = lax.broadcasted_iota(jnp.int32, (SUBS, LANES), 0)
    return lane, sub


def cut(c):
    return slice(c * LANES, (c + 1) * LANES)


def strided(tiles, c, x):
    return pl.ds(c * SUBS + x, SUBS, stride=tiles * SUBS)


def collide(f, fac):
    s = [f[2 * p + 1] + f[2 * p + 2] for p in range(9)]
    d = [f[2 * p + 1] - f[2 * p + 2] for p in range(9)]
    rho = f[0] + (((s[0] + s[1]) + (s[2] + s[3])) + ((s[4] + s[5]) + (s[6] + s[7])) + s[8])
    jx = d[0] + ((d[3] + d[4]) + (d[5] + d[6]))
    jy = d[1] + ((d[3] - d[4]) + (d[7] + d[8]))
    jz = d[2] + ((d[5] - d[6]) + (d[7] - d[8]))
    inv = fac / rho
    vx, vy, vz = jx * inv, jy * inv, jz * inv
    w1 = rho * np.float32(1.25 / 18)
    w2 = rho * np.float32(1.25 / 36)
    w4 = rho * np.float32(1.25 / 72)
    a1 = w1 - w1 * ((vx * vx + vy * vy + vz * vz) * np.float32(1.0 / 6))
    a2 = a1 * np.float32(0.5)
    post = [a1 * np.float32(6.0) - f[0] * np.float32(0.25)]
    axes = [vx, vy, vz, vx + vy, vx - vy, vx + vz, vx - vz, vy + vz, vy - vz]
    for p, v in enumerate(axes):
        wa, wh, base = (w1, w2, a1) if p < 3 else (w2, w4, a2)
        even = (base + (wh * v) * v) - s[p] * np.float32(0.125)
        odd = wa * v - d[p] * np.float32(0.125)
        post += [even + odd, even - odd]
    return post


def pull(load, q, c, tiles, halves, lane, sub):
    _, cross, layer = DIRS[q]
    v = load(q, c)
    if cross == 1:
        if c > 0:
            side = load(q, c - 1)
        else:
            side = jnp.where(sub % halves == 0, jnp.nan, pltpu.roll(load(q, tiles - 1), 1, 0))
        v = pltpu.roll(jnp.where(lane == LANES - 1, side, v), 1, 1)
    elif cross == -1:
        if c < tiles - 1:
            side = load(q, c + 1)
        else:
            side = jnp.where(sub % halves == halves - 1, jnp.nan, pltpu.roll(load(q, 0), SUBS - 1, 0))
        v = pltpu.roll(jnp.where(lane == 0, side, v), LANES - 1, 1)
    if layer:
        v = pltpu.roll(v, (layer * halves) % SUBS, 0)
    return v


def stream(g, lo, hi, x, c, tiles, halves, lane, sub, place):
    def load(q, cc):
        flow = DIRS[q][0]
        if flow == 1 and place == "first":
            return lo[UP.index(q), :, cut(cc)]
        if flow == -1 and place == "last":
            return hi[DOWN.index(q), :, cut(cc)]
        return g[q, x - flow, :, cut(cc)]

    f = [g[0, x, :, cut(c)]]
    for q in range(1, 19):
        v = pull(load, q, c, tiles, halves, lane, sub)
        f.append(jnp.where(v != v, g[OPP[q], x, :, cut(c)], v))
    return f


def drag(ph):
    return jnp.where(ph == 2, jnp.nan, jnp.where(ph == 1, np.float32(1.5), np.float32(3.0)))


def swap_tile(v, sub):
    v = list(v)
    for k in (4, 2, 1):
        low = sub & k == 0
        for i in range(SUBS):
            if not i & k:
                a, b = v[i], v[i + k]
                v[i] = jnp.where(low, a, pltpu.roll(b, k, 0))
                v[i + k] = jnp.where(low, pltpu.roll(a, SUBS - k, 0), b)
    return v


def upper(chain):
    odd = lax.rem(lax.axis_index("narrow"), 2) == 1
    return odd if chain else jnp.logical_not(odd)


def by_side(chain, side):
    pl.when(upper(chain))(lambda: side(True))
    pl.when(jnp.logical_not(upper(chain)))(lambda: side(False))


def pick(flag, a, b):
    return [jnp.where(flag, x, y) for x, y in zip(a, b)]


def start_row(tiles, pop, phase, x, row, c):
    at = strided(tiles, c, x)
    fc = drag(phase[at, :])
    post = collide([pop[q, at, :] for q in range(19)], fc)
    for q in range(19):
        row[q, :, cut(c)] = post[q]
    return fc


def look_ahead(tiles, halves, up, edge, beside, send):
    lane, sub = iotas()
    toward, back = (UP, DOWN) if up else (DOWN, UP)
    for c in range(tiles):
        sums = [None] * 3
        for q in range(19):
            if q in back:
                continue
            if q == 0:
                f = edge(0, c)
            else:
                f = pull(beside if q in toward else edge, q, c, tiles, halves, lane, sub)
                f = jnp.where(f != f, edge(OPP[q], c), f)
            if q in toward:
                i = toward.index(q)
                send[i, :, cut(c)] = edge(q, c)
                send[5 + i, :, cut(c)] = f
            else:
                for k, e in enumerate((1, *DIRS[q][1:])):
                    if e:
                        t = f if e > 0 else -f
                        sums[k] = t if sums[k] is None else sums[k] + t
        for k in range(3):
            send[10 + k, :, cut(c)] = sums[k]


def start_rows(tiles, halves, chain, pop, phase, row, send, beside, ready=None):
    up = upper(chain)
    x, inwards = jnp.where(up, SUBS - 1, 0), jnp.where(up, SUBS - 2, 1)
    for c in range(tiles):
        if ready is not None:
            ready(c)
        send[13, :, cut(c)] = start_row(tiles, pop, phase, x, row, c)
        start_row(tiles, pop, phase, inwards, beside, c)

    def side(up):
        look_ahead(
            tiles, halves, up, lambda q, c: row[q, :, cut(c)], lambda q, c: beside[q, :, cut(c)], send
        )

    by_side(chain, side)


def first_kernel(
    tiles, halves, pop_h, phase_h, conc_h, napl_h, poro_h, flags_h,
    pop, phase, conc, napl, poro, flags, row, send, beside, sems,
):
    small = [
        pltpu.make_async_copy(a, b, sems.at[tiles + i])
        for i, (a, b) in enumerate(
            ((phase_h, phase), (conc_h, conc), (poro_h, poro), (napl_h, napl), (flags_h, flags))
        )
    ]
    large = [pltpu.make_async_copy(pop_h.at[:, :, c], pop.at[:, :, c], sems.at[c]) for c in range(tiles)]
    small[0].start()
    for copy in large + small[1:]:
        copy.start()
    small[0].wait()
    flat = pop.reshape(pop.shape[0], SUBS * tiles * SUBS, LANES)
    start_rows(tiles, halves, 1, flat, phase, row, send, beside, ready=lambda c: large[c].wait())
    for copy in small[1:]:
        copy.wait()


def second_kernel(tiles, halves, pop, phase, after, row, send, beside):
    start_rows(tiles, halves, 0, pop, phase, row, send, beside)


def merge_rows(out, row0, row1, count):
    rows = out.shape[1]

    def side(up):
        for k in range(count):
            out[k, 0] = (row0 if up else row1)[k]
            out[k, rows - 1] = (row1 if up else row0)[k]

    by_side(1, side)


def first_inner_kernel(
    tiles, halves, pop, phase, conc, napl, poro, flags, row0, row1, g, fac, start, slabs, open_ends
):
    rows = g.shape[1]
    length = tiles * LANES
    _, sub = iotas()

    def to_slabs(read, write):
        for c in range(tiles):
            v = [read(pl.ds((i * tiles + c) * SUBS, SUBS)) for i in range(SUBS)]
            for x, t in enumerate(swap_tile(v, sub)):
                write(x, cut(c), t)

    def store(ref, k):
        def write(x, at, t):
            ref[k, x, :, at] = t

        return write

    def store_fac(x, at, t):
        fac[x, :, at] = t

    to_slabs(lambda at: drag(phase[at, :]), store_fac)

    def direction(q, _):
        to_slabs(lambda at: pop[q, at, :], store(start, q))
        return 0

    lax.fori_loop(0, 19, direction, 0)

    def row(x, _):
        for c in range(tiles):
            post = collide([start[q, x, :, cut(c)] for q in range(19)], fac[x, :, cut(c)])
            for q in range(19):
                g[q, x, :, cut(c)] = post[q]
        return 0

    lax.fori_loop(1, rows - 1, row, 0)
    merge_rows(g, row0, row1, 19)
    for k, ref in enumerate((conc, napl, poro)):
        to_slabs(lambda at, ref=ref: ref[at, :], store(slabs, k))
    for k in range(2):
        for z in range(SUBS // halves):
            for h in range(halves):
                line = flags[k, z : z + 1, h * length : (h + 1) * length]
                open_ends[k, z * halves + h : z * halves + h + 1, :] = line.astype(F32)


def inner_kernel(tiles, halves, g, fac, after, out):
    rows = g.shape[1]
    lane, sub = iotas()

    def row(x, _):
        for c in range(tiles):
            f = stream(g, None, None, x, c, tiles, halves, lane, sub, "mid")
            post = collide(f, fac[x, :, cut(c)])
            for q in range(19):
                out[q, x, :, cut(c)] = post[q]
        return 0

    lax.fori_loop(1, rows - 1, row, 0)


def put_kernel(inner, row0, row1, out):
    merge_rows(out, row0, row1, 19)


def arrive_kernel(tiles, halves, chain, g, fac, halo, first_halo, after, inner, out, ghost):
    rows = g.shape[1]
    lane, sub = iotas()

    def side(up):
        x = rows - 1 if up else 0
        lo, hi, place = (None, halo, "last") if up else (halo, None, "first")
        toward, back = (DOWN, UP) if up else (UP, DOWN)
        for c in range(tiles):
            post = collide(stream(g, lo, hi, x, c, tiles, halves, lane, sub, place), fac[x, :, cut(c)])
            for q in range(19):
                out[q, x, :, cut(c)] = post[q]
            near = [halo[5 + i, :, cut(c)] for i in range(5)]
            sums = [halo[10, :, cut(c)], None, halo[11, :, cut(c)], halo[12, :, cut(c)]]
            known = list(zip(toward, near))
            for i, q in enumerate(back):
                f = pull(lambda q, cc: g[q, x, :, cut(cc)], q, c, tiles, halves, lane, sub)
                known.append((q, jnp.where(f != f, halo[i, :, cut(c)], f)))
            for q, f in known:
                for k, e in enumerate((1, *DIRS[q])):
                    if e:
                        t = f if e > 0 else -f
                        sums[k] = t if sums[k] is None else sums[k] + t
            rho = sums[0]
            inv = first_halo[13, :, cut(c)] / rho
            v = [j * inv for j in sums[1:]]
            base = np.float32(1.0) - (v[0] * v[0] + v[1] * v[1] + v[2] * v[2]) * np.float32(1.0 / 6)
            for i, q in enumerate(toward):
                along = None
                for e, t in zip(DIRS[q], v):
                    if e:
                        t = t if e > 0 else -t
                        along = t if along is None else along + t
                weight = np.float32(1.25 / 18 if sum(map(abs, DIRS[q])) == 1 else 1.25 / 36)
                feq = (rho * weight) * (base + along * (along * np.float32(0.5) + np.float32(1.0)))
                ghost[i, :, cut(c)] = feq - near[i] * np.float32(0.25)

    by_side(chain, side)


def far_kernel(tiles, halves, chain, g, fac, halo, slabs, after, row, send, beside):
    rows = g.shape[1]
    lane, sub = iotas()

    def side(up):
        x, inwards = (rows - 1, rows - 2) if up else (0, 1)
        lo, hi, place = (None, halo, "last") if up else (halo, None, "first")
        for c in range(tiles):
            for at, ref, where in ((x, row, place), (inwards, beside, "mid")):
                f = stream(g, lo, hi, at, c, tiles, halves, lane, sub, where)
                post = collide(f, fac[at, :, cut(c)])
                for q in range(19):
                    ref[q, :, cut(c)] = post[q]
        look_ahead(
            tiles, halves, up, lambda q, c: row[q, :, cut(c)], lambda q, c: beside[q, :, cut(c)], send
        )
        send[13] = slabs[0, x]

    by_side(chain, side)


def speed(f, fc):
    s = [f[2 * p + 1] + f[2 * p + 2] for p in range(9)]
    d = [f[2 * p + 1] - f[2 * p + 2] for p in range(9)]
    rho = f[0] + (((s[0] + s[1]) + (s[2] + s[3])) + ((s[4] + s[5]) + (s[6] + s[7])) + s[8])
    jx = d[0] + ((d[3] + d[4]) + (d[5] + d[6]))
    jy = d[1] + ((d[3] - d[4]) + (d[7] + d[8]))
    jz = d[2] + ((d[5] - d[6]) + (d[7] - d[8]))
    inv = np.float32(1.0) / rho
    return [jnp.where(fc != fc, np.float32(0.0), j * inv) for j in (jz, jx, jy)]


def inner_speed_kernel(tiles, halves, g, fac, after, u):
    rows = g.shape[1]
    lane, sub = iotas()

    def row(x, _):
        for c in range(tiles):
            f = stream(g, None, None, x, c, tiles, halves, lane, sub, "mid")
            for i, v in enumerate(speed(f, fac[x, :, cut(c)])):
                u[i, x - 2, :, cut(c)] = v
        return 0

    lax.fori_loop(2, rows - 2, row, 0)


def final_kernel(tiles, halves, g, fac, halo0, halo1, start, after, out, token, buf, sems):
    rows = g.shape[1]
    lane, sub = iotas()
    odd = upper(1)
    token[...] = jnp.zeros(token.shape, F32)

    def row_of(q, x):
        at = x - DIRS[q][0]
        if at < 0:
            return lambda qq, cc: jnp.where(
                odd, halo0[UP.index(qq), :, cut(cc)], halo1[UP.index(qq), :, cut(cc)]
            )
        if at >= rows:
            return lambda qq, cc: jnp.where(
                odd, halo1[DOWN.index(qq), :, cut(cc)], halo0[DOWN.index(qq), :, cut(cc)]
            )
        return lambda qq, cc: g[qq, at, :, cut(cc)]

    copies = []
    for q in range(19):
        for c in range(tiles):
            new = []
            for x in range(rows):
                fc = fac[x, :, cut(c)]
                if q == 0:
                    v = g[0, x, :, cut(c)]
                else:
                    v = pull(row_of(q, x), q, c, tiles, halves, lane, sub)
                    v = jnp.where(v != v, g[OPP[q], x, :, cut(c)], v)
                new.append(jnp.where(fc != fc, start[q, x, :, cut(c)], v))
            for i, t in enumerate(swap_tile(new, sub)):
                first = (i * tiles + c) * SUBS
                buf[q, first : first + SUBS, :] = t
        copy = pltpu.make_async_copy(buf.at[q], out.at[q], sems.at[q])
        copy.start()
        copies.append(copy)
    for copy in copies:
        copy.wait()


def slope(p, q):
    return np.float32(0.5) * (
        jnp.maximum(jnp.minimum(p, q), np.float32(0.0)) + jnp.minimum(jnp.maximum(p, q), np.float32(0.0))
    )


def loss(s, c):
    return [np.float32(TRANSFER) * a * (np.float32(1.0) - b) for a, b in zip(s, c)]


def ends_of(parts, strips):
    place = lax.axis_index("wide") * parts + lax.axis_index("narrow")
    return place == 0, place == strips - 1


ZERO = np.float32(0.0)


def each(f, *lists):
    return [f(*t) for t in zip(*lists)]


def less(a, b):
    return each(lambda x, y: x - y, a, b)


def times(a, b):
    return each(lambda x, y: x * y, a, b)


def face(w, va, vb, c, cn, sl, sn, dn):
    a = each(lambda w, x, y: w * np.float32(0.5) * (x + y), w, va, vb)
    return each(
        lambda a, w, c, cn, sl, sn, dn: a * jnp.where(a > 0, c + sl, cn - sn) - np.float32(DIFFUSION) * w * dn,
        a, w, c, cn, sl, sn, dn,
    )


def floored(p):
    return [jnp.maximum(t, np.float32(FLOOR)) for t in p]


class Step:
    def __init__(self, tiles, halves, conc, poro, flow, cross, napl):
        self.tiles, self.halves = tiles, halves
        self.lane, self.sub = iotas()
        self.conc, self.poro, self.flow = (self.keep(f) for f in (conc, poro, flow))
        self.cross, self.napl = cross, napl
        self.gap = self.keep(lambda r: less(self.conc(r + 1), self.conc(r)))
        self.lean = self.keep(lambda r: each(slope, self.gap(r - 1), self.gap(r)))

    @staticmethod
    def keep(f):
        seen = {}

        def get(r):
            if r not in seen:
                seen[r] = f(r)
            return seen[r]

        return get

    def after(self, v):
        out = []
        for c in range(self.tiles):
            if c < self.tiles - 1:
                side = v[c + 1]
            else:
                edge = self.sub % self.halves == self.halves - 1
                side = jnp.where(edge, ZERO, pltpu.roll(v[0], SUBS - 1, 0))
            out.append(pltpu.roll(jnp.where(self.lane == 0, side, v[c]), LANES - 1, 1))
        return out

    def before(self, v):
        out = []
        for c in range(self.tiles):
            if c > 0:
                side = v[c - 1]
            else:
                edge = self.sub % self.halves == 0
                side = jnp.where(edge, ZERO, pltpu.roll(v[self.tiles - 1], 1, 0))
            out.append(pltpu.roll(jnp.where(self.lane == LANES - 1, side, v[c]), 1, 1))
        return out

    def above(self, v):
        return [pltpu.roll(t, SUBS - self.halves, 0) for t in v]

    def below(self, v):
        return [pltpu.roll(t, self.halves, 0) for t in v]

    def flow_face(self, r):
        return face(
            times(self.poro(r), self.poro(r + 1)), self.flow(r), self.flow(r + 1), self.conc(r), self.conc(r + 1),
            self.lean(r), self.lean(r + 1), self.gap(r),
        )

    def run(self, r, low=True, high=True):
        c, p, s = self.conc(r), self.poro(r), self.napl(r)
        change = None
        if low:
            change = self.flow_face(r - 1)
        if high:
            out = self.flow_face(r)
            change = [-t for t in out] if change is None else less(change, out)
        vel = self.cross(r)
        for after, before, v, open_ends in (
            (self.after, self.before, vel[0], True), (self.above, self.below, vel[1], False),
        ):
            cn = after(c)
            dn = less(cn, c)
            dm = less(c, before(c)) if open_ends else before(dn)
            s0 = each(slope, dm, dn)
            flux = face(times(p, after(p)), v, after(v), c, cn, s0, after(s0), dn)
            change = each(lambda t, a, b: t + (a - b), change, before(flux), flux)
        rate = loss(s, c)
        cnew = each(lambda c, t, k, p: c + (t + k) / p, c, change, rate, floored(p))
        return cnew, each(lambda s, k: s - np.float32(DEPLETION) * k, s, rate)


def read(slab):
    return [slab[:, cut(c)] for c in range(slab.shape[1] // LANES)]


def write(slab, tiles):
    for c, t in enumerate(tiles):
        slab[:, cut(c)] = t


def early_kernel(tiles, halves, slabs, u, ue0, ue1, cs):
    rows = slabs.shape[1]
    odd = upper(1)

    def flow(r):
        if r == 1:
            return pick(odd, read(ue0.at[1, 1]), read(ue1.at[1, 1]))
        if r == rows - 2:
            return pick(odd, read(ue1.at[1, 1]), read(ue0.at[1, 1]))
        return read(u.at[1, r - 2])

    step = Step(
        tiles, halves, lambda r: read(slabs.at[0, r]), lambda r: read(slabs.at[2, r]), flow,
        lambda r: (read(u.at[2, r - 2]), read(u.at[0, r - 2])), lambda r: read(slabs.at[1, r]),
    )
    for r in range(2, rows - 2):
        for k, v in enumerate(step.run(r)):
            write(cs.at[k, r - 2], v)


def static_readers(ends, up, slabs, halo, there, flags):
    rows = slabs.shape[1]
    first, last = ends_of(*ends)

    def conc(r):
        if 0 <= r < rows:
            return read(slabs.at[0, r])
        beyond = read(halo.at[13] if r in (-1, rows) else there.at[3])
        return pick(last, read(slabs.at[0, rows - 1]), beyond) if up else [jnp.where(first, ZERO, t) for t in beyond]

    def poro(r):
        if 0 <= r < rows:
            return read(slabs.at[2, r])
        return pick(last if up else first, read(flags.at[1 if up else 0]), read(there.at[4]))

    return conc, poro


def rim_kernel(tiles, halves, ends, chain, g, fac, ghost, u, slabs, halo, after, ue, cs, send):
    rows = g.shape[1]
    lane, sub = iotas()

    def side(up):
        x, beside = (rows - 1, rows - 2) if up else (0, 1)
        lo, hi, place = (None, ghost, "last") if up else (ghost, None, "first")
        for n, (at, where) in enumerate(((x, place), (beside, "mid"))):
            for c in range(tiles):
                f = stream(g, lo, hi, at, c, tiles, halves, lane, sub, where)
                for i, v in enumerate(speed(f, fac[at, :, cut(c)])):
                    ue[n, i, :, cut(c)] = v
        conc, poro = static_readers(ends, up, slabs, halo, None, None)

        def vel(k, r):
            return read(ue.at[0 if r == x else 1, k] if r in (x, beside) else u.at[k, r - 2])

        step = Step(
            tiles, halves, conc, poro, lambda r: vel(1, r), lambda r: (vel(2, r), vel(0, r)),
            lambda r: read(slabs.at[1, r]),
        )
        edge = step.run(x, low=up, high=not up)
        inward = step.run(beside)
        for i, new in enumerate((edge, inward)):
            for k in range(2):
                write(cs.at[i, k], new[k])
            write(send.at[1 + i], new[0])
        send[0] = ue[0, 1]
        send[3] = slabs[0, beside]
        send[4] = slabs[2, x]

    by_side(chain, side)


def state_reader(rows, edge, inner, rims):
    def state(k, r):
        if r in (0, rows - 1):
            return edge(k, r)
        if r in (1, rows - 2):
            return rims(k, r)
        return read(inner.at[k, r - 2])

    return state


def middle_kernel(tiles, halves, slabs, u, inner, rim0, rim1, out):
    rows = slabs.shape[1]
    odd = upper(1)

    def rims(k, r):
        a, b = (rim0, rim1) if r == 1 else (rim1, rim0)
        return pick(odd, read(a.at[1, k]), read(b.at[1, k]))

    state = state_reader(rows, None, inner, rims)
    step = Step(
        tiles, halves, lambda r: state(0, r), lambda r: read(slabs.at[2, r]), lambda r: read(u.at[1, r - 2]),
        lambda r: (read(u.at[2, r - 2]), read(u.at[0, r - 2])), lambda r: state(1, r),
    )
    for r in range(3, rows - 3):
        write(out.at[r - 3], step.run(r)[0])


def late_kernel(
    tiles, halves, ends, chain, slabs, u, ue, inner, rim, halo, flags, there, after, out
):
    rows = slabs.shape[1]
    first, last = ends_of(*ends)

    def side(up):
        x = rows - 1 if up else 0
        beyond = rows if up else -1
        ghost = last if up else first
        conc, poro = static_readers(ends, up, slabs, halo, there, flags)

        def vel(k, r):
            if r == beyond:
                return pick(ghost, read(ue.at[0, 1]), read(there.at[0]))
            if r in (x, x - 1 if up else x + 1):
                return read(ue.at[0 if r == x else 1, k])
            return read(u.at[k, r - 2])

        def cross(r):
            return vel(2, r), vel(0, r)

        one = Step(tiles, halves, conc, poro, lambda r: vel(1, r), cross, None)
        flux = one.flow_face(x if up else -1)
        sign = np.float32(-1.0 if up else 1.0)
        edge = each(lambda c, f, p: c + sign * f / p, read(rim.at[0, 0]), flux, floored(poro(x)))
        outer = each(lambda c, f, p: c - sign * f / p, read(there.at[1]), flux, floored(poro(beyond)))
        second = read(there.at[2])
        if up:
            outer, second = pick(ghost, edge, outer), pick(ghost, edge, second)
        else:
            outer, second = ([jnp.where(ghost, ZERO, t) for t in v] for v in (outer, second))
        state = state_reader(
            rows, lambda k, r: read(rim.at[0, k]) if k else edge, inner, lambda k, r: read(rim.at[1, k])
        )

        def after_one(r):
            if r < 0 or r >= rows:
                return outer if r == beyond else second
            return state(0, r)

        two = Step(tiles, halves, after_one, poro, lambda r: vel(1, r), cross, lambda r: state(1, r))
        for i in range(3):
            new = two.run(rows - 1 - i if up else i)
            write(out.at[i], new[0])
            if i == 0:
                write(out.at[3], new[1])

    by_side(chain, side)


def deal_kernel(tiles, halves, parts, inner, rim0, rim1, late0, late1, mid, *refs):
    *blocks, whole = refs
    rows = inner.shape[1] + 4
    odd = upper(1)
    _, sub = iotas()
    for c in range(tiles):

        def ends_pick(a, b):
            return jnp.where(odd, a, b)

        lo = [ends_pick(late0[i, :, cut(c)], late1[i, :, cut(c)]) for i in range(4)]
        hi = [ends_pick(late1[i, :, cut(c)], late0[i, :, cut(c)]) for i in range(4)]
        conc = lo[:3] + [mid[r, :, cut(c)] for r in range(rows - 6)] + hi[2::-1]
        left = [lo[3]]
        for r in range(1, rows - 1):
            if r in (1, rows - 2):
                a, b = (rim0, rim1) if r == 1 else (rim1, rim0)
                cc, ss = (ends_pick(a[1, k, :, cut(c)], b[1, k, :, cut(c)]) for k in range(2))
            else:
                cc, ss = (inner[k, r - 2, :, cut(c)] for k in range(2))
            left.append(ss - np.float32(DEPLETION) * loss([ss], [cc])[0])
        left.append(hi[3])
        run = whole.shape[3]
        for k, tile in enumerate((conc, left)):
            for i, t in enumerate(swap_tile(tile, sub)):
                column = (i % halves * tiles + c) * SUBS
                at = column % run
                whole[column // run, k, i // halves, at : at + SUBS, :] = t
    for k in range(parts):
        blocks[k][...] = whole[lax.axis_index("narrow") ^ k]


def gather_kernel(parts, order, *refs):
    blocks = refs[:parts]
    *outs, sems = refs[parts:]
    copies = []
    for k, block in zip(order, blocks):
        origin = lax.axis_index("narrow") ^ k
        for i, out in enumerate(outs):
            copies.append(pltpu.make_async_copy(block.at[i], out.at[:, origin], sems.at[i, k]))
            copies[-1].start()
    for copy in copies:
        copy.wait()


def call(kernel, out_shape, args, scratch=(), hbm=(), free=(), hbm_out=(), name=None, aliases=None):
    def spec(i, hbm, free=()):
        return pl.BlockSpec(memory_space=pltpu.HBM if i in hbm else pl.ANY if i in free else pltpu.VMEM)

    single = not isinstance(out_shape, tuple)
    shapes = (out_shape,) if single else out_shape
    out = pl.pallas_call(
        kernel,
        out_shape=shapes,
        in_specs=[spec(i, hbm, free) for i in range(len(args))],
        out_specs=tuple(spec(i, hbm_out) for i in range(len(shapes))),
        scratch_shapes=list(scratch),
        name=name,
        input_output_aliases=aliases or {},
        compiler_params=pltpu.CompilerParams(vmem_limit_bytes=VMEM_LIMIT),
        cost_estimate=pl.CostEstimate(flops=1024, bytes_accessed=1024, transcendentals=0),
    )(*args)
    return out[0] if single else out


def local(populations, phase, porosity, napl, concentration, flags):
    layers, rows, width = phase.shape
    halves = SUBS // layers
    length = width // halves
    tiles = length // LANES
    parts = lax.axis_size("narrow")
    strips = lax.axis_size("wide") * parts
    both = ("wide", "narrow")
    pairs = (
        [(i, i ^ 1) for i in range(strips)],
        [(i, (i + 1 if i % 2 else i - 1) % strips) for i in range(strips)],
    )
    slab = (SUBS, length)
    ends = (parts, strips)
    run = width // LANES * SUBS // parts

    def hold(*shape, dtype=F32):
        return pltpu.VMEM(shape, dtype)

    def swap(chain, array):
        return lax.ppermute(array, both, pairs[chain])

    pop = to_view(populations)
    views = [to_view(a) for a in (phase, concentration, napl, porosity)]
    flat = views[0].shape
    chunks = pop.reshape(19, SUBS, tiles, SUBS, LANES)
    given = [pltpu.with_memory_space_constraint(a, pltpu.HBM) for a in (chunks, *views, flags)]
    popv, phv, cov, nav, pov, flv, row1, send = call(
        functools.partial(first_kernel, tiles, halves),
        (
            hold(*chunks.shape), hold(*flat, dtype=jnp.int32), hold(*flat), hold(*flat), hold(*flat),
            hold(*flags.shape, dtype=jnp.int32), hold(19, *slab), hold(14, *slab),
        ),
        given, scratch=(pltpu.VMEM((19, *slab), F32), pltpu.SemaphoreType.DMA((tiles + 5,))),
        hbm=range(6), name="first",
    )
    popv = popv.reshape(pop.shape)
    halo1 = head1 = swap(1, send)
    row0, send = call(
        functools.partial(second_kernel, tiles, halves), (hold(19, *slab), hold(14, *slab)), (popv, phv, send),
        scratch=(pltpu.VMEM((19, *slab), F32),), free=(2,), name="second",
    )
    halo0 = head0 = swap(0, send)
    g, fac, start, slabs, open_ends = call(
        functools.partial(first_inner_kernel, tiles, halves),
        (
            hold(19, rows, *slab), hold(rows, *slab), hold(19, rows, *slab), hold(3, rows, *slab),
            hold(2, *slab),
        ),
        (popv, phv, cov, nav, pov, flv, row0, row1), name="first_inner",
    )

    def inner_rows(g, after):
        return call(
            functools.partial(inner_kernel, tiles, halves), hold(19, rows, *slab), (g, fac, after), free=(2,),
            name="inner",
        )

    def arrive(chain, g, halo, head, after, new):
        return call(
            functools.partial(arrive_kernel, tiles, halves, chain), (hold(19, rows, *slab), hold(5, *slab)),
            (g, fac, halo, head, after, new), free=(4, 5), name=f"arrive{chain}", aliases={5: 0},
        )

    def far(chain, g, ghost, after):
        return call(
            functools.partial(far_kernel, tiles, halves, chain), (hold(19, *slab), hold(14, *slab)),
            (g, fac, ghost, slabs, after), scratch=(pltpu.VMEM((19, *slab), F32),), free=(4,), name=f"far{chain}",
        )

    def rim(chain, g, ghost, halo, after):
        return call(
            functools.partial(rim_kernel, tiles, halves, ends, chain),
            (hold(2, 3, *slab), hold(2, 2, *slab), hold(5, *slab)),
            (g, fac, ghost, u, slabs, halo, after), free=(6,), name=f"rim{chain}",
        )

    after = slabs
    for pair in range(LBM_STEPS // 2):
        new = inner_rows(g, after)
        if pair < LBM_STEPS // 2 - 1:
            later, ghost1 = arrive(1, g, halo1, head1, g, new)
            row1, send1 = far(1, later, ghost1, ghost1)
            halo1 = swap(1, send1)
            later, ghost0 = arrive(0, g, halo0, head0, send1, later)
            row0, send0 = far(0, later, ghost0, ghost0)
            halo0 = swap(0, send0)
            new = inner_rows(later, send0)
            g = call(
                put_kernel, hold(19, rows, *slab), (new, row0, row1), name="put", aliases={0: 0}, free=(0,)
            )
            after = g
    u = call(
        functools.partial(inner_speed_kernel, tiles, halves), hold(3, rows - 4, *slab), (new, fac, new),
        free=(2,), name="inner_speed",
    )
    later, ghost1 = arrive(1, g, halo1, head1, u, new)
    ue1, rim1, send1 = rim(1, later, ghost1, halo1, ghost1)
    there1 = swap(1, send1)
    g, ghost0 = arrive(0, g, halo0, head0, send1, later)
    ue0, rim0, send0 = rim(0, g, ghost0, halo0, ghost0)
    there0 = swap(0, send0)
    inner = call(
        functools.partial(early_kernel, tiles, halves), hold(2, rows - 4, *slab), (slabs, u, ue0, ue1),
        name="early",
    )
    mid = call(
        functools.partial(middle_kernel, tiles, halves), hold(rows - 6, *slab), (slabs, u, inner, rim0, rim1),
        name="middle",
    )
    out, token = call(
        functools.partial(final_kernel, tiles, halves),
        (jax.ShapeDtypeStruct((19, *flat), F32), hold(SUBS, LANES)),
        (g, fac, ghost0, ghost1, start, mid),
        scratch=(pltpu.VMEM((19, *flat), F32), pltpu.SemaphoreType.DMA((19,))),
        free=(5,), hbm_out=(0,), name="final",
    )
    late1 = call(
        functools.partial(late_kernel, tiles, halves, ends, 1), hold(4, *slab),
        (slabs, u, ue1, inner, rim1, halo1, open_ends, there1, token), free=(8,), name="late1",
    )
    late0 = call(
        functools.partial(late_kernel, tiles, halves, ends, 0), hold(4, *slab),
        (slabs, u, ue0, inner, rim0, halo0, open_ends, there0, late1), free=(8,), name="late0",
    )
    block = (2, layers, run, LANES)
    blocks = call(
        functools.partial(deal_kernel, tiles, halves, parts), tuple(hold(*block) for _ in range(parts)),
        (inner, rim0, rim1, late0, late1, mid),
        scratch=(pltpu.VMEM((parts, *block), F32),), name="deal",
    )
    order = [0, *range(2, parts), 1]
    came = [blocks[0]]
    for k in order[1:]:
        came.append(lax.ppermute(blocks[k], "narrow", [(i, i ^ k) for i in range(parts)]))
    tile = (layers, parts, run, LANES)
    conc_out, napl_out = call(
        functools.partial(gather_kernel, parts, order),
        (jax.ShapeDtypeStruct(tile, F32), jax.ShapeDtypeStruct(tile, F32)),
        came, scratch=(pltpu.SemaphoreType.DMA((2, parts)),), hbm_out=(0, 1), name="gather",
    )
    shape = (layers, rows * parts, width // parts)

    def tile_of(a):
        return from_view(a.reshape(layers * parts * run, LANES), shape)

    return from_view(out, populations.shape), tile_of(conc_out), tile_of(napl_out)


def solution(mesh):
    strip = P(None, ("wide", "narrow"), None)
    in_specs = (P(None, None, ("wide", "narrow"), None), strip, strip, strip, strip, P())
    tile = P(None, "wide", "narrow")
    out_specs = (P(None, None, ("wide", "narrow"), None), tile, tile)
    return jax.shard_map(local, mesh=mesh, in_specs=in_specs, out_specs=out_specs, check_vma=False)
```

```python
import functools

import jax
import jax.numpy as jnp
import numpy as np
from jax import lax
from jax.experimental import pallas as pl
from jax.experimental.pallas import tpu as pltpu
from jax.sharding import PartitionSpec as P

LBM_STEPS = 4
F32 = jnp.float32

DIRS = [
    (0, 0, 0), (1, 0, 0), (-1, 0, 0), (0, 1, 0), (0, -1, 0), (0, 0, 1), (0, 0, -1),
    (1, 1, 0), (-1, -1, 0), (1, -1, 0), (-1, 1, 0), (1, 0, 1), (-1, 0, -1), (1, 0, -1),
    (-1, 0, 1), (0, 1, 1), (0, -1, -1), (0, 1, -1), (0, -1, 1),
]
OPP = [0, 2, 1, 4, 3, 6, 5, 8, 7, 10, 9, 12, 11, 14, 13, 16, 15, 18, 17]
UP = [1, 7, 9, 11, 13]
DOWN = [2, 8, 10, 12, 14]
DIFFUSION = 0.15
TRANSFER = 0.3
DEPLETION = 0.5
FLOOR = 0.3
SUBS = 8
LANES = 128
VMEM_LIMIT = 16 * 1024 * 1024


def to_view(array):
    *lead, rows, width = array.shape
    n = len(lead)
    t = array.reshape(*lead, rows // SUBS, SUBS, width // LANES, LANES)
    t = t.transpose(*range(n), n, n + 2, n + 1, n + 3)
    return t.reshape(*lead[:-1], lead[-1] * rows * width // LANES, LANES)


def from_view(view, shape):
    *lead, rows, width = shape
    n = len(lead)
    t = view.reshape(*lead, rows // SUBS, width // LANES, SUBS, LANES)
    t = t.transpose(*range(n), n, n + 2, n + 1, n + 3)
    return t.reshape(shape)


def iotas():
    lane = lax.broadcasted_iota(jnp.int32, (SUBS, LANES), 1)
    sub = lax.broadcasted_iota(jnp.int32, (SUBS, LANES), 0)
    return lane, sub


def cut(c):
    return slice(c * LANES, (c + 1) * LANES)


def strided(tiles, c, x):
    return pl.ds(c * SUBS + x, SUBS, stride=tiles * SUBS)


def collide(f, fac):
    s = [f[2 * p + 1] + f[2 * p + 2] for p in range(9)]
    d = [f[2 * p + 1] - f[2 * p + 2] for p in range(9)]
    rho = f[0] + (((s[0] + s[1]) + (s[2] + s[3])) + ((s[4] + s[5]) + (s[6] + s[7])) + s[8])
    jx = d[0] + ((d[3] + d[4]) + (d[5] + d[6]))
    jy = d[1] + ((d[3] - d[4]) + (d[7] + d[8]))
    jz = d[2] + ((d[5] - d[6]) + (d[7] - d[8]))
    inv = fac / rho
    vx, vy, vz = jx * inv, jy * inv, jz * inv
    w1 = rho * np.float32(1.25 / 18)
    w2 = rho * np.float32(1.25 / 36)
    w4 = rho * np.float32(1.25 / 72)
    a1 = w1 - w1 * ((vx * vx + vy * vy + vz * vz) * np.float32(1.0 / 6))
    a2 = a1 * np.float32(0.5)
    post = [a1 * np.float32(6.0) - f[0] * np.float32(0.25)]
    axes = [vx, vy, vz, vx + vy, vx - vy, vx + vz, vx - vz, vy + vz, vy - vz]
    for p, v in enumerate(axes):
        wa, wh, base = (w1, w2, a1) if p < 3 else (w2, w4, a2)
        even = (base + (wh * v) * v) - s[p] * np.float32(0.125)
        odd = wa * v - d[p] * np.float32(0.125)
        post += [even + odd, even - odd]
    return post


def pull(load, q, c, tiles, halves, lane, sub):
    _, cross, layer = DIRS[q]
    v = load(q, c)
    if cross == 1:
        if c > 0:
            side = load(q, c - 1)
        else:
            side = jnp.where(sub % halves == 0, jnp.nan, pltpu.roll(load(q, tiles - 1), 1, 0))
        v = pltpu.roll(jnp.where(lane == LANES - 1, side, v), 1, 1)
    elif cross == -1:
        if c < tiles - 1:
            side = load(q, c + 1)
        else:
            side = jnp.where(sub % halves == halves - 1, jnp.nan, pltpu.roll(load(q, 0), SUBS - 1, 0))
        v = pltpu.roll(jnp.where(lane == 0, side, v), LANES - 1, 1)
    if layer:
        v = pltpu.roll(v, (layer * halves) % SUBS, 0)
    return v


def stream(g, lo, hi, x, c, tiles, halves, lane, sub, place):
    def load(q, cc):
        flow = DIRS[q][0]
        if flow == 1 and place == "first":
            return lo[UP.index(q), :, cut(cc)]
        if flow == -1 and place == "last":
            return hi[DOWN.index(q), :, cut(cc)]
        return g[q, x - flow, :, cut(cc)]

    f = [g[0, x, :, cut(c)]]
    for q in range(1, 19):
        v = pull(load, q, c, tiles, halves, lane, sub)
        f.append(jnp.where(v != v, g[OPP[q], x, :, cut(c)], v))
    return f


def drag(ph):
    return jnp.where(ph == 2, jnp.nan, jnp.where(ph == 1, np.float32(1.5), np.float32(3.0)))


def swap_tile(v, sub):
    v = list(v)
    for k in (4, 2, 1):
        low = sub & k == 0
        for i in range(SUBS):
            if not i & k:
                a, b = v[i], v[i + k]
                v[i] = jnp.where(low, a, pltpu.roll(b, k, 0))
                v[i + k] = jnp.where(low, pltpu.roll(a, SUBS - k, 0), b)
    return v


def upper(chain):
    odd = lax.rem(lax.axis_index("narrow"), 2) == 1
    return odd if chain else jnp.logical_not(odd)


def by_side(chain, side):
    pl.when(upper(chain))(lambda: side(True))
    pl.when(jnp.logical_not(upper(chain)))(lambda: side(False))


def pick(flag, a, b):
    return [jnp.where(flag, x, y) for x, y in zip(a, b)]


def start_row(tiles, pop, phase, x, row, c):
    at = strided(tiles, c, x)
    fc = drag(phase[at, :])
    post = collide([pop[q, at, :] for q in range(19)], fc)
    for q in range(19):
        row[q, :, cut(c)] = post[q]
    return fc


def look_ahead(tiles, halves, up, edge, beside, send):
    lane, sub = iotas()
    toward, back = (UP, DOWN) if up else (DOWN, UP)
    for c in range(tiles):
        sums = [None] * 3
        for q in range(19):
            if q in back:
                continue
            if q == 0:
                f = edge(0, c)
            else:
                f = pull(beside if q in toward else edge, q, c, tiles, halves, lane, sub)
                f = jnp.where(f != f, edge(OPP[q], c), f)
            if q in toward:
                i = toward.index(q)
                send[i, :, cut(c)] = edge(q, c)
                send[5 + i, :, cut(c)] = f
            else:
                for k, e in enumerate((1, *DIRS[q][1:])):
                    if e:
                        t = f if e > 0 else -f
                        sums[k] = t if sums[k] is None else sums[k] + t
        for k in range(3):
            send[10 + k, :, cut(c)] = sums[k]


def start_rows(tiles, halves, chain, pop, phase, row, send, beside, ready=None):
    up = upper(chain)
    x, inwards = jnp.where(up, SUBS - 1, 0), jnp.where(up, SUBS - 2, 1)
    for c in range(tiles):
        if ready is not None:
            ready(c)
        send[13, :, cut(c)] = start_row(tiles, pop, phase, x, row, c)
        start_row(tiles, pop, phase, inwards, beside, c)

    def side(up):
        look_ahead(
            tiles, halves, up, lambda q, c: row[q, :, cut(c)], lambda q, c: beside[q, :, cut(c)], send
        )

    by_side(chain, side)


def first_kernel(
    tiles, halves, pop_h, phase_h, conc_h, napl_h, poro_h, flags_h,
    pop, phase, conc, napl, poro, flags, row, send, beside, sems,
):
    small = [
        pltpu.make_async_copy(a, b, sems.at[tiles + i])
        for i, (a, b) in enumerate(
            ((phase_h, phase), (conc_h, conc), (poro_h, poro), (napl_h, napl), (flags_h, flags))
        )
    ]
    large = [pltpu.make_async_copy(pop_h.at[:, :, c], pop.at[:, :, c], sems.at[c]) for c in range(tiles)]
    small[0].start()
    for copy in large + small[1:]:
        copy.start()
    small[0].wait()
    flat = pop.reshape(pop.shape[0], SUBS * tiles * SUBS, LANES)
    start_rows(tiles, halves, 1, flat, phase, row, send, beside, ready=lambda c: large[c].wait())
    for copy in small[1:]:
        copy.wait()


def second_kernel(tiles, halves, pop, phase, after, row, send, beside):
    start_rows(tiles, halves, 0, pop, phase, row, send, beside)


def merge_rows(out, row0, row1, count):
    rows = out.shape[1]

    def side(up):
        for k in range(count):
            out[k, 0] = (row0 if up else row1)[k]
            out[k, rows - 1] = (row1 if up else row0)[k]

    by_side(1, side)


def first_inner_kernel(
    tiles, halves, pop, phase, conc, napl, poro, flags, row0, row1, g, fac, start, slabs, open_ends
):
    rows = g.shape[1]
    length = tiles * LANES
    _, sub = iotas()

    def to_slabs(read, write):
        for c in range(tiles):
            v = [read(pl.ds((i * tiles + c) * SUBS, SUBS)) for i in range(SUBS)]
            for x, t in enumerate(swap_tile(v, sub)):
                write(x, cut(c), t)

    def store(ref, k):
        def write(x, at, t):
            ref[k, x, :, at] = t

        return write

    def store_fac(x, at, t):
        fac[x, :, at] = t

    to_slabs(lambda at: drag(phase[at, :]), store_fac)

    def direction(q, _):
        to_slabs(lambda at: pop[q, at, :], store(start, q))
        return 0

    lax.fori_loop(0, 19, direction, 0)

    def row(x, _):
        for c in range(tiles):
            post = collide([start[q, x, :, cut(c)] for q in range(19)], fac[x, :, cut(c)])
            for q in range(19):
                g[q, x, :, cut(c)] = post[q]
        return 0

    lax.fori_loop(1, rows - 1, row, 0)
    merge_rows(g, row0, row1, 19)
    for k, ref in enumerate((conc, napl, poro)):
        to_slabs(lambda at, ref=ref: ref[at, :], store(slabs, k))
    for k in range(2):
        for z in range(SUBS // halves):
            for h in range(halves):
                line = flags[k, z : z + 1, h * length : (h + 1) * length]
                open_ends[k, z * halves + h : z * halves + h + 1, :] = line.astype(F32)


def inner_kernel(tiles, halves, g, fac, after, out):
    rows = g.shape[1]
    lane, sub = iotas()

    def row(x, _):
        for c in range(tiles):
            f = stream(g, None, None, x, c, tiles, halves, lane, sub, "mid")
            post = collide(f, fac[x, :, cut(c)])
            for q in range(19):
                out[q, x, :, cut(c)] = post[q]
        return 0

    lax.fori_loop(1, rows - 1, row, 0)


def put_kernel(inner, row0, row1, out):
    merge_rows(out, row0, row1, 19)


def arrive_kernel(tiles, halves, chain, g, fac, halo, first_halo, after, inner, out, ghost):
    rows = g.shape[1]
    lane, sub = iotas()

    def side(up):
        x = rows - 1 if up else 0
        lo, hi, place = (None, halo, "last") if up else (halo, None, "first")
        toward, back = (DOWN, UP) if up else (UP, DOWN)
        for c in range(tiles):
            post = collide(stream(g, lo, hi, x, c, tiles, halves, lane, sub, place), fac[x, :, cut(c)])
            for q in range(19):
                out[q, x, :, cut(c)] = post[q]
            near = [halo[5 + i, :, cut(c)] for i in range(5)]
            sums = [halo[10, :, cut(c)], None, halo[11, :, cut(c)], halo[12, :, cut(c)]]
            known = list(zip(toward, near))
            for i, q in enumerate(back):
                f = pull(lambda q, cc: g[q, x, :, cut(cc)], q, c, tiles, halves, lane, sub)
                known.append((q, jnp.where(f != f, halo[i, :, cut(c)], f)))
            for q, f in known:
                for k, e in enumerate((1, *DIRS[q])):
                    if e:
                        t = f if e > 0 else -f
                        sums[k] = t if sums[k] is None else sums[k] + t
            rho = sums[0]
            inv = first_halo[13, :, cut(c)] / rho
            v = [j * inv for j in sums[1:]]
            base = np.float32(1.0) - (v[0] * v[0] + v[1] * v[1] + v[2] * v[2]) * np.float32(1.0 / 6)
            for i, q in enumerate(toward):
                along = None
                for e, t in zip(DIRS[q], v):
                    if e:
                        t = t if e > 0 else -t
                        along = t if along is None else along + t
                weight = np.float32(1.25 / 18 if sum(map(abs, DIRS[q])) == 1 else 1.25 / 36)
                feq = (rho * weight) * (base + along * (along * np.float32(0.5) + np.float32(1.0)))
                ghost[i, :, cut(c)] = feq - near[i] * np.float32(0.25)

    by_side(chain, side)


def far_kernel(tiles, halves, chain, g, fac, halo, slabs, after, row, send, beside):
    rows = g.shape[1]
    lane, sub = iotas()

    def side(up):
        x, inwards = (rows - 1, rows - 2) if up else (0, 1)
        lo, hi, place = (None, halo, "last") if up else (halo, None, "first")
        for c in range(tiles):
            for at, ref, where in ((x, row, place), (inwards, beside, "mid")):
                f = stream(g, lo, hi, at, c, tiles, halves, lane, sub, where)
                post = collide(f, fac[at, :, cut(c)])
                for q in range(19):
                    ref[q, :, cut(c)] = post[q]
        look_ahead(
            tiles, halves, up, lambda q, c: row[q, :, cut(c)], lambda q, c: beside[q, :, cut(c)], send
        )
        send[13] = slabs[0, x]

    by_side(chain, side)


def speed(f, fc):
    s = [f[2 * p + 1] + f[2 * p + 2] for p in range(9)]
    d = [f[2 * p + 1] - f[2 * p + 2] for p in range(9)]
    rho = f[0] + (((s[0] + s[1]) + (s[2] + s[3])) + ((s[4] + s[5]) + (s[6] + s[7])) + s[8])
    jx = d[0] + ((d[3] + d[4]) + (d[5] + d[6]))
    jy = d[1] + ((d[3] - d[4]) + (d[7] + d[8]))
    jz = d[2] + ((d[5] - d[6]) + (d[7] - d[8]))
    inv = np.float32(1.0) / rho
    return [jnp.where(fc != fc, np.float32(0.0), j * inv) for j in (jz, jx, jy)]


def inner_speed_kernel(tiles, halves, g, fac, after, u):
    rows = g.shape[1]
    lane, sub = iotas()

    def row(x, _):
        for c in range(tiles):
            f = stream(g, None, None, x, c, tiles, halves, lane, sub, "mid")
            for i, v in enumerate(speed(f, fac[x, :, cut(c)])):
                u[i, x - 2, :, cut(c)] = v
        return 0

    lax.fori_loop(2, rows - 2, row, 0)


def final_kernel(tiles, halves, g, fac, halo0, halo1, start, after, out, buf, sems):
    rows = g.shape[1]
    lane, sub = iotas()
    odd = upper(1)

    def row_of(q, x):
        at = x - DIRS[q][0]
        if at < 0:
            return lambda qq, cc: jnp.where(
                odd, halo0[UP.index(qq), :, cut(cc)], halo1[UP.index(qq), :, cut(cc)]
            )
        if at >= rows:
            return lambda qq, cc: jnp.where(
                odd, halo1[DOWN.index(qq), :, cut(cc)], halo0[DOWN.index(qq), :, cut(cc)]
            )
        return lambda qq, cc: g[qq, at, :, cut(cc)]

    copies = []
    for q in range(19):
        for c in range(tiles):
            new = []
            for x in range(rows):
                fc = fac[x, :, cut(c)]
                if q == 0:
                    v = g[0, x, :, cut(c)]
                else:
                    v = pull(row_of(q, x), q, c, tiles, halves, lane, sub)
                    v = jnp.where(v != v, g[OPP[q], x, :, cut(c)], v)
                new.append(jnp.where(fc != fc, start[q, x, :, cut(c)], v))
            for i, t in enumerate(swap_tile(new, sub)):
                first = (i * tiles + c) * SUBS
                buf[q, first : first + SUBS, :] = t
        copy = pltpu.make_async_copy(buf.at[q], out.at[q], sems.at[q])
        copy.start()
        copies.append(copy)
    for copy in copies:
        copy.wait()


def slope(p, q):
    return np.float32(0.5) * (
        jnp.maximum(jnp.minimum(p, q), np.float32(0.0)) + jnp.minimum(jnp.maximum(p, q), np.float32(0.0))
    )


def loss(s, c):
    return [np.float32(TRANSFER) * a * (np.float32(1.0) - b) for a, b in zip(s, c)]


def ends_of(parts, strips):
    place = lax.axis_index("wide") * parts + lax.axis_index("narrow")
    return place == 0, place == strips - 1


ZERO = np.float32(0.0)


def each(f, *lists):
    return [f(*t) for t in zip(*lists)]


def less(a, b):
    return each(lambda x, y: x - y, a, b)


def times(a, b):
    return each(lambda x, y: x * y, a, b)


def face(w, va, vb, c, cn, sl, sn, dn):
    a = each(lambda w, x, y: w * np.float32(0.5) * (x + y), w, va, vb)
    return each(
        lambda a, w, c, cn, sl, sn, dn: a * jnp.where(a > 0, c + sl, cn - sn) - np.float32(DIFFUSION) * w * dn,
        a, w, c, cn, sl, sn, dn,
    )


def floored(p):
    return [jnp.maximum(t, np.float32(FLOOR)) for t in p]


class Step:
    def __init__(self, tiles, halves, conc, poro, flow, cross, napl):
        self.tiles, self.halves = tiles, halves
        self.lane, self.sub = iotas()
        self.conc, self.poro, self.flow = (self.keep(f) for f in (conc, poro, flow))
        self.cross, self.napl = cross, napl
        self.gap = self.keep(lambda r: less(self.conc(r + 1), self.conc(r)))
        self.lean = self.keep(lambda r: each(slope, self.gap(r - 1), self.gap(r)))

    @staticmethod
    def keep(f):
        seen = {}

        def get(r):
            if r not in seen:
                seen[r] = f(r)
            return seen[r]

        return get

    def after(self, v):
        out = []
        for c in range(self.tiles):
            if c < self.tiles - 1:
                side = v[c + 1]
            else:
                edge = self.sub % self.halves == self.halves - 1
                side = jnp.where(edge, ZERO, pltpu.roll(v[0], SUBS - 1, 0))
            out.append(pltpu.roll(jnp.where(self.lane == 0, side, v[c]), LANES - 1, 1))
        return out

    def before(self, v):
        out = []
        for c in range(self.tiles):
            if c > 0:
                side = v[c - 1]
            else:
                edge = self.sub % self.halves == 0
                side = jnp.where(edge, ZERO, pltpu.roll(v[self.tiles - 1], 1, 0))
            out.append(pltpu.roll(jnp.where(self.lane == LANES - 1, side, v[c]), 1, 1))
        return out

    def above(self, v):
        return [pltpu.roll(t, SUBS - self.halves, 0) for t in v]

    def below(self, v):
        return [pltpu.roll(t, self.halves, 0) for t in v]

    def flow_face(self, r):
        return face(
            times(self.poro(r), self.poro(r + 1)), self.flow(r), self.flow(r + 1), self.conc(r), self.conc(r + 1),
            self.lean(r), self.lean(r + 1), self.gap(r),
        )

    def run(self, r, low=True, high=True):
        c, p, s = self.conc(r), self.poro(r), self.napl(r)
        change = None
        if low:
            change = self.flow_face(r - 1)
        if high:
            out = self.flow_face(r)
            change = [-t for t in out] if change is None else less(change, out)
        vel = self.cross(r)
        for after, before, v, open_ends in (
            (self.after, self.before, vel[0], True), (self.above, self.below, vel[1], False),
        ):
            cn = after(c)
            dn = less(cn, c)
            dm = less(c, before(c)) if open_ends else before(dn)
            s0 = each(slope, dm, dn)
            flux = face(times(p, after(p)), v, after(v), c, cn, s0, after(s0), dn)
            change = each(lambda t, a, b: t + (a - b), change, before(flux), flux)
        rate = loss(s, c)
        cnew = each(lambda c, t, k, p: c + (t + k) / p, c, change, rate, floored(p))
        return cnew, each(lambda s, k: s - np.float32(DEPLETION) * k, s, rate)


def read(slab):
    return [slab[:, cut(c)] for c in range(slab.shape[1] // LANES)]


def write(slab, tiles):
    for c, t in enumerate(tiles):
        slab[:, cut(c)] = t


def early_kernel(tiles, halves, slabs, u, ue0, ue1, cs):
    rows = slabs.shape[1]
    odd = upper(1)

    def flow(r):
        if r == 1:
            return pick(odd, read(ue0.at[1, 1]), read(ue1.at[1, 1]))
        if r == rows - 2:
            return pick(odd, read(ue1.at[1, 1]), read(ue0.at[1, 1]))
        return read(u.at[1, r - 2])

    step = Step(
        tiles, halves, lambda r: read(slabs.at[0, r]), lambda r: read(slabs.at[2, r]), flow,
        lambda r: (read(u.at[2, r - 2]), read(u.at[0, r - 2])), lambda r: read(slabs.at[1, r]),
    )
    for r in range(2, rows - 2):
        for k, v in enumerate(step.run(r)):
            write(cs.at[k, r - 2], v)


def static_readers(ends, up, slabs, halo, there, flags):
    rows = slabs.shape[1]
    first, last = ends_of(*ends)

    def conc(r):
        if 0 <= r < rows:
            return read(slabs.at[0, r])
        beyond = read(halo.at[13] if r in (-1, rows) else there.at[3])
        return pick(last, read(slabs.at[0, rows - 1]), beyond) if up else [jnp.where(first, ZERO, t) for t in beyond]

    def poro(r):
        if 0 <= r < rows:
            return read(slabs.at[2, r])
        return pick(last if up else first, read(flags.at[1 if up else 0]), read(there.at[4]))

    return conc, poro


def rim_kernel(tiles, halves, ends, chain, g, fac, ghost, u, slabs, halo, after, ue, cs, send):
    rows = g.shape[1]
    lane, sub = iotas()

    def side(up):
        x, beside = (rows - 1, rows - 2) if up else (0, 1)
        lo, hi, place = (None, ghost, "last") if up else (ghost, None, "first")
        for n, (at, where) in enumerate(((x, place), (beside, "mid"))):
            for c in range(tiles):
                f = stream(g, lo, hi, at, c, tiles, halves, lane, sub, where)
                for i, v in enumerate(speed(f, fac[at, :, cut(c)])):
                    ue[n, i, :, cut(c)] = v
        conc, poro = static_readers(ends, up, slabs, halo, None, None)

        def vel(k, r):
            return read(ue.at[0 if r == x else 1, k] if r in (x, beside) else u.at[k, r - 2])

        step = Step(
            tiles, halves, conc, poro, lambda r: vel(1, r), lambda r: (vel(2, r), vel(0, r)),
            lambda r: read(slabs.at[1, r]),
        )
        edge = step.run(x, low=up, high=not up)
        inward = step.run(beside)
        for i, new in enumerate((edge, inward)):
            for k in range(2):
                write(cs.at[i, k], new[k])
            write(send.at[1 + i], new[0])
        send[0] = ue[0, 1]
        send[3] = slabs[0, beside]
        send[4] = slabs[2, x]

    by_side(chain, side)


def state_reader(rows, edge, inner, rims):
    def state(k, r):
        if r in (0, rows - 1):
            return edge(k, r)
        if r in (1, rows - 2):
            return rims(k, r)
        return read(inner.at[k, r - 2])

    return state


def middle_kernel(tiles, halves, slabs, u, inner, rim0, rim1, out):
    rows = slabs.shape[1]
    odd = upper(1)

    def rims(k, r):
        a, b = (rim0, rim1) if r == 1 else (rim1, rim0)
        return pick(odd, read(a.at[1, k]), read(b.at[1, k]))

    state = state_reader(rows, None, inner, rims)
    step = Step(
        tiles, halves, lambda r: state(0, r), lambda r: read(slabs.at[2, r]), lambda r: read(u.at[1, r - 2]),
        lambda r: (read(u.at[2, r - 2]), read(u.at[0, r - 2])), lambda r: state(1, r),
    )
    for r in range(3, rows - 3):
        write(out.at[r - 3], step.run(r)[0])


def late_kernel(
    tiles, halves, ends, chain, slabs, u, ue, inner, rim, halo, flags, there, after, out
):
    rows = slabs.shape[1]
    first, last = ends_of(*ends)

    def side(up):
        x = rows - 1 if up else 0
        beyond = rows if up else -1
        ghost = last if up else first
        conc, poro = static_readers(ends, up, slabs, halo, there, flags)

        def vel(k, r):
            if r == beyond:
                return pick(ghost, read(ue.at[0, 1]), read(there.at[0]))
            if r in (x, x - 1 if up else x + 1):
                return read(ue.at[0 if r == x else 1, k])
            return read(u.at[k, r - 2])

        def cross(r):
            return vel(2, r), vel(0, r)

        one = Step(tiles, halves, conc, poro, lambda r: vel(1, r), cross, None)
        flux = one.flow_face(x if up else -1)
        sign = np.float32(-1.0 if up else 1.0)
        edge = each(lambda c, f, p: c + sign * f / p, read(rim.at[0, 0]), flux, floored(poro(x)))
        outer = each(lambda c, f, p: c - sign * f / p, read(there.at[1]), flux, floored(poro(beyond)))
        second = read(there.at[2])
        if up:
            outer, second = pick(ghost, edge, outer), pick(ghost, edge, second)
        else:
            outer, second = ([jnp.where(ghost, ZERO, t) for t in v] for v in (outer, second))
        state = state_reader(
            rows, lambda k, r: read(rim.at[0, k]) if k else edge, inner, lambda k, r: read(rim.at[1, k])
        )

        def after_one(r):
            if r < 0 or r >= rows:
                return outer if r == beyond else second
            return state(0, r)

        two = Step(tiles, halves, after_one, poro, lambda r: vel(1, r), cross, lambda r: state(1, r))
        for i in range(3):
            new = two.run(rows - 1 - i if up else i)
            write(out.at[i], new[0])
            if i == 0:
                write(out.at[3], new[1])

    by_side(chain, side)


def deal_kernel(tiles, halves, parts, inner, rim0, rim1, late0, late1, mid, *refs):
    *blocks, whole = refs
    rows = inner.shape[1] + 4
    odd = upper(1)
    _, sub = iotas()
    for c in range(tiles):

        def ends_pick(a, b):
            return jnp.where(odd, a, b)

        lo = [ends_pick(late0[i, :, cut(c)], late1[i, :, cut(c)]) for i in range(4)]
        hi = [ends_pick(late1[i, :, cut(c)], late0[i, :, cut(c)]) for i in range(4)]
        conc = lo[:3] + [mid[r, :, cut(c)] for r in range(rows - 6)] + hi[2::-1]
        left = [lo[3]]
        for r in range(1, rows - 1):
            if r in (1, rows - 2):
                a, b = (rim0, rim1) if r == 1 else (rim1, rim0)
                cc, ss = (ends_pick(a[1, k, :, cut(c)], b[1, k, :, cut(c)]) for k in range(2))
            else:
                cc, ss = (inner[k, r - 2, :, cut(c)] for k in range(2))
            left.append(ss - np.float32(DEPLETION) * loss([ss], [cc])[0])
        left.append(hi[3])
        run = whole.shape[3]
        for k, tile in enumerate((conc, left)):
            for i, t in enumerate(swap_tile(tile, sub)):
                column = (i % halves * tiles + c) * SUBS
                at = column % run
                whole[column // run, k, i // halves, at : at + SUBS, :] = t
    for k in range(parts):
        blocks[k][...] = whole[lax.axis_index("narrow") ^ k]


def gather_kernel(parts, order, *refs):
    blocks = refs[:parts]
    *outs, sems = refs[parts:]
    copies = []
    for k, block in zip(order, blocks):
        origin = lax.axis_index("narrow") ^ k
        for i, out in enumerate(outs):
            copies.append(pltpu.make_async_copy(block.at[i], out.at[:, origin], sems.at[i, k]))
            copies[-1].start()
    for copy in copies:
        copy.wait()


def call(kernel, out_shape, args, scratch=(), hbm=(), free=(), hbm_out=(), name=None, aliases=None):
    def spec(i, hbm, free=()):
        return pl.BlockSpec(memory_space=pltpu.HBM if i in hbm else pl.ANY if i in free else pltpu.VMEM)

    single = not isinstance(out_shape, tuple)
    shapes = (out_shape,) if single else out_shape
    out = pl.pallas_call(
        kernel,
        out_shape=shapes,
        in_specs=[spec(i, hbm, free) for i in range(len(args))],
        out_specs=tuple(spec(i, hbm_out) for i in range(len(shapes))),
        scratch_shapes=list(scratch),
        name=name,
        input_output_aliases=aliases or {},
        compiler_params=pltpu.CompilerParams(vmem_limit_bytes=VMEM_LIMIT),
        cost_estimate=pl.CostEstimate(flops=1024, bytes_accessed=1024, transcendentals=0),
    )(*args)
    return out[0] if single else out


def local(populations, phase, porosity, napl, concentration, flags):
    layers, rows, width = phase.shape
    halves = SUBS // layers
    length = width // halves
    tiles = length // LANES
    parts = lax.axis_size("narrow")
    strips = lax.axis_size("wide") * parts
    both = ("wide", "narrow")
    pairs = (
        [(i, i ^ 1) for i in range(strips)],
        [(i, (i + 1 if i % 2 else i - 1) % strips) for i in range(strips)],
    )
    slab = (SUBS, length)
    ends = (parts, strips)
    run = width // LANES * SUBS // parts

    def hold(*shape, dtype=F32):
        return pltpu.VMEM(shape, dtype)

    def swap(chain, array):
        return lax.ppermute(array, both, pairs[chain])

    pop = to_view(populations)
    views = [to_view(a) for a in (phase, concentration, napl, porosity)]
    flat = views[0].shape
    chunks = pop.reshape(19, SUBS, tiles, SUBS, LANES)
    given = [pltpu.with_memory_space_constraint(a, pltpu.HBM) for a in (chunks, *views, flags)]
    popv, phv, cov, nav, pov, flv, row1, send = call(
        functools.partial(first_kernel, tiles, halves),
        (
            hold(*chunks.shape), hold(*flat, dtype=jnp.int32), hold(*flat), hold(*flat), hold(*flat),
            hold(*flags.shape, dtype=jnp.int32), hold(19, *slab), hold(14, *slab),
        ),
        given, scratch=(pltpu.VMEM((19, *slab), F32), pltpu.SemaphoreType.DMA((tiles + 5,))),
        hbm=range(6), name="first",
    )
    popv = popv.reshape(pop.shape)
    halo1 = head1 = swap(1, send)
    row0, send = call(
        functools.partial(second_kernel, tiles, halves), (hold(19, *slab), hold(14, *slab)), (popv, phv, send),
        scratch=(pltpu.VMEM((19, *slab), F32),), free=(2,), name="second",
    )
    halo0 = head0 = swap(0, send)
    g, fac, start, slabs, open_ends = call(
        functools.partial(first_inner_kernel, tiles, halves),
        (
            hold(19, rows, *slab), hold(rows, *slab), hold(19, rows, *slab), hold(3, rows, *slab),
            hold(2, *slab),
        ),
        (popv, phv, cov, nav, pov, flv, row0, row1), name="first_inner",
    )

    def inner_rows(g, after):
        return call(
            functools.partial(inner_kernel, tiles, halves), hold(19, rows, *slab), (g, fac, after), free=(2,),
            name="inner",
        )

    def arrive(chain, g, halo, head, after, new):
        return call(
            functools.partial(arrive_kernel, tiles, halves, chain), (hold(19, rows, *slab), hold(5, *slab)),
            (g, fac, halo, head, after, new), free=(4, 5), name=f"arrive{chain}", aliases={5: 0},
        )

    def far(chain, g, ghost, after):
        return call(
            functools.partial(far_kernel, tiles, halves, chain), (hold(19, *slab), hold(14, *slab)),
            (g, fac, ghost, slabs, after), scratch=(pltpu.VMEM((19, *slab), F32),), free=(4,), name=f"far{chain}",
        )

    def rim(chain, g, ghost, halo, after):
        return call(
            functools.partial(rim_kernel, tiles, halves, ends, chain),
            (hold(2, 3, *slab), hold(2, 2, *slab), hold(5, *slab)),
            (g, fac, ghost, u, slabs, halo, after), free=(6,), name=f"rim{chain}",
        )

    after = slabs
    for pair in range(LBM_STEPS // 2):
        new = inner_rows(g, after)
        if pair < LBM_STEPS // 2 - 1:
            later, ghost1 = arrive(1, g, halo1, head1, g, new)
            row1, send1 = far(1, later, ghost1, ghost1)
            halo1 = swap(1, send1)
            later, ghost0 = arrive(0, g, halo0, head0, send1, later)
            row0, send0 = far(0, later, ghost0, ghost0)
            halo0 = swap(0, send0)
            new = inner_rows(later, send0)
            g = call(
                put_kernel, hold(19, rows, *slab), (new, row0, row1), name="put", aliases={0: 0}, free=(0,)
            )
            after = g
    u = call(
        functools.partial(inner_speed_kernel, tiles, halves), hold(3, rows - 4, *slab), (new, fac, new),
        free=(2,), name="inner_speed",
    )
    later, ghost1 = arrive(1, g, halo1, head1, u, new)
    ue1, rim1, send1 = rim(1, later, ghost1, halo1, ghost1)
    there1 = swap(1, send1)
    g, ghost0 = arrive(0, g, halo0, head0, send1, later)
    ue0, rim0, send0 = rim(0, g, ghost0, halo0, ghost0)
    there0 = swap(0, send0)
    inner = call(
        functools.partial(early_kernel, tiles, halves), hold(2, rows - 4, *slab), (slabs, u, ue0, ue1),
        name="early",
    )
    mid = call(
        functools.partial(middle_kernel, tiles, halves), hold(rows - 6, *slab), (slabs, u, inner, rim0, rim1),
        name="middle",
    )
    late1 = call(
        functools.partial(late_kernel, tiles, halves, ends, 1), hold(4, *slab),
        (slabs, u, ue1, inner, rim1, halo1, open_ends, there1, mid), free=(8,), name="late1",
    )
    late0 = call(
        functools.partial(late_kernel, tiles, halves, ends, 0), hold(4, *slab),
        (slabs, u, ue0, inner, rim0, halo0, open_ends, there0, late1), free=(8,), name="late0",
    )
    block = (2, layers, run, LANES)
    blocks = call(
        functools.partial(deal_kernel, tiles, halves, parts), tuple(hold(*block) for _ in range(parts)),
        (inner, rim0, rim1, late0, late1, mid),
        scratch=(pltpu.VMEM((parts, *block), F32),), name="deal",
    )
    order = [0, *range(parts - 1, 0, -1)]
    came = [blocks[0]]
    for k in order[1:]:
        came.append(lax.ppermute(blocks[k], "narrow", [(i, i ^ k) for i in range(parts)]))
    out = call(
        functools.partial(final_kernel, tiles, halves),
        jax.ShapeDtypeStruct((19, *flat), F32),
        (g, fac, ghost0, ghost1, start, blocks[0]),
        scratch=(pltpu.VMEM((19, *flat), F32), pltpu.SemaphoreType.DMA((19,))),
        free=(5,), hbm_out=(0,), name="final",
    )
    tile = (layers, parts, run, LANES)
    conc_out, napl_out = call(
        functools.partial(gather_kernel, parts, order),
        (jax.ShapeDtypeStruct(tile, F32), jax.ShapeDtypeStruct(tile, F32)),
        came, scratch=(pltpu.SemaphoreType.DMA((2, parts)),), hbm_out=(0, 1), name="gather",
    )
    shape = (layers, rows * parts, width // parts)

    def tile_of(a):
        return from_view(a.reshape(layers * parts * run, LANES), shape)

    return from_view(out, populations.shape), tile_of(conc_out), tile_of(napl_out)


def solution(mesh):
    strip = P(None, ("wide", "narrow"), None)
    in_specs = (P(None, None, ("wide", "narrow"), None), strip, strip, strip, strip, P())
    tile = P(None, "wide", "narrow")
    out_specs = (P(None, None, ("wide", "narrow"), None), tile, tile)
    return jax.shard_map(local, mesh=mesh, in_specs=in_specs, out_specs=out_specs, check_vma=False)
```

```python
import functools

import jax
import jax.numpy as jnp
import numpy as np
from jax import lax
from jax.experimental import pallas as pl
from jax.experimental.pallas import tpu as pltpu
from jax.sharding import PartitionSpec as P

LBM_STEPS = 4
F32 = jnp.float32

DIRS = [
    (0, 0, 0), (1, 0, 0), (-1, 0, 0), (0, 1, 0), (0, -1, 0), (0, 0, 1), (0, 0, -1),
    (1, 1, 0), (-1, -1, 0), (1, -1, 0), (-1, 1, 0), (1, 0, 1), (-1, 0, -1), (1, 0, -1),
    (-1, 0, 1), (0, 1, 1), (0, -1, -1), (0, 1, -1), (0, -1, 1),
]
OPP = [0, 2, 1, 4, 3, 6, 5, 8, 7, 10, 9, 12, 11, 14, 13, 16, 15, 18, 17]
UP = [1, 7, 9, 11, 13]
DOWN = [2, 8, 10, 12, 14]
DIFFUSION = 0.15
TRANSFER = 0.3
DEPLETION = 0.5
FLOOR = 0.3
SUBS = 8
LANES = 128
VMEM_LIMIT = 16 * 1024 * 1024


def to_view(array):
    *lead, rows, width = array.shape
    n = len(lead)
    t = array.reshape(*lead, rows // SUBS, SUBS, width // LANES, LANES)
    t = t.transpose(*range(n), n, n + 2, n + 1, n + 3)
    return t.reshape(*lead[:-1], lead[-1] * rows * width // LANES, LANES)


def from_view(view, shape):
    *lead, rows, width = shape
    n = len(lead)
    t = view.reshape(*lead, rows // SUBS, width // LANES, SUBS, LANES)
    t = t.transpose(*range(n), n, n + 2, n + 1, n + 3)
    return t.reshape(shape)


def iotas():
    lane = lax.broadcasted_iota(jnp.int32, (SUBS, LANES), 1)
    sub = lax.broadcasted_iota(jnp.int32, (SUBS, LANES), 0)
    return lane, sub


def cut(c):
    return slice(c * LANES, (c + 1) * LANES)


def strided(tiles, c, x):
    return pl.ds(c * SUBS + x, SUBS, stride=tiles * SUBS)


def collide(f, fac):
    s = [f[2 * p + 1] + f[2 * p + 2] for p in range(9)]
    d = [f[2 * p + 1] - f[2 * p + 2] for p in range(9)]
    rho = f[0] + (((s[0] + s[1]) + (s[2] + s[3])) + ((s[4] + s[5]) + (s[6] + s[7])) + s[8])
    jx = d[0] + ((d[3] + d[4]) + (d[5] + d[6]))
    jy = d[1] + ((d[3] - d[4]) + (d[7] + d[8]))
    jz = d[2] + ((d[5] - d[6]) + (d[7] - d[8]))
    inv = fac / rho
    vx, vy, vz = jx * inv, jy * inv, jz * inv
    w1 = rho * np.float32(1.25 / 18)
    w2 = rho * np.float32(1.25 / 36)
    w4 = rho * np.float32(1.25 / 72)
    a1 = w1 - w1 * ((vx * vx + vy * vy + vz * vz) * np.float32(1.0 / 6))
    a2 = a1 * np.float32(0.5)
    post = [a1 * np.float32(6.0) - f[0] * np.float32(0.25)]
    axes = [vx, vy, vz, vx + vy, vx - vy, vx + vz, vx - vz, vy + vz, vy - vz]
    for p, v in enumerate(axes):
        wa, wh, base = (w1, w2, a1) if p < 3 else (w2, w4, a2)
        even = (base + (wh * v) * v) - s[p] * np.float32(0.125)
        odd = wa * v - d[p] * np.float32(0.125)
        post += [even + odd, even - odd]
    return post


def pull(load, q, c, tiles, halves, lane, sub):
    _, cross, layer = DIRS[q]
    v = load(q, c)
    if cross == 1:
        if c > 0:
            side = load(q, c - 1)
        else:
            side = jnp.where(sub % halves == 0, jnp.nan, pltpu.roll(load(q, tiles - 1), 1, 0))
        v = pltpu.roll(jnp.where(lane == LANES - 1, side, v), 1, 1)
    elif cross == -1:
        if c < tiles - 1:
            side = load(q, c + 1)
        else:
            side = jnp.where(sub % halves == halves - 1, jnp.nan, pltpu.roll(load(q, 0), SUBS - 1, 0))
        v = pltpu.roll(jnp.where(lane == 0, side, v), LANES - 1, 1)
    if layer:
        v = pltpu.roll(v, (layer * halves) % SUBS, 0)
    return v


def stream(g, lo, hi, x, c, tiles, halves, lane, sub, place):
    def load(q, cc):
        flow = DIRS[q][0]
        if flow == 1 and place == "first":
            return lo[UP.index(q), :, cut(cc)]
        if flow == -1 and place == "last":
            return hi[DOWN.index(q), :, cut(cc)]
        return g[q, x - flow, :, cut(cc)]

    f = [g[0, x, :, cut(c)]]
    for q in range(1, 19):
        v = pull(load, q, c, tiles, halves, lane, sub)
        f.append(jnp.where(v != v, g[OPP[q], x, :, cut(c)], v))
    return f


def drag(ph):
    return jnp.where(ph == 2, jnp.nan, jnp.where(ph == 1, np.float32(1.5), np.float32(3.0)))


def swap_tile(v, sub):
    v = list(v)
    for k in (4, 2, 1):
        low = sub & k == 0
        for i in range(SUBS):
            if not i & k:
                a, b = v[i], v[i + k]
                v[i] = jnp.where(low, a, pltpu.roll(b, k, 0))
                v[i + k] = jnp.where(low, pltpu.roll(a, SUBS - k, 0), b)
    return v


def upper(chain):
    odd = lax.rem(lax.axis_index("narrow"), 2) == 1
    return odd if chain else jnp.logical_not(odd)


def by_side(chain, side):
    pl.when(upper(chain))(lambda: side(True))
    pl.when(jnp.logical_not(upper(chain)))(lambda: side(False))


def pick(flag, a, b):
    return [jnp.where(flag, x, y) for x, y in zip(a, b)]


def start_row(tiles, pop, phase, x, row, c):
    at = strided(tiles, c, x)
    fc = drag(phase[at, :])
    post = collide([pop[q, at, :] for q in range(19)], fc)
    for q in range(19):
        row[q, :, cut(c)] = post[q]
    return fc


def look_ahead(tiles, halves, up, edge, beside, send):
    lane, sub = iotas()
    toward, back = (UP, DOWN) if up else (DOWN, UP)
    for c in range(tiles):
        sums = [None] * 3
        for q in range(19):
            if q in back:
                continue
            if q == 0:
                f = edge(0, c)
            else:
                f = pull(beside if q in toward else edge, q, c, tiles, halves, lane, sub)
                f = jnp.where(f != f, edge(OPP[q], c), f)
            if q in toward:
                i = toward.index(q)
                send[i, :, cut(c)] = edge(q, c)
                send[5 + i, :, cut(c)] = f
            else:
                for k, e in enumerate((1, *DIRS[q][1:])):
                    if e:
                        t = f if e > 0 else -f
                        sums[k] = t if sums[k] is None else sums[k] + t
        for k in range(3):
            send[10 + k, :, cut(c)] = sums[k]


def start_rows(tiles, halves, chain, pop, phase, row, send, beside, ready=None):
    up = upper(chain)
    x, inwards = jnp.where(up, SUBS - 1, 0), jnp.where(up, SUBS - 2, 1)
    for c in range(tiles):
        if ready is not None:
            ready(c)
        send[13, :, cut(c)] = start_row(tiles, pop, phase, x, row, c)
        start_row(tiles, pop, phase, inwards, beside, c)

    def side(up):
        look_ahead(
            tiles, halves, up, lambda q, c: row[q, :, cut(c)], lambda q, c: beside[q, :, cut(c)], send
        )

    by_side(chain, side)


def first_kernel(
    tiles, halves, pop_h, phase_h, conc_h, napl_h, poro_h, flags_h,
    pop, phase, conc, napl, poro, flags, row, send, beside, sems,
):
    small = [
        pltpu.make_async_copy(a, b, sems.at[tiles + i])
        for i, (a, b) in enumerate(
            ((phase_h, phase), (conc_h, conc), (poro_h, poro), (napl_h, napl), (flags_h, flags))
        )
    ]
    large = [pltpu.make_async_copy(pop_h.at[:, :, c], pop.at[:, :, c], sems.at[c]) for c in range(tiles)]
    small[0].start()
    for copy in large + small[1:]:
        copy.start()
    small[0].wait()
    flat = pop.reshape(pop.shape[0], SUBS * tiles * SUBS, LANES)
    start_rows(tiles, halves, 1, flat, phase, row, send, beside, ready=lambda c: large[c].wait())
    for copy in small[1:]:
        copy.wait()


def second_kernel(tiles, halves, pop, phase, after, row, send, beside):
    start_rows(tiles, halves, 0, pop, phase, row, send, beside)


def merge_rows(out, row0, row1, count):
    rows = out.shape[1]

    def side(up):
        for k in range(count):
            out[k, 0] = (row0 if up else row1)[k]
            out[k, rows - 1] = (row1 if up else row0)[k]

    by_side(1, side)


def first_inner_kernel(
    tiles, halves, pop, phase, conc, napl, poro, flags, row0, row1, planes, g, fac, start, slabs, open_ends, passed
):
    passed[...] = planes[...]
    rows = g.shape[1]
    length = tiles * LANES
    _, sub = iotas()

    def to_slabs(read, write):
        for c in range(tiles):
            v = [read(pl.ds((i * tiles + c) * SUBS, SUBS)) for i in range(SUBS)]
            for x, t in enumerate(swap_tile(v, sub)):
                write(x, cut(c), t)

    def store(ref, k):
        def write(x, at, t):
            ref[k, x, :, at] = t

        return write

    def store_fac(x, at, t):
        fac[x, :, at] = t

    to_slabs(lambda at: drag(phase[at, :]), store_fac)

    def direction(q, _):
        to_slabs(lambda at: pop[q, at, :], store(start, q))
        return 0

    lax.fori_loop(0, 19, direction, 0)

    def row(x, _):
        for c in range(tiles):
            post = collide([start[q, x, :, cut(c)] for q in range(19)], fac[x, :, cut(c)])
            for q in range(19):
                g[q, x, :, cut(c)] = post[q]
        return 0

    lax.fori_loop(1, rows - 1, row, 0)
    merge_rows(g, row0, row1, 19)
    for k, ref in enumerate((conc, napl, poro)):
        to_slabs(lambda at, ref=ref: ref[at, :], store(slabs, k))
    for k in range(2):
        for z in range(SUBS // halves):
            for h in range(halves):
                line = flags[k, z : z + 1, h * length : (h + 1) * length]
                open_ends[k, z * halves + h : z * halves + h + 1, :] = line.astype(F32)


def inner_kernel(tiles, halves, g, fac, after, out):
    rows = g.shape[1]
    lane, sub = iotas()

    def row(x, _):
        for c in range(tiles):
            f = stream(g, None, None, x, c, tiles, halves, lane, sub, "mid")
            post = collide(f, fac[x, :, cut(c)])
            for q in range(19):
                out[q, x, :, cut(c)] = post[q]
        return 0

    lax.fori_loop(1, rows - 1, row, 0)


def put_kernel(inner, row0, row1, planes, out, passed):
    passed[...] = planes[...]
    merge_rows(out, row0, row1, 19)


def arrive_kernel(tiles, halves, chain, g, fac, halo, first_halo, after, inner, out, ghost):
    rows = g.shape[1]
    lane, sub = iotas()

    def side(up):
        x = rows - 1 if up else 0
        lo, hi, place = (None, halo, "last") if up else (halo, None, "first")
        toward, back = (DOWN, UP) if up else (UP, DOWN)
        for c in range(tiles):
            post = collide(stream(g, lo, hi, x, c, tiles, halves, lane, sub, place), fac[x, :, cut(c)])
            for q in range(19):
                out[q, x, :, cut(c)] = post[q]
            near = [halo[5 + i, :, cut(c)] for i in range(5)]
            sums = [halo[10, :, cut(c)], None, halo[11, :, cut(c)], halo[12, :, cut(c)]]
            known = list(zip(toward, near))
            for i, q in enumerate(back):
                f = pull(lambda q, cc: g[q, x, :, cut(cc)], q, c, tiles, halves, lane, sub)
                known.append((q, jnp.where(f != f, halo[i, :, cut(c)], f)))
            for q, f in known:
                for k, e in enumerate((1, *DIRS[q])):
                    if e:
                        t = f if e > 0 else -f
                        sums[k] = t if sums[k] is None else sums[k] + t
            rho = sums[0]
            inv = first_halo[13, :, cut(c)] / rho
            v = [j * inv for j in sums[1:]]
            base = np.float32(1.0) - (v[0] * v[0] + v[1] * v[1] + v[2] * v[2]) * np.float32(1.0 / 6)
            for i, q in enumerate(toward):
                along = None
                for e, t in zip(DIRS[q], v):
                    if e:
                        t = t if e > 0 else -t
                        along = t if along is None else along + t
                weight = np.float32(1.25 / 18 if sum(map(abs, DIRS[q])) == 1 else 1.25 / 36)
                feq = (rho * weight) * (base + along * (along * np.float32(0.5) + np.float32(1.0)))
                ghost[i, :, cut(c)] = feq - near[i] * np.float32(0.25)

    by_side(chain, side)


def far_kernel(tiles, halves, chain, g, fac, halo, slabs, after, row, send, beside):
    rows = g.shape[1]
    lane, sub = iotas()

    def side(up):
        x, inwards = (rows - 1, rows - 2) if up else (0, 1)
        lo, hi, place = (None, halo, "last") if up else (halo, None, "first")
        for c in range(tiles):
            for at, ref, where in ((x, row, place), (inwards, beside, "mid")):
                f = stream(g, lo, hi, at, c, tiles, halves, lane, sub, where)
                post = collide(f, fac[at, :, cut(c)])
                for q in range(19):
                    ref[q, :, cut(c)] = post[q]
        look_ahead(
            tiles, halves, up, lambda q, c: row[q, :, cut(c)], lambda q, c: beside[q, :, cut(c)], send
        )
        send[13] = slabs[0, x]

    by_side(chain, side)


def speed(f, fc):
    s = [f[2 * p + 1] + f[2 * p + 2] for p in range(9)]
    d = [f[2 * p + 1] - f[2 * p + 2] for p in range(9)]
    rho = f[0] + (((s[0] + s[1]) + (s[2] + s[3])) + ((s[4] + s[5]) + (s[6] + s[7])) + s[8])
    jx = d[0] + ((d[3] + d[4]) + (d[5] + d[6]))
    jy = d[1] + ((d[3] - d[4]) + (d[7] + d[8]))
    jz = d[2] + ((d[5] - d[6]) + (d[7] - d[8]))
    inv = np.float32(1.0) / rho
    return [jnp.where(fc != fc, np.float32(0.0), j * inv) for j in (jz, jx, jy)]


def inner_speed_kernel(tiles, halves, g, fac, after, u):
    rows = g.shape[1]
    lane, sub = iotas()

    def row(x, _):
        for c in range(tiles):
            f = stream(g, None, None, x, c, tiles, halves, lane, sub, "mid")
            for i, v in enumerate(speed(f, fac[x, :, cut(c)])):
                u[i, x - 2, :, cut(c)] = v
        return 0

    lax.fori_loop(2, rows - 2, row, 0)


def final_kernel(tiles, halves, g, fac, halo0, halo1, start, after, out, token, buf, sems):
    rows = g.shape[1]
    lane, sub = iotas()
    odd = upper(1)
    token[...] = jnp.zeros(token.shape, F32)

    def row_of(q, x):
        at = x - DIRS[q][0]
        if at < 0:
            return lambda qq, cc: jnp.where(
                odd, halo0[UP.index(qq), :, cut(cc)], halo1[UP.index(qq), :, cut(cc)]
            )
        if at >= rows:
            return lambda qq, cc: jnp.where(
                odd, halo1[DOWN.index(qq), :, cut(cc)], halo0[DOWN.index(qq), :, cut(cc)]
            )
        return lambda qq, cc: g[qq, at, :, cut(cc)]

    copies = []
    for q in range(19):
        for c in range(tiles):
            new = []
            for x in range(rows):
                fc = fac[x, :, cut(c)]
                if q == 0:
                    v = g[0, x, :, cut(c)]
                else:
                    v = pull(row_of(q, x), q, c, tiles, halves, lane, sub)
                    v = jnp.where(v != v, g[OPP[q], x, :, cut(c)], v)
                new.append(jnp.where(fc != fc, start[q, x, :, cut(c)], v))
            for i, t in enumerate(swap_tile(new, sub)):
                first = (i * tiles + c) * SUBS
                buf[q, first : first + SUBS, :] = t
        copy = pltpu.make_async_copy(buf.at[q], out.at[q], sems.at[q])
        copy.start()
        copies.append(copy)
    for copy in copies:
        copy.wait()


def slope(p, q):
    return np.float32(0.5) * (
        jnp.maximum(jnp.minimum(p, q), np.float32(0.0)) + jnp.minimum(jnp.maximum(p, q), np.float32(0.0))
    )


def loss(s, c):
    return [np.float32(TRANSFER) * a * (np.float32(1.0) - b) for a, b in zip(s, c)]


def ends_of(parts, strips):
    place = lax.axis_index("wide") * parts + lax.axis_index("narrow")
    return place == 0, place == strips - 1


ZERO = np.float32(0.0)


def each(f, *lists):
    return [f(*t) for t in zip(*lists)]


def less(a, b):
    return each(lambda x, y: x - y, a, b)


def times(a, b):
    return each(lambda x, y: x * y, a, b)


def face(w, va, vb, c, cn, sl, sn, dn):
    a = each(lambda w, x, y: w * np.float32(0.5) * (x + y), w, va, vb)
    return each(
        lambda a, w, c, cn, sl, sn, dn: a * jnp.where(a > 0, c + sl, cn - sn) - np.float32(DIFFUSION) * w * dn,
        a, w, c, cn, sl, sn, dn,
    )


def floored(p):
    return [jnp.maximum(t, np.float32(FLOOR)) for t in p]


class Step:
    def __init__(self, tiles, halves, conc, poro, flow, cross, napl):
        self.tiles, self.halves = tiles, halves
        self.lane, self.sub = iotas()
        self.conc, self.poro, self.flow = (self.keep(f) for f in (conc, poro, flow))
        self.cross, self.napl = cross, napl
        self.gap = self.keep(lambda r: less(self.conc(r + 1), self.conc(r)))
        self.lean = self.keep(lambda r: each(slope, self.gap(r - 1), self.gap(r)))

    @staticmethod
    def keep(f):
        seen = {}

        def get(r):
            if r not in seen:
                seen[r] = f(r)
            return seen[r]

        return get

    def after(self, v):
        out = []
        for c in range(self.tiles):
            if c < self.tiles - 1:
                side = v[c + 1]
            else:
                edge = self.sub % self.halves == self.halves - 1
                side = jnp.where(edge, ZERO, pltpu.roll(v[0], SUBS - 1, 0))
            out.append(pltpu.roll(jnp.where(self.lane == 0, side, v[c]), LANES - 1, 1))
        return out

    def before(self, v):
        out = []
        for c in range(self.tiles):
            if c > 0:
                side = v[c - 1]
            else:
                edge = self.sub % self.halves == 0
                side = jnp.where(edge, ZERO, pltpu.roll(v[self.tiles - 1], 1, 0))
            out.append(pltpu.roll(jnp.where(self.lane == LANES - 1, side, v[c]), 1, 1))
        return out

    def above(self, v):
        return [pltpu.roll(t, SUBS - self.halves, 0) for t in v]

    def below(self, v):
        return [pltpu.roll(t, self.halves, 0) for t in v]

    def flow_face(self, r):
        return face(
            times(self.poro(r), self.poro(r + 1)), self.flow(r), self.flow(r + 1), self.conc(r), self.conc(r + 1),
            self.lean(r), self.lean(r + 1), self.gap(r),
        )

    def run(self, r, low=True, high=True):
        c, p, s = self.conc(r), self.poro(r), self.napl(r)
        change = None
        if low:
            change = self.flow_face(r - 1)
        if high:
            out = self.flow_face(r)
            change = [-t for t in out] if change is None else less(change, out)
        vel = self.cross(r)
        for after, before, v, open_ends in (
            (self.after, self.before, vel[0], True), (self.above, self.below, vel[1], False),
        ):
            cn = after(c)
            dn = less(cn, c)
            dm = less(c, before(c)) if open_ends else before(dn)
            s0 = each(slope, dm, dn)
            flux = face(times(p, after(p)), v, after(v), c, cn, s0, after(s0), dn)
            change = each(lambda t, a, b: t + (a - b), change, before(flux), flux)
        rate = loss(s, c)
        cnew = each(lambda c, t, k, p: c + (t + k) / p, c, change, rate, floored(p))
        return cnew, each(lambda s, k: s - np.float32(DEPLETION) * k, s, rate)


def read(slab):
    return [slab[:, cut(c)] for c in range(slab.shape[1] // LANES)]


def write(slab, tiles):
    for c, t in enumerate(tiles):
        slab[:, cut(c)] = t


def early_kernel(tiles, halves, slabs, u, ue0, ue1, cs):
    rows = slabs.shape[1]
    odd = upper(1)

    def flow(r):
        if r == 1:
            return pick(odd, read(ue0.at[1, 1]), read(ue1.at[1, 1]))
        if r == rows - 2:
            return pick(odd, read(ue1.at[1, 1]), read(ue0.at[1, 1]))
        return read(u.at[1, r - 2])

    step = Step(
        tiles, halves, lambda r: read(slabs.at[0, r]), lambda r: read(slabs.at[2, r]), flow,
        lambda r: (read(u.at[2, r - 2]), read(u.at[0, r - 2])), lambda r: read(slabs.at[1, r]),
    )
    for r in range(2, rows - 2):
        for k, v in enumerate(step.run(r)):
            write(cs.at[k, r - 2], v)


def static_readers(ends, up, slabs, halo, there, flags):
    rows = slabs.shape[1]
    first, last = ends_of(*ends)

    def conc(r):
        if 0 <= r < rows:
            return read(slabs.at[0, r])
        beyond = read(halo.at[13] if r in (-1, rows) else there.at[3])
        return pick(last, read(slabs.at[0, rows - 1]), beyond) if up else [jnp.where(first, ZERO, t) for t in beyond]

    def poro(r):
        if 0 <= r < rows:
            return read(slabs.at[2, r])
        return pick(last if up else first, read(flags.at[1 if up else 0]), read(there.at[4]))

    return conc, poro


def rim_kernel(tiles, halves, ends, chain, g, fac, ghost, u, slabs, halo, after, ue, cs, send):
    rows = g.shape[1]
    lane, sub = iotas()

    def side(up):
        x, beside = (rows - 1, rows - 2) if up else (0, 1)
        lo, hi, place = (None, ghost, "last") if up else (ghost, None, "first")
        for n, (at, where) in enumerate(((x, place), (beside, "mid"))):
            for c in range(tiles):
                f = stream(g, lo, hi, at, c, tiles, halves, lane, sub, where)
                for i, v in enumerate(speed(f, fac[at, :, cut(c)])):
                    ue[n, i, :, cut(c)] = v
        conc, poro = static_readers(ends, up, slabs, halo, None, None)

        def vel(k, r):
            return read(ue.at[0 if r == x else 1, k] if r in (x, beside) else u.at[k, r - 2])

        step = Step(
            tiles, halves, conc, poro, lambda r: vel(1, r), lambda r: (vel(2, r), vel(0, r)),
            lambda r: read(slabs.at[1, r]),
        )
        edge = step.run(x, low=up, high=not up)
        inward = step.run(beside)
        for i, new in enumerate((edge, inward)):
            for k in range(2):
                write(cs.at[i, k], new[k])
            write(send.at[1 + i], new[0])
        send[0] = ue[0, 1]
        send[3] = slabs[0, beside]
        send[4] = slabs[2, x]

    by_side(chain, side)


def state_reader(rows, edge, inner, rims):
    def state(k, r):
        if r in (0, rows - 1):
            return edge(k, r)
        if r in (1, rows - 2):
            return rims(k, r)
        return read(inner.at[k, r - 2])

    return state


def middle_kernel(tiles, halves, slabs, u, inner, rim0, rim1, out):
    rows = slabs.shape[1]
    odd = upper(1)

    def rims(k, r):
        a, b = (rim0, rim1) if r == 1 else (rim1, rim0)
        return pick(odd, read(a.at[1, k]), read(b.at[1, k]))

    state = state_reader(rows, None, inner, rims)
    step = Step(
        tiles, halves, lambda r: state(0, r), lambda r: read(slabs.at[2, r]), lambda r: read(u.at[1, r - 2]),
        lambda r: (read(u.at[2, r - 2]), read(u.at[0, r - 2])), lambda r: state(1, r),
    )
    for r in range(3, rows - 3):
        write(out.at[r - 3], step.run(r)[0])


def late_kernel(
    tiles, halves, ends, chain, slabs, u, ue, inner, rim, halo, flags, there, after, out
):
    rows = slabs.shape[1]
    first, last = ends_of(*ends)

    def side(up):
        x = rows - 1 if up else 0
        beyond = rows if up else -1
        ghost = last if up else first
        conc, poro = static_readers(ends, up, slabs, halo, there, flags)

        def vel(k, r):
            if r == beyond:
                return pick(ghost, read(ue.at[0, 1]), read(there.at[0]))
            if r in (x, x - 1 if up else x + 1):
                return read(ue.at[0 if r == x else 1, k])
            return read(u.at[k, r - 2])

        def cross(r):
            return vel(2, r), vel(0, r)

        one = Step(tiles, halves, conc, poro, lambda r: vel(1, r), cross, None)
        flux = one.flow_face(x if up else -1)
        sign = np.float32(-1.0 if up else 1.0)
        edge = each(lambda c, f, p: c + sign * f / p, read(rim.at[0, 0]), flux, floored(poro(x)))
        outer = each(lambda c, f, p: c - sign * f / p, read(there.at[1]), flux, floored(poro(beyond)))
        second = read(there.at[2])
        if up:
            outer, second = pick(ghost, edge, outer), pick(ghost, edge, second)
        else:
            outer, second = ([jnp.where(ghost, ZERO, t) for t in v] for v in (outer, second))
        state = state_reader(
            rows, lambda k, r: read(rim.at[0, k]) if k else edge, inner, lambda k, r: read(rim.at[1, k])
        )

        def after_one(r):
            if r < 0 or r >= rows:
                return outer if r == beyond else second
            return state(0, r)

        two = Step(tiles, halves, after_one, poro, lambda r: vel(1, r), cross, lambda r: state(1, r))
        for i in range(3):
            new = two.run(rows - 1 - i if up else i)
            write(out.at[i], new[0])
            if i == 0:
                write(out.at[3], new[1])

    by_side(chain, side)


def deal_kernel(tiles, halves, parts, inner, rim0, rim1, late0, late1, mid, *refs):
    *blocks, whole = refs
    rows = inner.shape[1] + 4
    odd = upper(1)
    _, sub = iotas()
    for c in range(tiles):

        def ends_pick(a, b):
            return jnp.where(odd, a, b)

        lo = [ends_pick(late0[i, :, cut(c)], late1[i, :, cut(c)]) for i in range(4)]
        hi = [ends_pick(late1[i, :, cut(c)], late0[i, :, cut(c)]) for i in range(4)]
        conc = lo[:3] + [mid[r, :, cut(c)] for r in range(rows - 6)] + hi[2::-1]
        left = [lo[3]]
        for r in range(1, rows - 1):
            if r in (1, rows - 2):
                a, b = (rim0, rim1) if r == 1 else (rim1, rim0)
                cc, ss = (ends_pick(a[1, k, :, cut(c)], b[1, k, :, cut(c)]) for k in range(2))
            else:
                cc, ss = (inner[k, r - 2, :, cut(c)] for k in range(2))
            left.append(ss - np.float32(DEPLETION) * loss([ss], [cc])[0])
        left.append(hi[3])
        run = whole.shape[3]
        for k, tile in enumerate((conc, left)):
            for i, t in enumerate(swap_tile(tile, sub)):
                column = (i % halves * tiles + c) * SUBS
                at = column % run
                whole[column // run, k, i // halves, at : at + SUBS, :] = t
    for k in range(parts):
        blocks[k][...] = whole[lax.axis_index("narrow") ^ k]


def gather_kernel(parts, order, *refs):
    blocks = refs[:parts]
    *outs, sems = refs[parts:]
    copies = []
    for k, block in zip(order, blocks):
        origin = lax.axis_index("narrow") ^ k
        for i, out in enumerate(outs):
            copies.append(pltpu.make_async_copy(block.at[i], out.at[:, origin], sems.at[i, k]))
            copies[-1].start()
    for copy in copies:
        copy.wait()


def call(kernel, out_shape, args, scratch=(), hbm=(), free=(), hbm_out=(), name=None, aliases=None):
    def spec(i, hbm, free=()):
        return pl.BlockSpec(memory_space=pltpu.HBM if i in hbm else pl.ANY if i in free else pltpu.VMEM)

    single = not isinstance(out_shape, tuple)
    shapes = (out_shape,) if single else out_shape
    out = pl.pallas_call(
        kernel,
        out_shape=shapes,
        in_specs=[spec(i, hbm, free) for i in range(len(args))],
        out_specs=tuple(spec(i, hbm_out) for i in range(len(shapes))),
        scratch_shapes=list(scratch),
        name=name,
        input_output_aliases=aliases or {},
        compiler_params=pltpu.CompilerParams(vmem_limit_bytes=VMEM_LIMIT),
        cost_estimate=pl.CostEstimate(flops=1024, bytes_accessed=1024, transcendentals=0),
    )(*args)
    return out[0] if single else out


def local(populations, phase, porosity, napl, concentration, flags):
    layers, rows, width = phase.shape
    halves = SUBS // layers
    length = width // halves
    tiles = length // LANES
    parts = lax.axis_size("narrow")
    strips = lax.axis_size("wide") * parts
    both = ("wide", "narrow")
    pairs = (
        [(i, i ^ 1) for i in range(strips)],
        [(i, (i + 1 if i % 2 else i - 1) % strips) for i in range(strips)],
    )
    slab = (SUBS, length)
    ends = (parts, strips)
    run = width // LANES * SUBS // parts

    def hold(*shape, dtype=F32):
        return pltpu.VMEM(shape, dtype)

    def swap(chain, array):
        return lax.ppermute(array, both, pairs[chain])

    pop = to_view(populations)
    views = [to_view(a) for a in (phase, concentration, napl, porosity)]
    flat = views[0].shape
    chunks = pop.reshape(19, SUBS, tiles, SUBS, LANES)
    given = [pltpu.with_memory_space_constraint(a, pltpu.HBM) for a in (chunks, *views, flags)]
    popv, phv, cov, nav, pov, flv, row1, send = call(
        functools.partial(first_kernel, tiles, halves),
        (
            hold(*chunks.shape), hold(*flat, dtype=jnp.int32), hold(*flat), hold(*flat), hold(*flat),
            hold(*flags.shape, dtype=jnp.int32), hold(19, *slab), hold(14, *slab),
        ),
        given, scratch=(pltpu.VMEM((19, *slab), F32), pltpu.SemaphoreType.DMA((tiles + 5,))),
        hbm=range(6), name="first",
    )
    popv = popv.reshape(pop.shape)
    halo1 = head1 = swap(1, send)
    row0, planes = call(
        functools.partial(second_kernel, tiles, halves), (hold(19, *slab), hold(14, *slab)), (popv, phv, send),
        scratch=(pltpu.VMEM((19, *slab), F32),), free=(2,), name="second",
    )
    g, fac, start, slabs, open_ends, send = call(
        functools.partial(first_inner_kernel, tiles, halves),
        (
            hold(19, rows, *slab), hold(rows, *slab), hold(19, rows, *slab), hold(3, rows, *slab),
            hold(2, *slab), hold(14, *slab),
        ),
        (popv, phv, cov, nav, pov, flv, row0, row1, planes), name="first_inner",
    )
    halo0 = head0 = swap(0, send)

    def inner_rows(g, after):
        return call(
            functools.partial(inner_kernel, tiles, halves), hold(19, rows, *slab), (g, fac, after), free=(2,),
            name="inner",
        )

    def arrive(chain, g, halo, head, after, new):
        return call(
            functools.partial(arrive_kernel, tiles, halves, chain), (hold(19, rows, *slab), hold(5, *slab)),
            (g, fac, halo, head, after, new), free=(4, 5), name=f"arrive{chain}", aliases={5: 0},
        )

    def far(chain, g, ghost, after):
        return call(
            functools.partial(far_kernel, tiles, halves, chain), (hold(19, *slab), hold(14, *slab)),
            (g, fac, ghost, slabs, after), scratch=(pltpu.VMEM((19, *slab), F32),), free=(4,), name=f"far{chain}",
        )

    def rim(chain, g, ghost, halo, after):
        return call(
            functools.partial(rim_kernel, tiles, halves, ends, chain),
            (hold(2, 3, *slab), hold(2, 2, *slab), hold(5, *slab)),
            (g, fac, ghost, u, slabs, halo, after), free=(6,), name=f"rim{chain}",
        )

    after = slabs
    for pair in range(LBM_STEPS // 2):
        new = inner_rows(g, after)
        if pair < LBM_STEPS // 2 - 1:
            later, ghost1 = arrive(1, g, halo1, head1, g, new)
            row1, send1 = far(1, later, ghost1, ghost1)
            halo1 = swap(1, send1)
            later, ghost0 = arrive(0, g, halo0, head0, send1, later)
            row0, planes = far(0, later, ghost0, ghost0)
            new = inner_rows(later, planes)
            g, send0 = call(
                put_kernel, (hold(19, rows, *slab), hold(14, *slab)), (new, row0, row1, planes), name="put",
                aliases={0: 0}, free=(0,),
            )
            halo0 = swap(0, send0)
            after = g
    u = call(
        functools.partial(inner_speed_kernel, tiles, halves), hold(3, rows - 4, *slab), (new, fac, new),
        free=(2,), name="inner_speed",
    )
    later, ghost1 = arrive(1, g, halo1, head1, u, new)
    ue1, rim1, send1 = rim(1, later, ghost1, halo1, ghost1)
    there1 = swap(1, send1)
    g, ghost0 = arrive(0, g, halo0, head0, send1, later)
    ue0, rim0, send0 = rim(0, g, ghost0, halo0, ghost0)
    there0 = swap(0, send0)
    inner = call(
        functools.partial(early_kernel, tiles, halves), hold(2, rows - 4, *slab), (slabs, u, ue0, ue1),
        name="early",
    )
    mid = call(
        functools.partial(middle_kernel, tiles, halves), hold(rows - 6, *slab), (slabs, u, inner, rim0, rim1),
        name="middle",
    )
    out, token = call(
        functools.partial(final_kernel, tiles, halves),
        (jax.ShapeDtypeStruct((19, *flat), F32), hold(SUBS, LANES)),
        (g, fac, ghost0, ghost1, start, mid),
        scratch=(pltpu.VMEM((19, *flat), F32), pltpu.SemaphoreType.DMA((19,))),
        free=(5,), hbm_out=(0,), name="final",
    )
    late1 = call(
        functools.partial(late_kernel, tiles, halves, ends, 1), hold(4, *slab),
        (slabs, u, ue1, inner, rim1, halo1, open_ends, there1, token), free=(8,), name="late1",
    )
    late0 = call(
        functools.partial(late_kernel, tiles, halves, ends, 0), hold(4, *slab),
        (slabs, u, ue0, inner, rim0, halo0, open_ends, there0, late1), free=(8,), name="late0",
    )
    block = (2, layers, run, LANES)
    blocks = call(
        functools.partial(deal_kernel, tiles, halves, parts), tuple(hold(*block) for _ in range(parts)),
        (inner, rim0, rim1, late0, late1, mid),
        scratch=(pltpu.VMEM((parts, *block), F32),), name="deal",
    )
    order = [0, *range(2, parts), 1]
    came = [blocks[0]]
    for k in order[1:]:
        came.append(lax.ppermute(blocks[k], "narrow", [(i, i ^ k) for i in range(parts)]))
    tile = (layers, parts, run, LANES)
    conc_out, napl_out = call(
        functools.partial(gather_kernel, parts, order),
        (jax.ShapeDtypeStruct(tile, F32), jax.ShapeDtypeStruct(tile, F32)),
        came, scratch=(pltpu.SemaphoreType.DMA((2, parts)),), hbm_out=(0, 1), name="gather",
    )
    shape = (layers, rows * parts, width // parts)

    def tile_of(a):
        return from_view(a.reshape(layers * parts * run, LANES), shape)

    return from_view(out, populations.shape), tile_of(conc_out), tile_of(napl_out)


def solution(mesh):
    strip = P(None, ("wide", "narrow"), None)
    in_specs = (P(None, None, ("wide", "narrow"), None), strip, strip, strip, strip, P())
    tile = P(None, "wide", "narrow")
    out_specs = (P(None, None, ("wide", "narrow"), None), tile, tile)
    return jax.shard_map(local, mesh=mesh, in_specs=in_specs, out_specs=out_specs, check_vma=False)
```

```python
import functools

import jax
import jax.numpy as jnp
import numpy as np
from jax import lax
from jax.experimental import pallas as pl
from jax.experimental.pallas import tpu as pltpu
from jax.sharding import PartitionSpec as P

LBM_STEPS = 4
F32 = jnp.float32

DIRS = [
    (0, 0, 0), (1, 0, 0), (-1, 0, 0), (0, 1, 0), (0, -1, 0), (0, 0, 1), (0, 0, -1),
    (1, 1, 0), (-1, -1, 0), (1, -1, 0), (-1, 1, 0), (1, 0, 1), (-1, 0, -1), (1, 0, -1),
    (-1, 0, 1), (0, 1, 1), (0, -1, -1), (0, 1, -1), (0, -1, 1),
]
OPP = [0, 2, 1, 4, 3, 6, 5, 8, 7, 10, 9, 12, 11, 14, 13, 16, 15, 18, 17]
UP = [1, 7, 9, 11, 13]
DOWN = [2, 8, 10, 12, 14]
DIFFUSION = 0.15
TRANSFER = 0.3
DEPLETION = 0.5
FLOOR = 0.3
SUBS = 8
LANES = 128
VMEM_LIMIT = 16 * 1024 * 1024


def to_view(array):
    *lead, rows, width = array.shape
    n = len(lead)
    t = array.reshape(*lead, rows // SUBS, SUBS, width // LANES, LANES)
    t = t.transpose(*range(n), n, n + 2, n + 1, n + 3)
    return t.reshape(*lead[:-1], lead[-1] * rows * width // LANES, LANES)


def from_view(view, shape):
    *lead, rows, width = shape
    n = len(lead)
    t = view.reshape(*lead, rows // SUBS, width // LANES, SUBS, LANES)
    t = t.transpose(*range(n), n, n + 2, n + 1, n + 3)
    return t.reshape(shape)


def iotas():
    lane = lax.broadcasted_iota(jnp.int32, (SUBS, LANES), 1)
    sub = lax.broadcasted_iota(jnp.int32, (SUBS, LANES), 0)
    return lane, sub


def cut(c):
    return slice(c * LANES, (c + 1) * LANES)


def strided(tiles, c, x):
    return pl.ds(c * SUBS + x, SUBS, stride=tiles * SUBS)


def collide(f, fac):
    s = [f[2 * p + 1] + f[2 * p + 2] for p in range(9)]
    d = [f[2 * p + 1] - f[2 * p + 2] for p in range(9)]
    rho = f[0] + (((s[0] + s[1]) + (s[2] + s[3])) + ((s[4] + s[5]) + (s[6] + s[7])) + s[8])
    jx = d[0] + ((d[3] + d[4]) + (d[5] + d[6]))
    jy = d[1] + ((d[3] - d[4]) + (d[7] + d[8]))
    jz = d[2] + ((d[5] - d[6]) + (d[7] - d[8]))
    inv = fac / rho
    vx, vy, vz = jx * inv, jy * inv, jz * inv
    w1 = rho * np.float32(1.25 / 18)
    w2 = rho * np.float32(1.25 / 36)
    w4 = rho * np.float32(1.25 / 72)
    a1 = w1 - w1 * ((vx * vx + vy * vy + vz * vz) * np.float32(1.0 / 6))
    a2 = a1 * np.float32(0.5)
    post = [a1 * np.float32(6.0) - f[0] * np.float32(0.25)]
    axes = [vx, vy, vz, vx + vy, vx - vy, vx + vz, vx - vz, vy + vz, vy - vz]
    for p, v in enumerate(axes):
        wa, wh, base = (w1, w2, a1) if p < 3 else (w2, w4, a2)
        even = (base + (wh * v) * v) - s[p] * np.float32(0.125)
        odd = wa * v - d[p] * np.float32(0.125)
        post += [even + odd, even - odd]
    return post


def pull(load, q, c, tiles, halves, lane, sub):
    _, cross, layer = DIRS[q]
    v = load(q, c)
    if cross == 1:
        if c > 0:
            side = load(q, c - 1)
        else:
            side = jnp.where(sub % halves == 0, jnp.nan, pltpu.roll(load(q, tiles - 1), 1, 0))
        v = pltpu.roll(jnp.where(lane == LANES - 1, side, v), 1, 1)
    elif cross == -1:
        if c < tiles - 1:
            side = load(q, c + 1)
        else:
            side = jnp.where(sub % halves == halves - 1, jnp.nan, pltpu.roll(load(q, 0), SUBS - 1, 0))
        v = pltpu.roll(jnp.where(lane == 0, side, v), LANES - 1, 1)
    if layer:
        v = pltpu.roll(v, (layer * halves) % SUBS, 0)
    return v


def stream(g, lo, hi, x, c, tiles, halves, lane, sub, place):
    def load(q, cc):
        flow = DIRS[q][0]
        if flow == 1 and place == "first":
            return lo[UP.index(q), :, cut(cc)]
        if flow == -1 and place == "last":
            return hi[DOWN.index(q), :, cut(cc)]
        return g[q, x - flow, :, cut(cc)]

    f = [g[0, x, :, cut(c)]]
    for q in range(1, 19):
        v = pull(load, q, c, tiles, halves, lane, sub)
        f.append(jnp.where(v != v, g[OPP[q], x, :, cut(c)], v))
    return f


def drag(ph):
    return jnp.where(ph == 2, jnp.nan, jnp.where(ph == 1, np.float32(1.5), np.float32(3.0)))


def swap_tile(v, sub):
    v = list(v)
    for k in (4, 2, 1):
        low = sub & k == 0
        for i in range(SUBS):
            if not i & k:
                a, b = v[i], v[i + k]
                v[i] = jnp.where(low, a, pltpu.roll(b, k, 0))
                v[i + k] = jnp.where(low, pltpu.roll(a, SUBS - k, 0), b)
    return v


def upper(chain):
    odd = lax.rem(lax.axis_index("narrow"), 2) == 1
    return odd if chain else jnp.logical_not(odd)


def by_side(chain, side):
    pl.when(upper(chain))(lambda: side(True))
    pl.when(jnp.logical_not(upper(chain)))(lambda: side(False))


def pick(flag, a, b):
    return [jnp.where(flag, x, y) for x, y in zip(a, b)]


def look_ahead(tiles, halves, up, edge, beside, send):
    lane, sub = iotas()
    toward, back = (UP, DOWN) if up else (DOWN, UP)
    for c in range(tiles):
        sums = [None] * 3
        for q in range(19):
            if q in back:
                continue
            if q == 0:
                f = edge(0, c)
            else:
                f = pull(beside if q in toward else edge, q, c, tiles, halves, lane, sub)
                f = jnp.where(f != f, edge(OPP[q], c), f)
            if q in toward:
                i = toward.index(q)
                send[i, :, cut(c)] = edge(q, c)
                send[5 + i, :, cut(c)] = f
            else:
                for k, e in enumerate((1, *DIRS[q][1:])):
                    if e:
                        t = f if e > 0 else -f
                        sums[k] = t if sums[k] is None else sums[k] + t
        for k in range(3):
            send[10 + k, :, cut(c)] = sums[k]


def start_rows(tiles, halves, chain, pairs, phase, row, send, beside, ready):
    def tile(c, up):
        for at, k, ref in ((SUBS - 1, 1, row), (SUBS - 2, 0, beside)) if up else ((0, 0, row), (1, 1, beside)):
            fc = drag(phase[strided(tiles, c, at), :])
            post = collide([pairs[c, q, :, k, :] for q in range(19)], fc)
            for q in range(19):
                ref[q, :, cut(c)] = post[q]
            if ref is row:
                send[13, :, cut(c)] = fc

    for c in range(tiles):
        ready(c)
        by_side(chain, functools.partial(tile, c))

    def side(up):
        look_ahead(
            tiles, halves, up, lambda q, c: row[q, :, cut(c)], lambda q, c: beside[q, :, cut(c)], send
        )

    by_side(chain, side)


def first_kernel(tiles, halves, pairs_h, phase_h, phase, row, send, mate, beside, mine, sems):
    labels = pltpu.make_async_copy(phase_h, phase, sems.at[2 * tiles])
    labels.start()
    up = upper(1)
    copies = []
    for chain, into in ((1, mine), (0, mate)):
        pair = jnp.where(up, 3, 0) if chain else jnp.where(up, 0, 3)
        for c in range(tiles):
            copies.append(
                pltpu.make_async_copy(pairs_h.at[:, :, c, pair], into.at[c], sems.at[(1 - chain) * tiles + c])
            )
            copies[-1].start()
    labels.wait()
    start_rows(tiles, halves, 1, mine, phase, row, send, beside, lambda c: copies[c].wait())
    for copy in copies[tiles:]:
        copy.wait()


def second_kernel(tiles, halves, mate, phase, after, row, send, beside):
    start_rows(tiles, halves, 0, mate, phase, row, send, beside, lambda c: None)


def merge_rows(out, row0, row1, count):
    rows = out.shape[1]

    def side(up):
        for k in range(count):
            out[k, 0] = (row0 if up else row1)[k]
            out[k, rows - 1] = (row1 if up else row0)[k]

    by_side(1, side)


def first_inner_kernel(
    tiles, halves, pop_h, conc_h, napl_h, poro_h, flags_h, phase, row0, row1, g, fac, start, slabs, open_ends,
    pop, conc, napl, poro, flags, sems,
):
    rows = g.shape[1]
    length = tiles * LANES
    _, sub = iotas()

    def load(q):
        return pltpu.make_async_copy(pop_h.at[q], pop.at[q], sems.at[q])

    for q in range(19):
        load(q).start()
    small = [
        pltpu.make_async_copy(a, b, sems.at[19 + i])
        for i, (a, b) in enumerate(((conc_h, conc), (napl_h, napl), (poro_h, poro), (flags_h, flags)))
    ]
    for copy in small:
        copy.start()

    def to_slabs(read, write):
        for c in range(tiles):
            v = [read(pl.ds((i * tiles + c) * SUBS, SUBS)) for i in range(SUBS)]
            for x, t in enumerate(swap_tile(v, sub)):
                write(x, cut(c), t)

    def store(ref, k):
        def write(x, at, t):
            ref[k, x, :, at] = t

        return write

    def store_fac(x, at, t):
        fac[x, :, at] = t

    to_slabs(lambda at: drag(phase[at, :]), store_fac)

    def direction(q, _):
        load(q).wait()
        to_slabs(lambda at: pop[q, at, :], store(start, q))
        return 0

    lax.fori_loop(0, 19, direction, 0)

    def row(x, _):
        for c in range(tiles):
            post = collide([start[q, x, :, cut(c)] for q in range(19)], fac[x, :, cut(c)])
            for q in range(19):
                g[q, x, :, cut(c)] = post[q]
        return 0

    lax.fori_loop(1, rows - 1, row, 0)
    merge_rows(g, row0, row1, 19)
    for copy in small:
        copy.wait()
    for k, ref in enumerate((conc, napl, poro)):
        to_slabs(lambda at, ref=ref: ref[at, :], store(slabs, k))
    for k in range(2):
        for z in range(SUBS // halves):
            for h in range(halves):
                line = flags[k, z : z + 1, h * length : (h + 1) * length]
                open_ends[k, z * halves + h : z * halves + h + 1, :] = line.astype(F32)


def inner_kernel(tiles, halves, g, fac, after, out):
    rows = g.shape[1]
    lane, sub = iotas()

    def row(x, _):
        for c in range(tiles):
            f = stream(g, None, None, x, c, tiles, halves, lane, sub, "mid")
            post = collide(f, fac[x, :, cut(c)])
            for q in range(19):
                out[q, x, :, cut(c)] = post[q]
        return 0

    lax.fori_loop(1, rows - 1, row, 0)


def put_kernel(inner, row0, row1, out):
    merge_rows(out, row0, row1, 19)


def arrive_kernel(tiles, halves, chain, g, fac, halo, first_halo, after, inner, out, ghost):
    rows = g.shape[1]
    lane, sub = iotas()

    def side(up):
        x = rows - 1 if up else 0
        lo, hi, place = (None, halo, "last") if up else (halo, None, "first")
        toward, back = (DOWN, UP) if up else (UP, DOWN)
        for c in range(tiles):
            post = collide(stream(g, lo, hi, x, c, tiles, halves, lane, sub, place), fac[x, :, cut(c)])
            for q in range(19):
                out[q, x, :, cut(c)] = post[q]
            near = [halo[5 + i, :, cut(c)] for i in range(5)]
            sums = [halo[10, :, cut(c)], None, halo[11, :, cut(c)], halo[12, :, cut(c)]]
            known = list(zip(toward, near))
            for i, q in enumerate(back):
                f = pull(lambda q, cc: g[q, x, :, cut(cc)], q, c, tiles, halves, lane, sub)
                known.append((q, jnp.where(f != f, halo[i, :, cut(c)], f)))
            for q, f in known:
                for k, e in enumerate((1, *DIRS[q])):
                    if e:
                        t = f if e > 0 else -f
                        sums[k] = t if sums[k] is None else sums[k] + t
            rho = sums[0]
            inv = first_halo[13, :, cut(c)] / rho
            v = [j * inv for j in sums[1:]]
            base = np.float32(1.0) - (v[0] * v[0] + v[1] * v[1] + v[2] * v[2]) * np.float32(1.0 / 6)
            for i, q in enumerate(toward):
                along = None
                for e, t in zip(DIRS[q], v):
                    if e:
                        t = t if e > 0 else -t
                        along = t if along is None else along + t
                weight = np.float32(1.25 / 18 if sum(map(abs, DIRS[q])) == 1 else 1.25 / 36)
                feq = (rho * weight) * (base + along * (along * np.float32(0.5) + np.float32(1.0)))
                ghost[i, :, cut(c)] = feq - near[i] * np.float32(0.25)

    by_side(chain, side)


def far_kernel(tiles, halves, chain, g, fac, halo, slabs, after, row, send, beside):
    rows = g.shape[1]
    lane, sub = iotas()

    def side(up):
        x, inwards = (rows - 1, rows - 2) if up else (0, 1)
        lo, hi, place = (None, halo, "last") if up else (halo, None, "first")
        for c in range(tiles):
            for at, ref, where in ((x, row, place), (inwards, beside, "mid")):
                f = stream(g, lo, hi, at, c, tiles, halves, lane, sub, where)
                post = collide(f, fac[at, :, cut(c)])
                for q in range(19):
                    ref[q, :, cut(c)] = post[q]
        look_ahead(
            tiles, halves, up, lambda q, c: row[q, :, cut(c)], lambda q, c: beside[q, :, cut(c)], send
        )
        send[13] = slabs[0, x]

    by_side(chain, side)


def speed(f, fc):
    s = [f[2 * p + 1] + f[2 * p + 2] for p in range(9)]
    d = [f[2 * p + 1] - f[2 * p + 2] for p in range(9)]
    rho = f[0] + (((s[0] + s[1]) + (s[2] + s[3])) + ((s[4] + s[5]) + (s[6] + s[7])) + s[8])
    jx = d[0] + ((d[3] + d[4]) + (d[5] + d[6]))
    jy = d[1] + ((d[3] - d[4]) + (d[7] + d[8]))
    jz = d[2] + ((d[5] - d[6]) + (d[7] - d[8]))
    inv = np.float32(1.0) / rho
    return [jnp.where(fc != fc, np.float32(0.0), j * inv) for j in (jz, jx, jy)]


def inner_speed_kernel(tiles, halves, g, fac, after, u):
    rows = g.shape[1]
    lane, sub = iotas()

    def row(x, _):
        for c in range(tiles):
            f = stream(g, None, None, x, c, tiles, halves, lane, sub, "mid")
            for i, v in enumerate(speed(f, fac[x, :, cut(c)])):
                u[i, x - 2, :, cut(c)] = v
        return 0

    lax.fori_loop(2, rows - 2, row, 0)


def final_kernel(tiles, halves, g, fac, halo0, halo1, start, after, out, buf, sems):
    rows = g.shape[1]
    lane, sub = iotas()
    odd = upper(1)

    def row_of(q, x):
        at = x - DIRS[q][0]
        if at < 0:
            return lambda qq, cc: jnp.where(
                odd, halo0[UP.index(qq), :, cut(cc)], halo1[UP.index(qq), :, cut(cc)]
            )
        if at >= rows:
            return lambda qq, cc: jnp.where(
                odd, halo1[DOWN.index(qq), :, cut(cc)], halo0[DOWN.index(qq), :, cut(cc)]
            )
        return lambda qq, cc: g[qq, at, :, cut(cc)]

    copies = []
    for q in range(19):
        for c in range(tiles):
            new = []
            for x in range(rows):
                fc = fac[x, :, cut(c)]
                if q == 0:
                    v = g[0, x, :, cut(c)]
                else:
                    v = pull(row_of(q, x), q, c, tiles, halves, lane, sub)
                    v = jnp.where(v != v, g[OPP[q], x, :, cut(c)], v)
                new.append(jnp.where(fc != fc, start[q, x, :, cut(c)], v))
            for i, t in enumerate(swap_tile(new, sub)):
                first = (i * tiles + c) * SUBS
                buf[q, first : first + SUBS, :] = t
        copy = pltpu.make_async_copy(buf.at[q], out.at[q], sems.at[q])
        copy.start()
        copies.append(copy)
    for copy in copies:
        copy.wait()


def slope(p, q):
    return np.float32(0.5) * (
        jnp.maximum(jnp.minimum(p, q), np.float32(0.0)) + jnp.minimum(jnp.maximum(p, q), np.float32(0.0))
    )


def loss(s, c):
    return [np.float32(TRANSFER) * a * (np.float32(1.0) - b) for a, b in zip(s, c)]


def ends_of(parts, strips):
    place = lax.axis_index("wide") * parts + lax.axis_index("narrow")
    return place == 0, place == strips - 1


ZERO = np.float32(0.0)


def each(f, *lists):
    return [f(*t) for t in zip(*lists)]


def less(a, b):
    return each(lambda x, y: x - y, a, b)


def times(a, b):
    return each(lambda x, y: x * y, a, b)


def face(w, va, vb, c, cn, sl, sn, dn):
    a = each(lambda w, x, y: w * np.float32(0.5) * (x + y), w, va, vb)
    return each(
        lambda a, w, c, cn, sl, sn, dn: a * jnp.where(a > 0, c + sl, cn - sn) - np.float32(DIFFUSION) * w * dn,
        a, w, c, cn, sl, sn, dn,
    )


def floored(p):
    return [jnp.maximum(t, np.float32(FLOOR)) for t in p]


class Step:
    def __init__(self, tiles, halves, conc, poro, flow, cross, napl):
        self.tiles, self.halves = tiles, halves
        self.lane, self.sub = iotas()
        self.conc, self.poro, self.flow = (self.keep(f) for f in (conc, poro, flow))
        self.cross, self.napl = cross, napl
        self.gap = self.keep(lambda r: less(self.conc(r + 1), self.conc(r)))
        self.lean = self.keep(lambda r: each(slope, self.gap(r - 1), self.gap(r)))

    @staticmethod
    def keep(f):
        seen = {}

        def get(r):
            if r not in seen:
                seen[r] = f(r)
            return seen[r]

        return get

    def after(self, v):
        out = []
        for c in range(self.tiles):
            if c < self.tiles - 1:
                side = v[c + 1]
            else:
                edge = self.sub % self.halves == self.halves - 1
                side = jnp.where(edge, ZERO, pltpu.roll(v[0], SUBS - 1, 0))
            out.append(pltpu.roll(jnp.where(self.lane == 0, side, v[c]), LANES - 1, 1))
        return out

    def before(self, v):
        out = []
        for c in range(self.tiles):
            if c > 0:
                side = v[c - 1]
            else:
                edge = self.sub % self.halves == 0
                side = jnp.where(edge, ZERO, pltpu.roll(v[self.tiles - 1], 1, 0))
            out.append(pltpu.roll(jnp.where(self.lane == LANES - 1, side, v[c]), 1, 1))
        return out

    def above(self, v):
        return [pltpu.roll(t, SUBS - self.halves, 0) for t in v]

    def below(self, v):
        return [pltpu.roll(t, self.halves, 0) for t in v]

    def flow_face(self, r):
        return face(
            times(self.poro(r), self.poro(r + 1)), self.flow(r), self.flow(r + 1), self.conc(r), self.conc(r + 1),
            self.lean(r), self.lean(r + 1), self.gap(r),
        )

    def run(self, r, low=True, high=True):
        c, p, s = self.conc(r), self.poro(r), self.napl(r)
        change = None
        if low:
            change = self.flow_face(r - 1)
        if high:
            out = self.flow_face(r)
            change = [-t for t in out] if change is None else less(change, out)
        vel = self.cross(r)
        for after, before, v, open_ends in (
            (self.after, self.before, vel[0], True), (self.above, self.below, vel[1], False),
        ):
            cn = after(c)
            dn = less(cn, c)
            dm = less(c, before(c)) if open_ends else before(dn)
            s0 = each(slope, dm, dn)
            flux = face(times(p, after(p)), v, after(v), c, cn, s0, after(s0), dn)
            change = each(lambda t, a, b: t + (a - b), change, before(flux), flux)
        rate = loss(s, c)
        cnew = each(lambda c, t, k, p: c + (t + k) / p, c, change, rate, floored(p))
        return cnew, each(lambda s, k: s - np.float32(DEPLETION) * k, s, rate)


def read(slab):
    return [slab[:, cut(c)] for c in range(slab.shape[1] // LANES)]


def write(slab, tiles):
    for c, t in enumerate(tiles):
        slab[:, cut(c)] = t


def early_kernel(tiles, halves, slabs, u, ue0, ue1, cs):
    rows = slabs.shape[1]
    odd = upper(1)

    def flow(r):
        if r == 1:
            return pick(odd, read(ue0.at[1, 1]), read(ue1.at[1, 1]))
        if r == rows - 2:
            return pick(odd, read(ue1.at[1, 1]), read(ue0.at[1, 1]))
        return read(u.at[1, r - 2])

    step = Step(
        tiles, halves, lambda r: read(slabs.at[0, r]), lambda r: read(slabs.at[2, r]), flow,
        lambda r: (read(u.at[2, r - 2]), read(u.at[0, r - 2])), lambda r: read(slabs.at[1, r]),
    )
    for r in range(2, rows - 2):
        for k, v in enumerate(step.run(r)):
            write(cs.at[k, r - 2], v)


def static_readers(ends, up, slabs, halo, there, flags):
    rows = slabs.shape[1]
    first, last = ends_of(*ends)

    def conc(r):
        if 0 <= r < rows:
            return read(slabs.at[0, r])
        beyond = read(halo.at[13] if r in (-1, rows) else there.at[3])
        return pick(last, read(slabs.at[0, rows - 1]), beyond) if up else [jnp.where(first, ZERO, t) for t in beyond]

    def poro(r):
        if 0 <= r < rows:
            return read(slabs.at[2, r])
        return pick(last if up else first, read(flags.at[1 if up else 0]), read(there.at[4]))

    return conc, poro


def rim_kernel(tiles, halves, ends, chain, g, fac, ghost, u, slabs, halo, after, ue, cs, send):
    rows = g.shape[1]
    lane, sub = iotas()

    def side(up):
        x, beside = (rows - 1, rows - 2) if up else (0, 1)
        lo, hi, place = (None, ghost, "last") if up else (ghost, None, "first")
        for n, (at, where) in enumerate(((x, place), (beside, "mid"))):
            for c in range(tiles):
                f = stream(g, lo, hi, at, c, tiles, halves, lane, sub, where)
                for i, v in enumerate(speed(f, fac[at, :, cut(c)])):
                    ue[n, i, :, cut(c)] = v
        conc, poro = static_readers(ends, up, slabs, halo, None, None)

        def vel(k, r):
            return read(ue.at[0 if r == x else 1, k] if r in (x, beside) else u.at[k, r - 2])

        step = Step(
            tiles, halves, conc, poro, lambda r: vel(1, r), lambda r: (vel(2, r), vel(0, r)),
            lambda r: read(slabs.at[1, r]),
        )
        edge = step.run(x, low=up, high=not up)
        inward = step.run(beside)
        for i, new in enumerate((edge, inward)):
            for k in range(2):
                write(cs.at[i, k], new[k])
            write(send.at[1 + i], new[0])
        send[0] = ue[0, 1]
        send[3] = slabs[0, beside]
        send[4] = slabs[2, x]

    by_side(chain, side)


def state_reader(rows, edge, inner, rims):
    def state(k, r):
        if r in (0, rows - 1):
            return edge(k, r)
        if r in (1, rows - 2):
            return rims(k, r)
        return read(inner.at[k, r - 2])

    return state


def middle_kernel(tiles, halves, slabs, u, inner, rim0, rim1, out):
    rows = slabs.shape[1]
    odd = upper(1)

    def rims(k, r):
        a, b = (rim0, rim1) if r == 1 else (rim1, rim0)
        return pick(odd, read(a.at[1, k]), read(b.at[1, k]))

    state = state_reader(rows, None, inner, rims)
    step = Step(
        tiles, halves, lambda r: state(0, r), lambda r: read(slabs.at[2, r]), lambda r: read(u.at[1, r - 2]),
        lambda r: (read(u.at[2, r - 2]), read(u.at[0, r - 2])), lambda r: state(1, r),
    )
    for r in range(3, rows - 3):
        write(out.at[r - 3], step.run(r)[0])


def late_kernel(
    tiles, halves, ends, chain, slabs, u, ue, inner, rim, halo, flags, there, after, out
):
    rows = slabs.shape[1]
    first, last = ends_of(*ends)

    def side(up):
        x = rows - 1 if up else 0
        beyond = rows if up else -1
        ghost = last if up else first
        conc, poro = static_readers(ends, up, slabs, halo, there, flags)

        def vel(k, r):
            if r == beyond:
                return pick(ghost, read(ue.at[0, 1]), read(there.at[0]))
            if r in (x, x - 1 if up else x + 1):
                return read(ue.at[0 if r == x else 1, k])
            return read(u.at[k, r - 2])

        def cross(r):
            return vel(2, r), vel(0, r)

        one = Step(tiles, halves, conc, poro, lambda r: vel(1, r), cross, None)
        flux = one.flow_face(x if up else -1)
        sign = np.float32(-1.0 if up else 1.0)
        edge = each(lambda c, f, p: c + sign * f / p, read(rim.at[0, 0]), flux, floored(poro(x)))
        outer = each(lambda c, f, p: c - sign * f / p, read(there.at[1]), flux, floored(poro(beyond)))
        second = read(there.at[2])
        if up:
            outer, second = pick(ghost, edge, outer), pick(ghost, edge, second)
        else:
            outer, second = ([jnp.where(ghost, ZERO, t) for t in v] for v in (outer, second))
        state = state_reader(
            rows, lambda k, r: read(rim.at[0, k]) if k else edge, inner, lambda k, r: read(rim.at[1, k])
        )

        def after_one(r):
            if r < 0 or r >= rows:
                return outer if r == beyond else second
            return state(0, r)

        two = Step(tiles, halves, after_one, poro, lambda r: vel(1, r), cross, lambda r: state(1, r))
        for i in range(3):
            new = two.run(rows - 1 - i if up else i)
            write(out.at[i], new[0])
            if i == 0:
                write(out.at[3], new[1])

    by_side(chain, side)


def deal_kernel(tiles, halves, parts, inner, rim0, rim1, late0, late1, mid, *refs):
    *blocks, whole = refs
    rows = inner.shape[1] + 4
    odd = upper(1)
    _, sub = iotas()
    for c in range(tiles):

        def ends_pick(a, b):
            return jnp.where(odd, a, b)

        lo = [ends_pick(late0[i, :, cut(c)], late1[i, :, cut(c)]) for i in range(4)]
        hi = [ends_pick(late1[i, :, cut(c)], late0[i, :, cut(c)]) for i in range(4)]
        conc = lo[:3] + [mid[r, :, cut(c)] for r in range(rows - 6)] + hi[2::-1]
        left = [lo[3]]
        for r in range(1, rows - 1):
            if r in (1, rows - 2):
                a, b = (rim0, rim1) if r == 1 else (rim1, rim0)
                cc, ss = (ends_pick(a[1, k, :, cut(c)], b[1, k, :, cut(c)]) for k in range(2))
            else:
                cc, ss = (inner[k, r - 2, :, cut(c)] for k in range(2))
            left.append(ss - np.float32(DEPLETION) * loss([ss], [cc])[0])
        left.append(hi[3])
        run = whole.shape[3]
        for k, tile in enumerate((conc, left)):
            for i, t in enumerate(swap_tile(tile, sub)):
                column = (i % halves * tiles + c) * SUBS
                at = column % run
                whole[column // run, k, i // halves, at : at + SUBS, :] = t
    for k in range(parts):
        blocks[k][...] = whole[lax.axis_index("narrow") ^ k]


def gather_kernel(parts, order, *refs):
    blocks = refs[:parts]
    *outs, sems = refs[parts:]
    copies = []
    for k, block in zip(order, blocks):
        origin = lax.axis_index("narrow") ^ k
        for i, out in enumerate(outs):
            copies.append(pltpu.make_async_copy(block.at[i], out.at[:, origin], sems.at[i, k]))
            copies[-1].start()
    for copy in copies:
        copy.wait()


def call(kernel, out_shape, args, scratch=(), hbm=(), free=(), hbm_out=(), name=None, aliases=None):
    def spec(i, hbm, free=()):
        return pl.BlockSpec(memory_space=pltpu.HBM if i in hbm else pl.ANY if i in free else pltpu.VMEM)

    single = not isinstance(out_shape, tuple)
    shapes = (out_shape,) if single else out_shape
    out = pl.pallas_call(
        kernel,
        out_shape=shapes,
        in_specs=[spec(i, hbm, free) for i in range(len(args))],
        out_specs=tuple(spec(i, hbm_out) for i in range(len(shapes))),
        scratch_shapes=list(scratch),
        name=name,
        input_output_aliases=aliases or {},
        compiler_params=pltpu.CompilerParams(vmem_limit_bytes=VMEM_LIMIT),
        cost_estimate=pl.CostEstimate(flops=1024, bytes_accessed=1024, transcendentals=0),
    )(*args)
    return out[0] if single else out


def local(populations, phase, porosity, napl, concentration, flags):
    layers, rows, width = phase.shape
    halves = SUBS // layers
    length = width // halves
    tiles = length // LANES
    parts = lax.axis_size("narrow")
    strips = lax.axis_size("wide") * parts
    both = ("wide", "narrow")
    pairs = (
        [(i, i ^ 1) for i in range(strips)],
        [(i, (i + 1 if i % 2 else i - 1) % strips) for i in range(strips)],
    )
    slab = (SUBS, length)
    ends = (parts, strips)
    run = width // LANES * SUBS // parts

    def hold(*shape, dtype=F32):
        return pltpu.VMEM(shape, dtype)

    def swap(chain, array):
        return lax.ppermute(array, both, pairs[chain])

    pop = to_view(populations)
    views = [to_view(a) for a in (phase, concentration, napl, porosity)]
    flat = views[0].shape
    pairs_of = pop.reshape(19, SUBS, tiles, SUBS // 2, 2, LANES)
    given = [pltpu.with_memory_space_constraint(a, pltpu.HBM) for a in (pairs_of, *views, pop, flags)]
    phv, row1, send, mate = call(
        functools.partial(first_kernel, tiles, halves),
        (
            hold(*flat, dtype=jnp.int32), hold(19, *slab), hold(14, *slab), hold(tiles, 19, SUBS, 2, LANES),
        ),
        given[:2],
        scratch=(
            pltpu.VMEM((19, *slab), F32), pltpu.VMEM((tiles, 19, SUBS, 2, LANES), F32),
            pltpu.SemaphoreType.DMA((2 * tiles + 1,)),
        ),
        hbm=range(2), name="first",
    )
    halo1 = head1 = swap(1, send)
    row0, send = call(
        functools.partial(second_kernel, tiles, halves), (hold(19, *slab), hold(14, *slab)), (mate, phv, send),
        scratch=(pltpu.VMEM((19, *slab), F32),), free=(2,), name="second",
    )
    halo0 = head0 = swap(0, send)
    g, fac, start, slabs, open_ends = call(
        functools.partial(first_inner_kernel, tiles, halves),
        (
            hold(19, rows, *slab), hold(rows, *slab), hold(19, rows, *slab), hold(3, rows, *slab),
            hold(2, *slab),
        ),
        (given[5], *given[2:5], given[6], phv, row0, row1),
        scratch=(
            pltpu.VMEM((19, *flat), F32), pltpu.VMEM(flat, F32), pltpu.VMEM(flat, F32), pltpu.VMEM(flat, F32),
            pltpu.VMEM(flags.shape, jnp.int32), pltpu.SemaphoreType.DMA((23,)),
        ),
        hbm=range(5), name="first_inner",
    )

    def inner_rows(g, after):
        return call(
            functools.partial(inner_kernel, tiles, halves), hold(19, rows, *slab), (g, fac, after), free=(2,),
            name="inner",
        )

    def arrive(chain, g, halo, head, after, new):
        return call(
            functools.partial(arrive_kernel, tiles, halves, chain), (hold(19, rows, *slab), hold(5, *slab)),
            (g, fac, halo, head, after, new), free=(4, 5), name=f"arrive{chain}", aliases={5: 0},
        )

    def far(chain, g, ghost, after):
        return call(
            functools.partial(far_kernel, tiles, halves, chain), (hold(19, *slab), hold(14, *slab)),
            (g, fac, ghost, slabs, after), scratch=(pltpu.VMEM((19, *slab), F32),), free=(4,), name=f"far{chain}",
        )

    def rim(chain, g, ghost, halo, after):
        return call(
            functools.partial(rim_kernel, tiles, halves, ends, chain),
            (hold(2, 3, *slab), hold(2, 2, *slab), hold(5, *slab)),
            (g, fac, ghost, u, slabs, halo, after), free=(6,), name=f"rim{chain}",
        )

    after = slabs
    for pair in range(LBM_STEPS // 2):
        new = inner_rows(g, after)
        if pair < LBM_STEPS // 2 - 1:
            later, ghost1 = arrive(1, g, halo1, head1, g, new)
            row1, send1 = far(1, later, ghost1, ghost1)
            halo1 = swap(1, send1)
            later, ghost0 = arrive(0, g, halo0, head0, send1, later)
            row0, send0 = far(0, later, ghost0, ghost0)
            halo0 = swap(0, send0)
            new = inner_rows(later, send0)
            g = call(
                put_kernel, hold(19, rows, *slab), (new, row0, row1), name="put", aliases={0: 0}, free=(0,)
            )
            after = g
    u = call(
        functools.partial(inner_speed_kernel, tiles, halves), hold(3, rows - 4, *slab), (new, fac, new),
        free=(2,), name="inner_speed",
    )
    later, ghost1 = arrive(1, g, halo1, head1, u, new)
    ue1, rim1, send1 = rim(1, later, ghost1, halo1, ghost1)
    there1 = swap(1, send1)
    g, ghost0 = arrive(0, g, halo0, head0, send1, later)
    ue0, rim0, send0 = rim(0, g, ghost0, halo0, ghost0)
    there0 = swap(0, send0)
    inner = call(
        functools.partial(early_kernel, tiles, halves), hold(2, rows - 4, *slab), (slabs, u, ue0, ue1),
        name="early",
    )
    mid = call(
        functools.partial(middle_kernel, tiles, halves), hold(rows - 6, *slab), (slabs, u, inner, rim0, rim1),
        name="middle",
    )
    late1 = call(
        functools.partial(late_kernel, tiles, halves, ends, 1), hold(4, *slab),
        (slabs, u, ue1, inner, rim1, halo1, open_ends, there1, mid), free=(8,), name="late1",
    )
    late0 = call(
        functools.partial(late_kernel, tiles, halves, ends, 0), hold(4, *slab),
        (slabs, u, ue0, inner, rim0, halo0, open_ends, there0, late1), free=(8,), name="late0",
    )
    block = (2, layers, run, LANES)
    blocks = call(
        functools.partial(deal_kernel, tiles, halves, parts), tuple(hold(*block) for _ in range(parts)),
        (inner, rim0, rim1, late0, late1, mid),
        scratch=(pltpu.VMEM((parts, *block), F32),), name="deal",
    )
    order = [0, *range(2, parts), 1]
    came = [blocks[0]]
    for k in order[1:]:
        came.append(lax.ppermute(blocks[k], "narrow", [(i, i ^ k) for i in range(parts)]))
    out = call(
        functools.partial(final_kernel, tiles, halves),
        jax.ShapeDtypeStruct((19, *flat), F32),
        (g, fac, ghost0, ghost1, start, blocks[0]),
        scratch=(pltpu.VMEM((19, *flat), F32), pltpu.SemaphoreType.DMA((19,))),
        free=(5,), hbm_out=(0,), name="final",
    )
    tile = (layers, parts, run, LANES)
    conc_out, napl_out = call(
        functools.partial(gather_kernel, parts, order),
        (jax.ShapeDtypeStruct(tile, F32), jax.ShapeDtypeStruct(tile, F32)),
        came, scratch=(pltpu.SemaphoreType.DMA((2, parts)),), hbm_out=(0, 1), name="gather",
    )
    shape = (layers, rows * parts, width // parts)

    def tile_of(a):
        return from_view(a.reshape(layers * parts * run, LANES), shape)

    return from_view(out, populations.shape), tile_of(conc_out), tile_of(napl_out)


def solution(mesh):
    strip = P(None, ("wide", "narrow"), None)
    in_specs = (P(None, None, ("wide", "narrow"), None), strip, strip, strip, strip, P())
    tile = P(None, "wide", "narrow")
    out_specs = (P(None, None, ("wide", "narrow"), None), tile, tile)
    return jax.shard_map(local, mesh=mesh, in_specs=in_specs, out_specs=out_specs, check_vma=False)
```

```python
import functools

import jax
import jax.numpy as jnp
import numpy as np
from jax import lax
from jax.experimental import pallas as pl
from jax.experimental.pallas import tpu as pltpu
from jax.sharding import PartitionSpec as P

LBM_STEPS = 4
F32 = jnp.float32

DIRS = [
    (0, 0, 0), (1, 0, 0), (-1, 0, 0), (0, 1, 0), (0, -1, 0), (0, 0, 1), (0, 0, -1),
    (1, 1, 0), (-1, -1, 0), (1, -1, 0), (-1, 1, 0), (1, 0, 1), (-1, 0, -1), (1, 0, -1),
    (-1, 0, 1), (0, 1, 1), (0, -1, -1), (0, 1, -1), (0, -1, 1),
]
OPP = [0, 2, 1, 4, 3, 6, 5, 8, 7, 10, 9, 12, 11, 14, 13, 16, 15, 18, 17]
UP = [1, 7, 9, 11, 13]
DOWN = [2, 8, 10, 12, 14]
DIFFUSION = 0.15
TRANSFER = 0.3
DEPLETION = 0.5
FLOOR = 0.3
SUBS = 8
LANES = 128
VMEM_LIMIT = 16 * 1024 * 1024


def to_view(array):
    *lead, rows, width = array.shape
    n = len(lead)
    t = array.reshape(*lead, rows // SUBS, SUBS, width // LANES, LANES)
    t = t.transpose(*range(n), n, n + 2, n + 1, n + 3)
    return t.reshape(*lead[:-1], lead[-1] * rows * width // LANES, LANES)


def from_view(view, shape):
    *lead, rows, width = shape
    n = len(lead)
    t = view.reshape(*lead, rows // SUBS, width // LANES, SUBS, LANES)
    t = t.transpose(*range(n), n, n + 2, n + 1, n + 3)
    return t.reshape(shape)


def iotas():
    lane = lax.broadcasted_iota(jnp.int32, (SUBS, LANES), 1)
    sub = lax.broadcasted_iota(jnp.int32, (SUBS, LANES), 0)
    return lane, sub


def cut(c):
    return slice(c * LANES, (c + 1) * LANES)


def strided(tiles, c, x):
    return pl.ds(c * SUBS + x, SUBS, stride=tiles * SUBS)


def collide(f, fac):
    s = [f[2 * p + 1] + f[2 * p + 2] for p in range(9)]
    d = [f[2 * p + 1] - f[2 * p + 2] for p in range(9)]
    rho = f[0] + (((s[0] + s[1]) + (s[2] + s[3])) + ((s[4] + s[5]) + (s[6] + s[7])) + s[8])
    jx = d[0] + ((d[3] + d[4]) + (d[5] + d[6]))
    jy = d[1] + ((d[3] - d[4]) + (d[7] + d[8]))
    jz = d[2] + ((d[5] - d[6]) + (d[7] - d[8]))
    inv = fac / rho
    vx, vy, vz = jx * inv, jy * inv, jz * inv
    w1 = rho * np.float32(1.25 / 18)
    w2 = rho * np.float32(1.25 / 36)
    w4 = rho * np.float32(1.25 / 72)
    a1 = w1 - w1 * ((vx * vx + vy * vy + vz * vz) * np.float32(1.0 / 6))
    a2 = a1 * np.float32(0.5)
    post = [a1 * np.float32(6.0) - f[0] * np.float32(0.25)]
    axes = [vx, vy, vz, vx + vy, vx - vy, vx + vz, vx - vz, vy + vz, vy - vz]
    for p, v in enumerate(axes):
        wa, wh, base = (w1, w2, a1) if p < 3 else (w2, w4, a2)
        even = (base + (wh * v) * v) - s[p] * np.float32(0.125)
        odd = wa * v - d[p] * np.float32(0.125)
        post += [even + odd, even - odd]
    return post


def pull(load, q, c, tiles, halves, lane, sub):
    _, cross, layer = DIRS[q]
    v = load(q, c)
    if cross == 1:
        if c > 0:
            side = load(q, c - 1)
        else:
            side = jnp.where(sub % halves == 0, jnp.nan, pltpu.roll(load(q, tiles - 1), 1, 0))
        v = pltpu.roll(jnp.where(lane == LANES - 1, side, v), 1, 1)
    elif cross == -1:
        if c < tiles - 1:
            side = load(q, c + 1)
        else:
            side = jnp.where(sub % halves == halves - 1, jnp.nan, pltpu.roll(load(q, 0), SUBS - 1, 0))
        v = pltpu.roll(jnp.where(lane == 0, side, v), LANES - 1, 1)
    if layer:
        v = pltpu.roll(v, (layer * halves) % SUBS, 0)
    return v


def stream(g, lo, hi, x, c, tiles, halves, lane, sub, place):
    def load(q, cc):
        flow = DIRS[q][0]
        if flow == 1 and place == "first":
            return lo[UP.index(q), :, cut(cc)]
        if flow == -1 and place == "last":
            return hi[DOWN.index(q), :, cut(cc)]
        return g[q, x - flow, :, cut(cc)]

    f = [g[0, x, :, cut(c)]]
    for q in range(1, 19):
        v = pull(load, q, c, tiles, halves, lane, sub)
        f.append(jnp.where(v != v, g[OPP[q], x, :, cut(c)], v))
    return f


def drag(ph):
    return jnp.where(ph == 2, jnp.nan, jnp.where(ph == 1, np.float32(1.5), np.float32(3.0)))


def swap_tile(v, sub):
    v = list(v)
    for k in (4, 2, 1):
        low = sub & k == 0
        for i in range(SUBS):
            if not i & k:
                a, b = v[i], v[i + k]
                v[i] = jnp.where(low, a, pltpu.roll(b, k, 0))
                v[i + k] = jnp.where(low, pltpu.roll(a, SUBS - k, 0), b)
    return v


def upper(chain):
    odd = lax.rem(lax.axis_index("narrow"), 2) == 1
    return odd if chain else jnp.logical_not(odd)


def by_side(chain, side):
    pl.when(upper(chain))(lambda: side(True))
    pl.when(jnp.logical_not(upper(chain)))(lambda: side(False))


def pick(flag, a, b):
    return [jnp.where(flag, x, y) for x, y in zip(a, b)]


def start_row(tiles, pop, phase, x, row, c):
    at = strided(tiles, c, x)
    fc = drag(phase[at, :])
    post = collide([pop[q, at, :] for q in range(19)], fc)
    for q in range(19):
        row[q, :, cut(c)] = post[q]
    return fc


def look_ahead(tiles, halves, up, edge, beside, send):
    lane, sub = iotas()
    toward, back = (UP, DOWN) if up else (DOWN, UP)
    for c in range(tiles):
        sums = [None] * 3
        for q in range(19):
            if q in back:
                continue
            if q == 0:
                f = edge(0, c)
            else:
                f = pull(beside if q in toward else edge, q, c, tiles, halves, lane, sub)
                f = jnp.where(f != f, edge(OPP[q], c), f)
            if q in toward:
                i = toward.index(q)
                send[i, :, cut(c)] = edge(q, c)
                send[5 + i, :, cut(c)] = f
            else:
                for k, e in enumerate((1, *DIRS[q][1:])):
                    if e:
                        t = f if e > 0 else -f
                        sums[k] = t if sums[k] is None else sums[k] + t
        for k in range(3):
            send[10 + k, :, cut(c)] = sums[k]


def start_rows(tiles, halves, chain, pop, phase, row, send, beside, ready=None):
    up = upper(chain)
    x, inwards = jnp.where(up, SUBS - 1, 0), jnp.where(up, SUBS - 2, 1)
    for c in range(tiles):
        if ready is not None:
            ready(c)
        send[13, :, cut(c)] = start_row(tiles, pop, phase, x, row, c)
        start_row(tiles, pop, phase, inwards, beside, c)

    def side(up):
        look_ahead(
            tiles, halves, up, lambda q, c: row[q, :, cut(c)], lambda q, c: beside[q, :, cut(c)], send
        )

    by_side(chain, side)


def first_kernel(
    tiles, halves, pop_h, phase_h, conc_h, napl_h, poro_h, flags_h,
    pop, phase, conc, napl, poro, flags, row, send, beside, sems,
):
    small = [
        pltpu.make_async_copy(a, b, sems.at[tiles + i])
        for i, (a, b) in enumerate(
            ((phase_h, phase), (conc_h, conc), (poro_h, poro), (napl_h, napl), (flags_h, flags))
        )
    ]
    large = [pltpu.make_async_copy(pop_h.at[:, :, c], pop.at[:, :, c], sems.at[c]) for c in range(tiles)]
    small[0].start()
    for copy in large + small[1:]:
        copy.start()
    small[0].wait()
    flat = pop.reshape(pop.shape[0], SUBS * tiles * SUBS, LANES)
    start_rows(tiles, halves, 1, flat, phase, row, send, beside, ready=lambda c: large[c].wait())
    for copy in small[1:]:
        copy.wait()


def second_kernel(tiles, pop, phase, after, row, send):
    x = jnp.where(upper(0), SUBS - 1, 0)
    for c in range(tiles):
        start_row(tiles, pop, phase, x, row, c)

    def side(up):
        for i, q in enumerate(UP if up else DOWN):
            send[i] = row[q]

    by_side(0, side)


def merge_rows(out, row0, row1, count):
    rows = out.shape[1]

    def side(up):
        for k in range(count):
            out[k, 0] = (row0 if up else row1)[k]
            out[k, rows - 1] = (row1 if up else row0)[k]

    by_side(1, side)


def first_inner_kernel(
    tiles, halves, pop, phase, conc, napl, poro, flags, row0, row1, g, fac, start, slabs, open_ends
):
    rows = g.shape[1]
    length = tiles * LANES
    _, sub = iotas()

    def to_slabs(read, write):
        for c in range(tiles):
            v = [read(pl.ds((i * tiles + c) * SUBS, SUBS)) for i in range(SUBS)]
            for x, t in enumerate(swap_tile(v, sub)):
                write(x, cut(c), t)

    def store(ref, k):
        def write(x, at, t):
            ref[k, x, :, at] = t

        return write

    def store_fac(x, at, t):
        fac[x, :, at] = t

    to_slabs(lambda at: drag(phase[at, :]), store_fac)

    def direction(q, _):
        to_slabs(lambda at: pop[q, at, :], store(start, q))
        return 0

    lax.fori_loop(0, 19, direction, 0)

    def row(x, _):
        for c in range(tiles):
            post = collide([start[q, x, :, cut(c)] for q in range(19)], fac[x, :, cut(c)])
            for q in range(19):
                g[q, x, :, cut(c)] = post[q]
        return 0

    lax.fori_loop(1, rows - 1, row, 0)
    merge_rows(g, row0, row1, 19)
    for k, ref in enumerate((conc, napl, poro)):
        to_slabs(lambda at, ref=ref: ref[at, :], store(slabs, k))
    for k in range(2):
        for z in range(SUBS // halves):
            for h in range(halves):
                line = flags[k, z : z + 1, h * length : (h + 1) * length]
                open_ends[k, z * halves + h : z * halves + h + 1, :] = line.astype(F32)


def inner_kernel(tiles, halves, g, fac, after, out):
    rows = g.shape[1]
    lane, sub = iotas()

    def row(x, _):
        for c in range(tiles):
            f = stream(g, None, None, x, c, tiles, halves, lane, sub, "mid")
            post = collide(f, fac[x, :, cut(c)])
            for q in range(19):
                out[q, x, :, cut(c)] = post[q]
        return 0

    lax.fori_loop(1, rows - 1, row, 0)


def put_kernel(chain, inner, row, out):
    rows = out.shape[1]

    def side(up):
        for q in range(19):
            out[q, rows - 1 if up else 0] = row[q]

    by_side(chain, side)


def edge_kernel(tiles, halves, chain, g, fac, halo, slabs, after, row, send):
    rows = g.shape[1]
    lane, sub = iotas()

    def side(up):
        x = rows - 1 if up else 0
        lo, hi, place = (None, halo, "last") if up else (halo, None, "first")
        for c in range(tiles):
            post = collide(stream(g, lo, hi, x, c, tiles, halves, lane, sub, place), fac[x, :, cut(c)])
            for q in range(19):
                row[q, :, cut(c)] = post[q]
            for i, q in enumerate(UP if up else DOWN):
                send[i, :, cut(c)] = post[q]
        send[5] = slabs[0, x]

    by_side(chain, side)


def arrive_kernel(tiles, halves, chain, g, fac, halo, first_halo, other, after, inner, out, ghost):
    rows = g.shape[1]
    lane, sub = iotas()

    def side(up):
        x = rows - 1 if up else 0
        lo, hi, place = (None, halo, "last") if up else (halo, None, "first")
        toward, back = (DOWN, UP) if up else (UP, DOWN)
        for q in range(19):
            out[q, rows - 1 - x] = other[q]
        for c in range(tiles):
            post = collide(stream(g, lo, hi, x, c, tiles, halves, lane, sub, place), fac[x, :, cut(c)])
            for q in range(19):
                out[q, x, :, cut(c)] = post[q]
            near = [halo[5 + i, :, cut(c)] for i in range(5)]
            sums = [halo[10, :, cut(c)], None, halo[11, :, cut(c)], halo[12, :, cut(c)]]
            known = list(zip(toward, near))
            for i, q in enumerate(back):
                f = pull(lambda q, cc: g[q, x, :, cut(cc)], q, c, tiles, halves, lane, sub)
                known.append((q, jnp.where(f != f, halo[i, :, cut(c)], f)))
            for q, f in known:
                for k, e in enumerate((1, *DIRS[q])):
                    if e:
                        t = f if e > 0 else -f
                        sums[k] = t if sums[k] is None else sums[k] + t
            rho = sums[0]
            inv = first_halo[13, :, cut(c)] / rho
            v = [j * inv for j in sums[1:]]
            base = np.float32(1.0) - (v[0] * v[0] + v[1] * v[1] + v[2] * v[2]) * np.float32(1.0 / 6)
            for i, q in enumerate(toward):
                along = None
                for e, t in zip(DIRS[q], v):
                    if e:
                        t = t if e > 0 else -t
                        along = t if along is None else along + t
                weight = np.float32(1.25 / 18 if sum(map(abs, DIRS[q])) == 1 else 1.25 / 36)
                feq = (rho * weight) * (base + along * (along * np.float32(0.5) + np.float32(1.0)))
                ghost[i, :, cut(c)] = feq - near[i] * np.float32(0.25)

    by_side(chain, side)


def far_kernel(tiles, halves, chain, g, fac, halo, slabs, after, row, send, beside):
    rows = g.shape[1]
    lane, sub = iotas()

    def side(up):
        x, inwards = (rows - 1, rows - 2) if up else (0, 1)
        lo, hi, place = (None, halo, "last") if up else (halo, None, "first")
        for c in range(tiles):
            for at, ref, where in ((x, row, place), (inwards, beside, "mid")):
                f = stream(g, lo, hi, at, c, tiles, halves, lane, sub, where)
                post = collide(f, fac[at, :, cut(c)])
                for q in range(19):
                    ref[q, :, cut(c)] = post[q]
        look_ahead(
            tiles, halves, up, lambda q, c: row[q, :, cut(c)], lambda q, c: beside[q, :, cut(c)], send
        )
        send[13] = slabs[0, x] if chain else fac[x]

    by_side(chain, side)


def speed(f, fc):
    s = [f[2 * p + 1] + f[2 * p + 2] for p in range(9)]
    d = [f[2 * p + 1] - f[2 * p + 2] for p in range(9)]
    rho = f[0] + (((s[0] + s[1]) + (s[2] + s[3])) + ((s[4] + s[5]) + (s[6] + s[7])) + s[8])
    jx = d[0] + ((d[3] + d[4]) + (d[5] + d[6]))
    jy = d[1] + ((d[3] - d[4]) + (d[7] + d[8]))
    jz = d[2] + ((d[5] - d[6]) + (d[7] - d[8]))
    inv = np.float32(1.0) / rho
    return [jnp.where(fc != fc, np.float32(0.0), j * inv) for j in (jz, jx, jy)]


def inner_speed_kernel(tiles, halves, g, fac, after, u):
    rows = g.shape[1]
    lane, sub = iotas()

    def row(x, _):
        for c in range(tiles):
            f = stream(g, None, None, x, c, tiles, halves, lane, sub, "mid")
            for i, v in enumerate(speed(f, fac[x, :, cut(c)])):
                u[i, x - 2, :, cut(c)] = v
        return 0

    lax.fori_loop(2, rows - 2, row, 0)


def final_kernel(tiles, halves, g, fac, halo0, halo1, start, after, out, token, buf, sems):
    rows = g.shape[1]
    lane, sub = iotas()
    odd = upper(1)
    token[...] = jnp.zeros(token.shape, F32)

    def row_of(q, x):
        at = x - DIRS[q][0]
        if at < 0:
            return lambda qq, cc: jnp.where(
                odd, halo0[UP.index(qq), :, cut(cc)], halo1[UP.index(qq), :, cut(cc)]
            )
        if at >= rows:
            return lambda qq, cc: jnp.where(
                odd, halo1[DOWN.index(qq), :, cut(cc)], halo0[DOWN.index(qq), :, cut(cc)]
            )
        return lambda qq, cc: g[qq, at, :, cut(cc)]

    copies = []
    for q in range(19):
        for c in range(tiles):
            new = []
            for x in range(rows):
                fc = fac[x, :, cut(c)]
                if q == 0:
                    v = g[0, x, :, cut(c)]
                else:
                    v = pull(row_of(q, x), q, c, tiles, halves, lane, sub)
                    v = jnp.where(v != v, g[OPP[q], x, :, cut(c)], v)
                new.append(jnp.where(fc != fc, start[q, x, :, cut(c)], v))
            for i, t in enumerate(swap_tile(new, sub)):
                first = (i * tiles + c) * SUBS
                buf[q, first : first + SUBS, :] = t
        copy = pltpu.make_async_copy(buf.at[q], out.at[q], sems.at[q])
        copy.start()
        copies.append(copy)
    for copy in copies:
        copy.wait()


def slope(p, q):
    return np.float32(0.5) * (
        jnp.maximum(jnp.minimum(p, q), np.float32(0.0)) + jnp.minimum(jnp.maximum(p, q), np.float32(0.0))
    )


def loss(s, c):
    return [np.float32(TRANSFER) * a * (np.float32(1.0) - b) for a, b in zip(s, c)]


def ends_of(parts, strips):
    place = lax.axis_index("wide") * parts + lax.axis_index("narrow")
    return place == 0, place == strips - 1


ZERO = np.float32(0.0)


def each(f, *lists):
    return [f(*t) for t in zip(*lists)]


def less(a, b):
    return each(lambda x, y: x - y, a, b)


def times(a, b):
    return each(lambda x, y: x * y, a, b)


def face(w, va, vb, c, cn, sl, sn, dn):
    a = each(lambda w, x, y: w * np.float32(0.5) * (x + y), w, va, vb)
    return each(
        lambda a, w, c, cn, sl, sn, dn: a * jnp.where(a > 0, c + sl, cn - sn) - np.float32(DIFFUSION) * w * dn,
        a, w, c, cn, sl, sn, dn,
    )


def floored(p):
    return [jnp.maximum(t, np.float32(FLOOR)) for t in p]


class Step:
    def __init__(self, tiles, halves, conc, poro, flow, cross, napl):
        self.tiles, self.halves = tiles, halves
        self.lane, self.sub = iotas()
        self.conc, self.poro, self.flow = (self.keep(f) for f in (conc, poro, flow))
        self.cross, self.napl = cross, napl
        self.gap = self.keep(lambda r: less(self.conc(r + 1), self.conc(r)))
        self.lean = self.keep(lambda r: each(slope, self.gap(r - 1), self.gap(r)))

    @staticmethod
    def keep(f):
        seen = {}

        def get(r):
            if r not in seen:
                seen[r] = f(r)
            return seen[r]

        return get

    def after(self, v):
        out = []
        for c in range(self.tiles):
            if c < self.tiles - 1:
                side = v[c + 1]
            else:
                edge = self.sub % self.halves == self.halves - 1
                side = jnp.where(edge, ZERO, pltpu.roll(v[0], SUBS - 1, 0))
            out.append(pltpu.roll(jnp.where(self.lane == 0, side, v[c]), LANES - 1, 1))
        return out

    def before(self, v):
        out = []
        for c in range(self.tiles):
            if c > 0:
                side = v[c - 1]
            else:
                edge = self.sub % self.halves == 0
                side = jnp.where(edge, ZERO, pltpu.roll(v[self.tiles - 1], 1, 0))
            out.append(pltpu.roll(jnp.where(self.lane == LANES - 1, side, v[c]), 1, 1))
        return out

    def above(self, v):
        return [pltpu.roll(t, SUBS - self.halves, 0) for t in v]

    def below(self, v):
        return [pltpu.roll(t, self.halves, 0) for t in v]

    def flow_face(self, r):
        return face(
            times(self.poro(r), self.poro(r + 1)), self.flow(r), self.flow(r + 1), self.conc(r), self.conc(r + 1),
            self.lean(r), self.lean(r + 1), self.gap(r),
        )

    def run(self, r, low=True, high=True):
        c, p, s = self.conc(r), self.poro(r), self.napl(r)
        change = None
        if low:
            change = self.flow_face(r - 1)
        if high:
            out = self.flow_face(r)
            change = [-t for t in out] if change is None else less(change, out)
        vel = self.cross(r)
        for after, before, v, open_ends in (
            (self.after, self.before, vel[0], True), (self.above, self.below, vel[1], False),
        ):
            cn = after(c)
            dn = less(cn, c)
            dm = less(c, before(c)) if open_ends else before(dn)
            s0 = each(slope, dm, dn)
            flux = face(times(p, after(p)), v, after(v), c, cn, s0, after(s0), dn)
            change = each(lambda t, a, b: t + (a - b), change, before(flux), flux)
        rate = loss(s, c)
        cnew = each(lambda c, t, k, p: c + (t + k) / p, c, change, rate, floored(p))
        return cnew, each(lambda s, k: s - np.float32(DEPLETION) * k, s, rate)


def read(slab):
    return [slab[:, cut(c)] for c in range(slab.shape[1] // LANES)]


def write(slab, tiles):
    for c, t in enumerate(tiles):
        slab[:, cut(c)] = t


def early_kernel(tiles, halves, slabs, u, ue0, ue1, cs):
    rows = slabs.shape[1]
    odd = upper(1)

    def flow(r):
        if r == 1:
            return pick(odd, read(ue0.at[1, 1]), read(ue1.at[1, 1]))
        if r == rows - 2:
            return pick(odd, read(ue1.at[1, 1]), read(ue0.at[1, 1]))
        return read(u.at[1, r - 2])

    step = Step(
        tiles, halves, lambda r: read(slabs.at[0, r]), lambda r: read(slabs.at[2, r]), flow,
        lambda r: (read(u.at[2, r - 2]), read(u.at[0, r - 2])), lambda r: read(slabs.at[1, r]),
    )
    for r in range(2, rows - 2):
        for k, v in enumerate(step.run(r)):
            write(cs.at[k, r - 2], v)


def static_readers(ends, up, slabs, halo, k, there, flags):
    rows = slabs.shape[1]
    first, last = ends_of(*ends)

    def conc(r):
        if 0 <= r < rows:
            return read(slabs.at[0, r])
        beyond = read(halo.at[k] if r in (-1, rows) else there.at[3])
        return pick(last, read(slabs.at[0, rows - 1]), beyond) if up else [jnp.where(first, ZERO, t) for t in beyond]

    def poro(r):
        if 0 <= r < rows:
            return read(slabs.at[2, r])
        return pick(last if up else first, read(flags.at[1 if up else 0]), read(there.at[4]))

    return conc, poro


def rim_kernel(tiles, halves, ends, chain, g, fac, ghost, u, slabs, halo, after, ue, cs, send):
    rows = g.shape[1]
    lane, sub = iotas()

    def side(up):
        x, beside = (rows - 1, rows - 2) if up else (0, 1)
        lo, hi, place = (None, ghost, "last") if up else (ghost, None, "first")
        for n, (at, where) in enumerate(((x, place), (beside, "mid"))):
            for c in range(tiles):
                f = stream(g, lo, hi, at, c, tiles, halves, lane, sub, where)
                for i, v in enumerate(speed(f, fac[at, :, cut(c)])):
                    ue[n, i, :, cut(c)] = v
        conc, poro = static_readers(ends, up, slabs, halo, 13 if chain else 5, None, None)

        def vel(k, r):
            return read(ue.at[0 if r == x else 1, k] if r in (x, beside) else u.at[k, r - 2])

        step = Step(
            tiles, halves, conc, poro, lambda r: vel(1, r), lambda r: (vel(2, r), vel(0, r)),
            lambda r: read(slabs.at[1, r]),
        )
        edge = step.run(x, low=up, high=not up)
        inward = step.run(beside)
        for i, new in enumerate((edge, inward)):
            for k in range(2):
                write(cs.at[i, k], new[k])
            write(send.at[1 + i], new[0])
        send[0] = ue[0, 1]
        send[3] = slabs[0, beside]
        send[4] = slabs[2, x]

    by_side(chain, side)


def state_reader(rows, edge, inner, rims):
    def state(k, r):
        if r in (0, rows - 1):
            return edge(k, r)
        if r in (1, rows - 2):
            return rims(k, r)
        return read(inner.at[k, r - 2])

    return state


def middle_kernel(tiles, halves, slabs, u, inner, rim0, rim1, out):
    rows = slabs.shape[1]
    odd = upper(1)

    def rims(k, r):
        a, b = (rim0, rim1) if r == 1 else (rim1, rim0)
        return pick(odd, read(a.at[1, k]), read(b.at[1, k]))

    state = state_reader(rows, None, inner, rims)
    step = Step(
        tiles, halves, lambda r: state(0, r), lambda r: read(slabs.at[2, r]), lambda r: read(u.at[1, r - 2]),
        lambda r: (read(u.at[2, r - 2]), read(u.at[0, r - 2])), lambda r: state(1, r),
    )
    for r in range(3, rows - 3):
        write(out.at[r - 3], step.run(r)[0])


def late_kernel(
    tiles, halves, ends, chain, slabs, u, ue, inner, rim, halo, flags, there, after, out
):
    rows = slabs.shape[1]
    first, last = ends_of(*ends)

    def side(up):
        x = rows - 1 if up else 0
        beyond = rows if up else -1
        ghost = last if up else first
        conc, poro = static_readers(ends, up, slabs, halo, 13 if chain else 5, there, flags)

        def vel(k, r):
            if r == beyond:
                return pick(ghost, read(ue.at[0, 1]), read(there.at[0]))
            if r in (x, x - 1 if up else x + 1):
                return read(ue.at[0 if r == x else 1, k])
            return read(u.at[k, r - 2])

        def cross(r):
            return vel(2, r), vel(0, r)

        one = Step(tiles, halves, conc, poro, lambda r: vel(1, r), cross, None)
        flux = one.flow_face(x if up else -1)
        sign = np.float32(-1.0 if up else 1.0)
        edge = each(lambda c, f, p: c + sign * f / p, read(rim.at[0, 0]), flux, floored(poro(x)))
        outer = each(lambda c, f, p: c - sign * f / p, read(there.at[1]), flux, floored(poro(beyond)))
        second = read(there.at[2])
        if up:
            outer, second = pick(ghost, edge, outer), pick(ghost, edge, second)
        else:
            outer, second = ([jnp.where(ghost, ZERO, t) for t in v] for v in (outer, second))
        state = state_reader(
            rows, lambda k, r: read(rim.at[0, k]) if k else edge, inner, lambda k, r: read(rim.at[1, k])
        )

        def after_one(r):
            if r < 0 or r >= rows:
                return outer if r == beyond else second
            return state(0, r)

        two = Step(tiles, halves, after_one, poro, lambda r: vel(1, r), cross, lambda r: state(1, r))
        for i in range(3):
            new = two.run(rows - 1 - i if up else i)
            write(out.at[i], new[0])
            if i == 0:
                write(out.at[3], new[1])

    by_side(chain, side)


def deal_kernel(tiles, halves, parts, inner, rim0, rim1, late0, late1, mid, *refs):
    *blocks, whole = refs
    rows = inner.shape[1] + 4
    odd = upper(1)
    _, sub = iotas()
    for c in range(tiles):

        def ends_pick(a, b):
            return jnp.where(odd, a, b)

        lo = [ends_pick(late0[i, :, cut(c)], late1[i, :, cut(c)]) for i in range(4)]
        hi = [ends_pick(late1[i, :, cut(c)], late0[i, :, cut(c)]) for i in range(4)]
        conc = lo[:3] + [mid[r, :, cut(c)] for r in range(rows - 6)] + hi[2::-1]
        left = [lo[3]]
        for r in range(1, rows - 1):
            if r in (1, rows - 2):
                a, b = (rim0, rim1) if r == 1 else (rim1, rim0)
                cc, ss = (ends_pick(a[1, k, :, cut(c)], b[1, k, :, cut(c)]) for k in range(2))
            else:
                cc, ss = (inner[k, r - 2, :, cut(c)] for k in range(2))
            left.append(ss - np.float32(DEPLETION) * loss([ss], [cc])[0])
        left.append(hi[3])
        run = whole.shape[3]
        for k, tile in enumerate((conc, left)):
            for i, t in enumerate(swap_tile(tile, sub)):
                column = (i % halves * tiles + c) * SUBS
                at = column % run
                whole[column // run, k, i // halves, at : at + SUBS, :] = t
    for k in range(parts):
        blocks[k][...] = whole[lax.axis_index("narrow") ^ k]


def gather_kernel(parts, order, *refs):
    blocks = refs[:parts]
    *outs, sems = refs[parts:]
    copies = []
    for k, block in zip(order, blocks):
        origin = lax.axis_index("narrow") ^ k
        for i, out in enumerate(outs):
            copies.append(pltpu.make_async_copy(block.at[i], out.at[:, origin], sems.at[i, k]))
            copies[-1].start()
    for copy in copies:
        copy.wait()


def call(kernel, out_shape, args, scratch=(), hbm=(), free=(), hbm_out=(), name=None, aliases=None):
    def spec(i, hbm, free=()):
        return pl.BlockSpec(memory_space=pltpu.HBM if i in hbm else pl.ANY if i in free else pltpu.VMEM)

    single = not isinstance(out_shape, tuple)
    shapes = (out_shape,) if single else out_shape
    out = pl.pallas_call(
        kernel,
        out_shape=shapes,
        in_specs=[spec(i, hbm, free) for i in range(len(args))],
        out_specs=tuple(spec(i, hbm_out) for i in range(len(shapes))),
        scratch_shapes=list(scratch),
        name=name,
        input_output_aliases=aliases or {},
        compiler_params=pltpu.CompilerParams(vmem_limit_bytes=VMEM_LIMIT),
        cost_estimate=pl.CostEstimate(flops=1024, bytes_accessed=1024, transcendentals=0),
    )(*args)
    return out[0] if single else out


def local(populations, phase, porosity, napl, concentration, flags):
    layers, rows, width = phase.shape
    halves = SUBS // layers
    length = width // halves
    tiles = length // LANES
    parts = lax.axis_size("narrow")
    strips = lax.axis_size("wide") * parts
    both = ("wide", "narrow")
    pairs = (
        [(i, i ^ 1) for i in range(strips)],
        [(i, (i + 1 if i % 2 else i - 1) % strips) for i in range(strips)],
    )
    slab = (SUBS, length)
    ends = (parts, strips)
    run = width // LANES * SUBS // parts

    def hold(*shape, dtype=F32):
        return pltpu.VMEM(shape, dtype)

    def swap(chain, array):
        return lax.ppermute(array, both, pairs[chain])

    pop = to_view(populations)
    views = [to_view(a) for a in (phase, concentration, napl, porosity)]
    flat = views[0].shape
    chunks = pop.reshape(19, SUBS, tiles, SUBS, LANES)
    given = [pltpu.with_memory_space_constraint(a, pltpu.HBM) for a in (chunks, *views, flags)]
    popv, phv, cov, nav, pov, flv, row1, send = call(
        functools.partial(first_kernel, tiles, halves),
        (
            hold(*chunks.shape), hold(*flat, dtype=jnp.int32), hold(*flat), hold(*flat), hold(*flat),
            hold(*flags.shape, dtype=jnp.int32), hold(19, *slab), hold(14, *slab),
        ),
        given, scratch=(pltpu.VMEM((19, *slab), F32), pltpu.SemaphoreType.DMA((tiles + 5,))),
        hbm=range(6), name="first",
    )
    popv = popv.reshape(pop.shape)
    halo1 = head1 = swap(1, send)
    row0, send = call(
        functools.partial(second_kernel, tiles), (hold(19, *slab), hold(5, *slab)), (popv, phv, send),
        free=(2,), name="second",
    )
    halo0 = swap(0, send)
    g, fac, start, slabs, open_ends = call(
        functools.partial(first_inner_kernel, tiles, halves),
        (
            hold(19, rows, *slab), hold(rows, *slab), hold(19, rows, *slab), hold(3, rows, *slab),
            hold(2, *slab),
        ),
        (popv, phv, cov, nav, pov, flv, row0, row1), name="first_inner",
    )

    def inner_rows(g, after):
        return call(
            functools.partial(inner_kernel, tiles, halves), hold(19, rows, *slab), (g, fac, after), free=(2,),
            name="inner",
        )

    def arrive(chain, g, halo, head, other, after, new):
        return call(
            functools.partial(arrive_kernel, tiles, halves, chain), (hold(19, rows, *slab), hold(5, *slab)),
            (g, fac, halo, head, other, after, new), free=(5, 6), name=f"arrive{chain}", aliases={6: 0},
        )

    def far(chain, g, ghost, after):
        return call(
            functools.partial(far_kernel, tiles, halves, chain), (hold(19, *slab), hold(14, *slab)),
            (g, fac, ghost, slabs, after), scratch=(pltpu.VMEM((19, *slab), F32),), free=(4,), name=f"far{chain}",
        )

    def rim(chain, g, ghost, halo, after):
        return call(
            functools.partial(rim_kernel, tiles, halves, ends, chain),
            (hold(2, 3, *slab), hold(2, 2, *slab), hold(5, *slab)),
            (g, fac, ghost, u, slabs, halo, after), free=(6,), name=f"rim{chain}",
        )

    new = inner_rows(g, slabs)
    row0, send0 = far(0, g, halo0, new)
    halo0 = swap(0, send0)
    g, ghost1 = arrive(1, g, halo1, head1, row0, send0, new)
    row1, send1 = far(1, g, ghost1, ghost1)
    halo1 = swap(1, send1)
    new = inner_rows(g, send1)
    g, ghost0 = arrive(0, g, halo0, halo0, row1, row1, new)
    row0, send0 = call(
        functools.partial(edge_kernel, tiles, halves, 0), (hold(19, *slab), hold(6, *slab)),
        (g, fac, ghost0, slabs, ghost0), free=(4,), name="edge0",
    )
    halo0 = swap(0, send0)
    new = inner_rows(g, send0)
    u = call(
        functools.partial(inner_speed_kernel, tiles, halves), hold(3, rows - 4, *slab), (new, fac, new),
        free=(2,), name="inner_speed",
    )
    part = call(
        functools.partial(put_kernel, 0), hold(19, rows, *slab), (new, row0), name="put", aliases={0: 0}, free=(0,)
    )
    ue0, rim0, send0 = rim(0, part, halo0, halo0, u)
    there0 = swap(0, send0)
    g, ghost1 = arrive(1, g, halo1, head1, row0, send0, part)
    ue1, rim1, send1 = rim(1, g, ghost1, halo1, ghost1)
    there1 = swap(1, send1)
    inner = call(
        functools.partial(early_kernel, tiles, halves), hold(2, rows - 4, *slab), (slabs, u, ue0, ue1),
        name="early",
    )
    mid = call(
        functools.partial(middle_kernel, tiles, halves), hold(rows - 6, *slab), (slabs, u, inner, rim0, rim1),
        name="middle",
    )
    late0 = call(
        functools.partial(late_kernel, tiles, halves, ends, 0), hold(4, *slab),
        (slabs, u, ue0, inner, rim0, halo0, open_ends, there0, mid), free=(8,), name="late0",
    )
    out, token = call(
        functools.partial(final_kernel, tiles, halves),
        (jax.ShapeDtypeStruct((19, *flat), F32), hold(SUBS, LANES)),
        (g, fac, halo0, ghost1, start, late0),
        scratch=(pltpu.VMEM((19, *flat), F32), pltpu.SemaphoreType.DMA((19,))),
        free=(5,), hbm_out=(0,), name="final",
    )
    late1 = call(
        functools.partial(late_kernel, tiles, halves, ends, 1), hold(4, *slab),
        (slabs, u, ue1, inner, rim1, halo1, open_ends, there1, token), free=(8,), name="late1",
    )
    block = (2, layers, run, LANES)
    blocks = call(
        functools.partial(deal_kernel, tiles, halves, parts), tuple(hold(*block) for _ in range(parts)),
        (inner, rim0, rim1, late0, late1, mid),
        scratch=(pltpu.VMEM((parts, *block), F32),), name="deal",
    )
    order = [0, *range(2, parts), 1]
    came = [blocks[0]]
    for k in order[1:]:
        came.append(lax.ppermute(blocks[k], "narrow", [(i, i ^ k) for i in range(parts)]))
    tile = (layers, parts, run, LANES)
    conc_out, napl_out = call(
        functools.partial(gather_kernel, parts, order),
        (jax.ShapeDtypeStruct(tile, F32), jax.ShapeDtypeStruct(tile, F32)),
        came, scratch=(pltpu.SemaphoreType.DMA((2, parts)),), hbm_out=(0, 1), name="gather",
    )
    shape = (layers, rows * parts, width // parts)

    def tile_of(a):
        return from_view(a.reshape(layers * parts * run, LANES), shape)

    return from_view(out, populations.shape), tile_of(conc_out), tile_of(napl_out)


def solution(mesh):
    strip = P(None, ("wide", "narrow"), None)
    in_specs = (P(None, None, ("wide", "narrow"), None), strip, strip, strip, strip, P())
    tile = P(None, "wide", "narrow")
    out_specs = (P(None, None, ("wide", "narrow"), None), tile, tile)
    return jax.shard_map(local, mesh=mesh, in_specs=in_specs, out_specs=out_specs, check_vma=False)
```

```python
import functools

import jax
import jax.numpy as jnp
import numpy as np
from jax import lax
from jax.experimental import pallas as pl
from jax.experimental.pallas import tpu as pltpu
from jax.sharding import PartitionSpec as P

LBM_STEPS = 4
F32 = jnp.float32

DIRS = [
    (0, 0, 0), (1, 0, 0), (-1, 0, 0), (0, 1, 0), (0, -1, 0), (0, 0, 1), (0, 0, -1),
    (1, 1, 0), (-1, -1, 0), (1, -1, 0), (-1, 1, 0), (1, 0, 1), (-1, 0, -1), (1, 0, -1),
    (-1, 0, 1), (0, 1, 1), (0, -1, -1), (0, 1, -1), (0, -1, 1),
]
OPP = [0, 2, 1, 4, 3, 6, 5, 8, 7, 10, 9, 12, 11, 14, 13, 16, 15, 18, 17]
UP = [1, 7, 9, 11, 13]
DOWN = [2, 8, 10, 12, 14]
DIFFUSION = 0.15
TRANSFER = 0.3
DEPLETION = 0.5
FLOOR = 0.3
SUBS = 8
LANES = 128
VMEM_LIMIT = 16 * 1024 * 1024


def to_view(array):
    *lead, rows, width = array.shape
    n = len(lead)
    t = array.reshape(*lead, rows // SUBS, SUBS, width // LANES, LANES)
    t = t.transpose(*range(n), n, n + 2, n + 1, n + 3)
    return t.reshape(*lead[:-1], lead[-1] * rows * width // LANES, LANES)


def from_view(view, shape):
    *lead, rows, width = shape
    n = len(lead)
    t = view.reshape(*lead, rows // SUBS, width // LANES, SUBS, LANES)
    t = t.transpose(*range(n), n, n + 2, n + 1, n + 3)
    return t.reshape(shape)


def iotas():
    lane = lax.broadcasted_iota(jnp.int32, (SUBS, LANES), 1)
    sub = lax.broadcasted_iota(jnp.int32, (SUBS, LANES), 0)
    return lane, sub


def cut(c):
    return slice(c * LANES, (c + 1) * LANES)


def strided(tiles, c, x):
    return pl.ds(c * SUBS + x, SUBS, stride=tiles * SUBS)


def collide(f, fac):
    s = [f[2 * p + 1] + f[2 * p + 2] for p in range(9)]
    d = [f[2 * p + 1] - f[2 * p + 2] for p in range(9)]
    rho = f[0] + (((s[0] + s[1]) + (s[2] + s[3])) + ((s[4] + s[5]) + (s[6] + s[7])) + s[8])
    jx = d[0] + ((d[3] + d[4]) + (d[5] + d[6]))
    jy = d[1] + ((d[3] - d[4]) + (d[7] + d[8]))
    jz = d[2] + ((d[5] - d[6]) + (d[7] - d[8]))
    inv = fac / rho
    vx, vy, vz = jx * inv, jy * inv, jz * inv
    w1 = rho * np.float32(1.25 / 18)
    w2 = rho * np.float32(1.25 / 36)
    w4 = rho * np.float32(1.25 / 72)
    a1 = w1 - w1 * ((vx * vx + vy * vy + vz * vz) * np.float32(1.0 / 6))
    a2 = a1 * np.float32(0.5)
    post = [a1 * np.float32(6.0) - f[0] * np.float32(0.25)]
    axes = [vx, vy, vz, vx + vy, vx - vy, vx + vz, vx - vz, vy + vz, vy - vz]
    for p, v in enumerate(axes):
        wa, wh, base = (w1, w2, a1) if p < 3 else (w2, w4, a2)
        even = (base + (wh * v) * v) - s[p] * np.float32(0.125)
        odd = wa * v - d[p] * np.float32(0.125)
        post += [even + odd, even - odd]
    return post


def pull(load, q, c, tiles, halves, lane, sub):
    _, cross, layer = DIRS[q]
    v = load(q, c)
    if cross == 1:
        if c > 0:
            side = load(q, c - 1)
        else:
            side = jnp.where(sub % halves == 0, jnp.nan, pltpu.roll(load(q, tiles - 1), 1, 0))
        v = pltpu.roll(jnp.where(lane == LANES - 1, side, v), 1, 1)
    elif cross == -1:
        if c < tiles - 1:
            side = load(q, c + 1)
        else:
            side = jnp.where(sub % halves == halves - 1, jnp.nan, pltpu.roll(load(q, 0), SUBS - 1, 0))
        v = pltpu.roll(jnp.where(lane == 0, side, v), LANES - 1, 1)
    if layer:
        v = pltpu.roll(v, (layer * halves) % SUBS, 0)
    return v


def stream(g, lo, hi, x, c, tiles, halves, lane, sub, place):
    def load(q, cc):
        flow = DIRS[q][0]
        if flow == 1 and place == "first":
            return lo[UP.index(q), :, cut(cc)]
        if flow == -1 and place == "last":
            return hi[DOWN.index(q), :, cut(cc)]
        return g[q, x - flow, :, cut(cc)]

    f = [g[0, x, :, cut(c)]]
    for q in range(1, 19):
        v = pull(load, q, c, tiles, halves, lane, sub)
        f.append(jnp.where(v != v, g[OPP[q], x, :, cut(c)], v))
    return f


def drag(ph):
    return jnp.where(ph == 2, jnp.nan, jnp.where(ph == 1, np.float32(1.5), np.float32(3.0)))


def swap_tile(v, sub):
    v = list(v)
    for k in (4, 2, 1):
        low = sub & k == 0
        for i in range(SUBS):
            if not i & k:
                a, b = v[i], v[i + k]
                v[i] = jnp.where(low, a, pltpu.roll(b, k, 0))
                v[i + k] = jnp.where(low, pltpu.roll(a, SUBS - k, 0), b)
    return v


def upper(chain):
    odd = lax.rem(lax.axis_index("narrow"), 2) == 1
    return odd if chain else jnp.logical_not(odd)


def by_side(chain, side):
    pl.when(upper(chain))(lambda: side(True))
    pl.when(jnp.logical_not(upper(chain)))(lambda: side(False))


def pick(flag, a, b):
    return [jnp.where(flag, x, y) for x, y in zip(a, b)]


def start_row(tiles, pop, phase, x, row, c):
    at = strided(tiles, c, x)
    fc = drag(phase[at, :])
    post = collide([pop[q, at, :] for q in range(19)], fc)
    for q in range(19):
        row[q, :, cut(c)] = post[q]
    return fc


def look_ahead(tiles, halves, up, edge, beside, send):
    lane, sub = iotas()
    toward, back = (UP, DOWN) if up else (DOWN, UP)
    for c in range(tiles):
        sums = [None] * 3
        for q in range(19):
            if q in back:
                continue
            if q == 0:
                f = edge(0, c)
            else:
                f = pull(beside if q in toward else edge, q, c, tiles, halves, lane, sub)
                f = jnp.where(f != f, edge(OPP[q], c), f)
            if q in toward:
                i = toward.index(q)
                send[i, :, cut(c)] = edge(q, c)
                send[5 + i, :, cut(c)] = f
            else:
                for k, e in enumerate((1, *DIRS[q][1:])):
                    if e:
                        t = f if e > 0 else -f
                        sums[k] = t if sums[k] is None else sums[k] + t
        for k in range(3):
            send[10 + k, :, cut(c)] = sums[k]


def start_rows(tiles, halves, chain, pop, phase, row, send, beside, ready=None):
    def tile(c, up):
        x, inwards = (SUBS - 1, SUBS - 2) if up else (0, 1)
        send[13, :, cut(c)] = start_row(tiles, pop, phase, x, row, c)
        start_row(tiles, pop, phase, inwards, beside, c)

    for c in range(tiles):
        if ready is not None:
            ready(c)
        by_side(chain, functools.partial(tile, c))

    def side(up):
        look_ahead(
            tiles, halves, up, lambda q, c: row[q, :, cut(c)], lambda q, c: beside[q, :, cut(c)], send
        )

    by_side(chain, side)


def first_kernel(
    tiles, halves, pop_h, phase_h, conc_h, napl_h, poro_h, flags_h,
    pop, phase, conc, napl, poro, flags, row, send, beside, sems,
):
    small = [
        pltpu.make_async_copy(a, b, sems.at[tiles + i])
        for i, (a, b) in enumerate(
            ((phase_h, phase), (conc_h, conc), (poro_h, poro), (napl_h, napl), (flags_h, flags))
        )
    ]
    large = [pltpu.make_async_copy(pop_h.at[:, :, c], pop.at[:, :, c], sems.at[c]) for c in range(tiles)]
    small[0].start()
    for copy in large + small[1:]:
        copy.start()
    small[0].wait()
    flat = pop.reshape(pop.shape[0], SUBS * tiles * SUBS, LANES)
    start_rows(tiles, halves, 1, flat, phase, row, send, beside, ready=lambda c: large[c].wait())
    for copy in small[1:]:
        copy.wait()


def second_kernel(tiles, halves, pop, phase, after, row, send, beside):
    start_rows(tiles, halves, 0, pop, phase, row, send, beside)


def merge_rows(out, row0, row1, count):
    rows = out.shape[1]

    def side(up):
        for k in range(count):
            out[k, 0] = (row0 if up else row1)[k]
            out[k, rows - 1] = (row1 if up else row0)[k]

    by_side(1, side)


def first_inner_kernel(
    tiles, halves, pop, phase, conc, napl, poro, flags, row0, row1, g, fac, start, slabs, open_ends
):
    rows = g.shape[1]
    length = tiles * LANES
    _, sub = iotas()

    def to_slabs(read, write):
        for c in range(tiles):
            v = [read(pl.ds((i * tiles + c) * SUBS, SUBS)) for i in range(SUBS)]
            for x, t in enumerate(swap_tile(v, sub)):
                write(x, cut(c), t)

    def store(ref, k):
        def write(x, at, t):
            ref[k, x, :, at] = t

        return write

    def store_fac(x, at, t):
        fac[x, :, at] = t

    to_slabs(lambda at: drag(phase[at, :]), store_fac)

    def direction(q, _):
        to_slabs(lambda at: pop[q, at, :], store(start, q))
        return 0

    lax.fori_loop(0, 19, direction, 0)

    def row(x, _):
        for c in range(tiles):
            post = collide([start[q, x, :, cut(c)] for q in range(19)], fac[x, :, cut(c)])
            for q in range(19):
                g[q, x, :, cut(c)] = post[q]
        return 0

    lax.fori_loop(1, rows - 1, row, 0)
    merge_rows(g, row0, row1, 19)
    for k, ref in enumerate((conc, napl, poro)):
        to_slabs(lambda at, ref=ref: ref[at, :], store(slabs, k))
    for k in range(2):
        for z in range(SUBS // halves):
            for h in range(halves):
                line = flags[k, z : z + 1, h * length : (h + 1) * length]
                open_ends[k, z * halves + h : z * halves + h + 1, :] = line.astype(F32)


def inner_kernel(tiles, halves, g, fac, after, out):
    rows = g.shape[1]
    lane, sub = iotas()

    def row(x, _):
        for c in range(tiles):
            f = stream(g, None, None, x, c, tiles, halves, lane, sub, "mid")
            post = collide(f, fac[x, :, cut(c)])
            for q in range(19):
                out[q, x, :, cut(c)] = post[q]
        return 0

    lax.fori_loop(1, rows - 1, row, 0)


def put_kernel(inner, row0, row1, out):
    merge_rows(out, row0, row1, 19)


def arrive_kernel(tiles, halves, chain, g, fac, halo, first_halo, after, inner, out, ghost):
    rows = g.shape[1]
    lane, sub = iotas()

    def side(up):
        x = rows - 1 if up else 0
        lo, hi, place = (None, halo, "last") if up else (halo, None, "first")
        toward, back = (DOWN, UP) if up else (UP, DOWN)
        for c in range(tiles):
            post = collide(stream(g, lo, hi, x, c, tiles, halves, lane, sub, place), fac[x, :, cut(c)])
            for q in range(19):
                out[q, x, :, cut(c)] = post[q]
            near = [halo[5 + i, :, cut(c)] for i in range(5)]
            sums = [halo[10, :, cut(c)], None, halo[11, :, cut(c)], halo[12, :, cut(c)]]
            known = list(zip(toward, near))
            for i, q in enumerate(back):
                f = pull(lambda q, cc: g[q, x, :, cut(cc)], q, c, tiles, halves, lane, sub)
                known.append((q, jnp.where(f != f, halo[i, :, cut(c)], f)))
            for q, f in known:
                for k, e in enumerate((1, *DIRS[q])):
                    if e:
                        t = f if e > 0 else -f
                        sums[k] = t if sums[k] is None else sums[k] + t
            rho = sums[0]
            inv = first_halo[13, :, cut(c)] / rho
            v = [j * inv for j in sums[1:]]
            base = np.float32(1.0) - (v[0] * v[0] + v[1] * v[1] + v[2] * v[2]) * np.float32(1.0 / 6)
            for i, q in enumerate(toward):
                along = None
                for e, t in zip(DIRS[q], v):
                    if e:
                        t = t if e > 0 else -t
                        along = t if along is None else along + t
                weight = np.float32(1.25 / 18 if sum(map(abs, DIRS[q])) == 1 else 1.25 / 36)
                feq = (rho * weight) * (base + along * (along * np.float32(0.5) + np.float32(1.0)))
                ghost[i, :, cut(c)] = feq - near[i] * np.float32(0.25)

    by_side(chain, side)


def far_kernel(tiles, halves, chain, g, fac, halo, slabs, after, row, send, beside):
    rows = g.shape[1]
    lane, sub = iotas()

    def side(up):
        x, inwards = (rows - 1, rows - 2) if up else (0, 1)
        lo, hi, place = (None, halo, "last") if up else (halo, None, "first")
        for c in range(tiles):
            for at, ref, where in ((x, row, place), (inwards, beside, "mid")):
                f = stream(g, lo, hi, at, c, tiles, halves, lane, sub, where)
                post = collide(f, fac[at, :, cut(c)])
                for q in range(19):
                    ref[q, :, cut(c)] = post[q]
        look_ahead(
            tiles, halves, up, lambda q, c: row[q, :, cut(c)], lambda q, c: beside[q, :, cut(c)], send
        )
        send[13] = slabs[0, x]

    by_side(chain, side)


def speed(f, fc):
    s = [f[2 * p + 1] + f[2 * p + 2] for p in range(9)]
    d = [f[2 * p + 1] - f[2 * p + 2] for p in range(9)]
    rho = f[0] + (((s[0] + s[1]) + (s[2] + s[3])) + ((s[4] + s[5]) + (s[6] + s[7])) + s[8])
    jx = d[0] + ((d[3] + d[4]) + (d[5] + d[6]))
    jy = d[1] + ((d[3] - d[4]) + (d[7] + d[8]))
    jz = d[2] + ((d[5] - d[6]) + (d[7] - d[8]))
    inv = np.float32(1.0) / rho
    return [jnp.where(fc != fc, np.float32(0.0), j * inv) for j in (jz, jx, jy)]


def inner_speed_kernel(tiles, halves, g, fac, after, u):
    rows = g.shape[1]
    lane, sub = iotas()

    def row(x, _):
        for c in range(tiles):
            f = stream(g, None, None, x, c, tiles, halves, lane, sub, "mid")
            for i, v in enumerate(speed(f, fac[x, :, cut(c)])):
                u[i, x - 2, :, cut(c)] = v
        return 0

    lax.fori_loop(2, rows - 2, row, 0)


def final_kernel(tiles, halves, g, fac, halo0, halo1, start, after, out, token, buf, sems):
    rows = g.shape[1]
    lane, sub = iotas()
    odd = upper(1)
    token[...] = jnp.zeros(token.shape, F32)

    def row_of(q, x):
        at = x - DIRS[q][0]
        if at < 0:
            return lambda qq, cc: jnp.where(
                odd, halo0[UP.index(qq), :, cut(cc)], halo1[UP.index(qq), :, cut(cc)]
            )
        if at >= rows:
            return lambda qq, cc: jnp.where(
                odd, halo1[DOWN.index(qq), :, cut(cc)], halo0[DOWN.index(qq), :, cut(cc)]
            )
        return lambda qq, cc: g[qq, at, :, cut(cc)]

    copies = []
    for q in range(19):
        for c in range(tiles):
            new = []
            for x in range(rows):
                fc = fac[x, :, cut(c)]
                if q == 0:
                    v = g[0, x, :, cut(c)]
                else:
                    v = pull(row_of(q, x), q, c, tiles, halves, lane, sub)
                    v = jnp.where(v != v, g[OPP[q], x, :, cut(c)], v)
                new.append(jnp.where(fc != fc, start[q, x, :, cut(c)], v))
            for i, t in enumerate(swap_tile(new, sub)):
                first = (i * tiles + c) * SUBS
                buf[q, first : first + SUBS, :] = t
        copy = pltpu.make_async_copy(buf.at[q], out.at[q], sems.at[q])
        copy.start()
        copies.append(copy)
    for copy in copies:
        copy.wait()


def slope(p, q):
    return np.float32(0.5) * (
        jnp.maximum(jnp.minimum(p, q), np.float32(0.0)) + jnp.minimum(jnp.maximum(p, q), np.float32(0.0))
    )


def loss(s, c):
    return [np.float32(TRANSFER) * a * (np.float32(1.0) - b) for a, b in zip(s, c)]


def ends_of(parts, strips):
    place = lax.axis_index("wide") * parts + lax.axis_index("narrow")
    return place == 0, place == strips - 1


ZERO = np.float32(0.0)


def each(f, *lists):
    return [f(*t) for t in zip(*lists)]


def less(a, b):
    return each(lambda x, y: x - y, a, b)


def times(a, b):
    return each(lambda x, y: x * y, a, b)


def face(w, va, vb, c, cn, sl, sn, dn):
    a = each(lambda w, x, y: w * np.float32(0.5) * (x + y), w, va, vb)
    return each(
        lambda a, w, c, cn, sl, sn, dn: a * jnp.where(a > 0, c + sl, cn - sn) - np.float32(DIFFUSION) * w * dn,
        a, w, c, cn, sl, sn, dn,
    )


def floored(p):
    return [jnp.maximum(t, np.float32(FLOOR)) for t in p]


class Step:
    def __init__(self, tiles, halves, conc, poro, flow, cross, napl):
        self.tiles, self.halves = tiles, halves
        self.lane, self.sub = iotas()
        self.conc, self.poro, self.flow = (self.keep(f) for f in (conc, poro, flow))
        self.cross, self.napl = cross, napl
        self.gap = self.keep(lambda r: less(self.conc(r + 1), self.conc(r)))
        self.lean = self.keep(lambda r: each(slope, self.gap(r - 1), self.gap(r)))

    @staticmethod
    def keep(f):
        seen = {}

        def get(r):
            if r not in seen:
                seen[r] = f(r)
            return seen[r]

        return get

    def after(self, v):
        out = []
        for c in range(self.tiles):
            if c < self.tiles - 1:
                side = v[c + 1]
            else:
                edge = self.sub % self.halves == self.halves - 1
                side = jnp.where(edge, ZERO, pltpu.roll(v[0], SUBS - 1, 0))
            out.append(pltpu.roll(jnp.where(self.lane == 0, side, v[c]), LANES - 1, 1))
        return out

    def before(self, v):
        out = []
        for c in range(self.tiles):
            if c > 0:
                side = v[c - 1]
            else:
                edge = self.sub % self.halves == 0
                side = jnp.where(edge, ZERO, pltpu.roll(v[self.tiles - 1], 1, 0))
            out.append(pltpu.roll(jnp.where(self.lane == LANES - 1, side, v[c]), 1, 1))
        return out

    def above(self, v):
        return [pltpu.roll(t, SUBS - self.halves, 0) for t in v]

    def below(self, v):
        return [pltpu.roll(t, self.halves, 0) for t in v]

    def flow_face(self, r):
        return face(
            times(self.poro(r), self.poro(r + 1)), self.flow(r), self.flow(r + 1), self.conc(r), self.conc(r + 1),
            self.lean(r), self.lean(r + 1), self.gap(r),
        )

    def run(self, r, low=True, high=True):
        c, p, s = self.conc(r), self.poro(r), self.napl(r)
        change = None
        if low:
            change = self.flow_face(r - 1)
        if high:
            out = self.flow_face(r)
            change = [-t for t in out] if change is None else less(change, out)
        vel = self.cross(r)
        for after, before, v, open_ends in (
            (self.after, self.before, vel[0], True), (self.above, self.below, vel[1], False),
        ):
            cn = after(c)
            dn = less(cn, c)
            dm = less(c, before(c)) if open_ends else before(dn)
            s0 = each(slope, dm, dn)
            flux = face(times(p, after(p)), v, after(v), c, cn, s0, after(s0), dn)
            change = each(lambda t, a, b: t + (a - b), change, before(flux), flux)
        rate = loss(s, c)
        cnew = each(lambda c, t, k, p: c + (t + k) / p, c, change, rate, floored(p))
        return cnew, each(lambda s, k: s - np.float32(DEPLETION) * k, s, rate)


def read(slab):
    return [slab[:, cut(c)] for c in range(slab.shape[1] // LANES)]


def write(slab, tiles):
    for c, t in enumerate(tiles):
        slab[:, cut(c)] = t


def early_kernel(tiles, halves, slabs, u, ue0, ue1, cs):
    rows = slabs.shape[1]
    odd = upper(1)

    def flow(r):
        if r == 1:
            return pick(odd, read(ue0.at[1, 1]), read(ue1.at[1, 1]))
        if r == rows - 2:
            return pick(odd, read(ue1.at[1, 1]), read(ue0.at[1, 1]))
        return read(u.at[1, r - 2])

    step = Step(
        tiles, halves, lambda r: read(slabs.at[0, r]), lambda r: read(slabs.at[2, r]), flow,
        lambda r: (read(u.at[2, r - 2]), read(u.at[0, r - 2])), lambda r: read(slabs.at[1, r]),
    )
    for r in range(2, rows - 2):
        for k, v in enumerate(step.run(r)):
            write(cs.at[k, r - 2], v)


def static_readers(ends, up, slabs, halo, there, flags):
    rows = slabs.shape[1]
    first, last = ends_of(*ends)

    def conc(r):
        if 0 <= r < rows:
            return read(slabs.at[0, r])
        beyond = read(halo.at[13] if r in (-1, rows) else there.at[3])
        return pick(last, read(slabs.at[0, rows - 1]), beyond) if up else [jnp.where(first, ZERO, t) for t in beyond]

    def poro(r):
        if 0 <= r < rows:
            return read(slabs.at[2, r])
        return pick(last if up else first, read(flags.at[1 if up else 0]), read(there.at[4]))

    return conc, poro


def rim_kernel(tiles, halves, ends, chain, g, fac, ghost, u, slabs, halo, after, ue, cs, send):
    rows = g.shape[1]
    lane, sub = iotas()

    def side(up):
        x, beside = (rows - 1, rows - 2) if up else (0, 1)
        lo, hi, place = (None, ghost, "last") if up else (ghost, None, "first")
        for n, (at, where) in enumerate(((x, place), (beside, "mid"))):
            for c in range(tiles):
                f = stream(g, lo, hi, at, c, tiles, halves, lane, sub, where)
                for i, v in enumerate(speed(f, fac[at, :, cut(c)])):
                    ue[n, i, :, cut(c)] = v
        conc, poro = static_readers(ends, up, slabs, halo, None, None)

        def vel(k, r):
            return read(ue.at[0 if r == x else 1, k] if r in (x, beside) else u.at[k, r - 2])

        step = Step(
            tiles, halves, conc, poro, lambda r: vel(1, r), lambda r: (vel(2, r), vel(0, r)),
            lambda r: read(slabs.at[1, r]),
        )
        edge = step.run(x, low=up, high=not up)
        inward = step.run(beside)
        for i, new in enumerate((edge, inward)):
            for k in range(2):
                write(cs.at[i, k], new[k])
            write(send.at[1 + i], new[0])
        send[0] = ue[0, 1]
        send[3] = slabs[0, beside]
        send[4] = slabs[2, x]

    by_side(chain, side)


def state_reader(rows, edge, inner, rims):
    def state(k, r):
        if r in (0, rows - 1):
            return edge(k, r)
        if r in (1, rows - 2):
            return rims(k, r)
        return read(inner.at[k, r - 2])

    return state


def middle_kernel(tiles, halves, slabs, u, inner, rim0, rim1, out):
    rows = slabs.shape[1]
    odd = upper(1)

    def rims(k, r):
        a, b = (rim0, rim1) if r == 1 else (rim1, rim0)
        return pick(odd, read(a.at[1, k]), read(b.at[1, k]))

    state = state_reader(rows, None, inner, rims)
    step = Step(
        tiles, halves, lambda r: state(0, r), lambda r: read(slabs.at[2, r]), lambda r: read(u.at[1, r - 2]),
        lambda r: (read(u.at[2, r - 2]), read(u.at[0, r - 2])), lambda r: state(1, r),
    )
    for r in range(3, rows - 3):
        write(out.at[r - 3], step.run(r)[0])


def late_kernel(
    tiles, halves, ends, chain, slabs, u, ue, inner, rim, halo, flags, there, after, out
):
    rows = slabs.shape[1]
    first, last = ends_of(*ends)

    def side(up):
        x = rows - 1 if up else 0
        beyond = rows if up else -1
        ghost = last if up else first
        conc, poro = static_readers(ends, up, slabs, halo, there, flags)

        def vel(k, r):
            if r == beyond:
                return pick(ghost, read(ue.at[0, 1]), read(there.at[0]))
            if r in (x, x - 1 if up else x + 1):
                return read(ue.at[0 if r == x else 1, k])
            return read(u.at[k, r - 2])

        def cross(r):
            return vel(2, r), vel(0, r)

        one = Step(tiles, halves, conc, poro, lambda r: vel(1, r), cross, None)
        flux = one.flow_face(x if up else -1)
        sign = np.float32(-1.0 if up else 1.0)
        edge = each(lambda c, f, p: c + sign * f / p, read(rim.at[0, 0]), flux, floored(poro(x)))
        outer = each(lambda c, f, p: c - sign * f / p, read(there.at[1]), flux, floored(poro(beyond)))
        second = read(there.at[2])
        if up:
            outer, second = pick(ghost, edge, outer), pick(ghost, edge, second)
        else:
            outer, second = ([jnp.where(ghost, ZERO, t) for t in v] for v in (outer, second))
        state = state_reader(
            rows, lambda k, r: read(rim.at[0, k]) if k else edge, inner, lambda k, r: read(rim.at[1, k])
        )

        def after_one(r):
            if r < 0 or r >= rows:
                return outer if r == beyond else second
            return state(0, r)

        two = Step(tiles, halves, after_one, poro, lambda r: vel(1, r), cross, lambda r: state(1, r))
        for i in range(3):
            new = two.run(rows - 1 - i if up else i)
            write(out.at[i], new[0])
            if i == 0:
                write(out.at[3], new[1])

    by_side(chain, side)


def deal_kernel(tiles, halves, parts, inner, rim0, rim1, late0, late1, mid, *refs):
    *blocks, whole = refs
    rows = inner.shape[1] + 4
    odd = upper(1)
    _, sub = iotas()
    for c in range(tiles):

        def ends_pick(a, b):
            return jnp.where(odd, a, b)

        lo = [ends_pick(late0[i, :, cut(c)], late1[i, :, cut(c)]) for i in range(4)]
        hi = [ends_pick(late1[i, :, cut(c)], late0[i, :, cut(c)]) for i in range(4)]
        conc = lo[:3] + [mid[r, :, cut(c)] for r in range(rows - 6)] + hi[2::-1]
        left = [lo[3]]
        for r in range(1, rows - 1):
            if r in (1, rows - 2):
                a, b = (rim0, rim1) if r == 1 else (rim1, rim0)
                cc, ss = (ends_pick(a[1, k, :, cut(c)], b[1, k, :, cut(c)]) for k in range(2))
            else:
                cc, ss = (inner[k, r - 2, :, cut(c)] for k in range(2))
            left.append(ss - np.float32(DEPLETION) * loss([ss], [cc])[0])
        left.append(hi[3])
        run = whole.shape[3]
        for k, tile in enumerate((conc, left)):
            for i, t in enumerate(swap_tile(tile, sub)):
                column = (i % halves * tiles + c) * SUBS
                at = column % run
                whole[column // run, k, i // halves, at : at + SUBS, :] = t
    for k in range(parts):
        blocks[k][...] = whole[lax.axis_index("narrow") ^ k]


def gather_kernel(parts, order, *refs):
    blocks = refs[:parts]
    *outs, sems = refs[parts:]
    copies = []
    for k, block in zip(order, blocks):
        origin = lax.axis_index("narrow") ^ k
        for i, out in enumerate(outs):
            copies.append(pltpu.make_async_copy(block.at[i], out.at[:, origin], sems.at[i, k]))
            copies[-1].start()
    for copy in copies:
        copy.wait()


def call(kernel, out_shape, args, scratch=(), hbm=(), free=(), hbm_out=(), name=None, aliases=None):
    def spec(i, hbm, free=()):
        return pl.BlockSpec(memory_space=pltpu.HBM if i in hbm else pl.ANY if i in free else pltpu.VMEM)

    single = not isinstance(out_shape, tuple)
    shapes = (out_shape,) if single else out_shape
    out = pl.pallas_call(
        kernel,
        out_shape=shapes,
        in_specs=[spec(i, hbm, free) for i in range(len(args))],
        out_specs=tuple(spec(i, hbm_out) for i in range(len(shapes))),
        scratch_shapes=list(scratch),
        name=name,
        input_output_aliases=aliases or {},
        compiler_params=pltpu.CompilerParams(vmem_limit_bytes=VMEM_LIMIT),
        cost_estimate=pl.CostEstimate(flops=1024, bytes_accessed=1024, transcendentals=0),
    )(*args)
    return out[0] if single else out


def local(populations, phase, porosity, napl, concentration, flags):
    layers, rows, width = phase.shape
    halves = SUBS // layers
    length = width // halves
    tiles = length // LANES
    parts = lax.axis_size("narrow")
    strips = lax.axis_size("wide") * parts
    both = ("wide", "narrow")
    pairs = (
        [(i, i ^ 1) for i in range(strips)],
        [(i, (i + 1 if i % 2 else i - 1) % strips) for i in range(strips)],
    )
    slab = (SUBS, length)
    ends = (parts, strips)
    run = width // LANES * SUBS // parts

    def hold(*shape, dtype=F32):
        return pltpu.VMEM(shape, dtype)

    def swap(chain, array):
        return lax.ppermute(array, both, pairs[chain])

    pop = to_view(populations)
    views = [to_view(a) for a in (phase, concentration, napl, porosity)]
    flat = views[0].shape
    chunks = pop.reshape(19, SUBS, tiles, SUBS, LANES)
    given = [pltpu.with_memory_space_constraint(a, pltpu.HBM) for a in (chunks, *views, flags)]
    popv, phv, cov, nav, pov, flv, row1, send = call(
        functools.partial(first_kernel, tiles, halves),
        (
            hold(*chunks.shape), hold(*flat, dtype=jnp.int32), hold(*flat), hold(*flat), hold(*flat),
            hold(*flags.shape, dtype=jnp.int32), hold(19, *slab), hold(14, *slab),
        ),
        given, scratch=(pltpu.VMEM((19, *slab), F32), pltpu.SemaphoreType.DMA((tiles + 5,))),
        hbm=range(6), name="first",
    )
    popv = popv.reshape(pop.shape)
    halo1 = head1 = swap(1, send)
    row0, send = call(
        functools.partial(second_kernel, tiles, halves), (hold(19, *slab), hold(14, *slab)), (popv, phv, send),
        scratch=(pltpu.VMEM((19, *slab), F32),), free=(2,), name="second",
    )
    halo0 = head0 = swap(0, send)
    g, fac, start, slabs, open_ends = call(
        functools.partial(first_inner_kernel, tiles, halves),
        (
            hold(19, rows, *slab), hold(rows, *slab), hold(19, rows, *slab), hold(3, rows, *slab),
            hold(2, *slab),
        ),
        (popv, phv, cov, nav, pov, flv, row0, row1), name="first_inner",
    )

    def inner_rows(g, after):
        return call(
            functools.partial(inner_kernel, tiles, halves), hold(19, rows, *slab), (g, fac, after), free=(2,),
            name="inner",
        )

    def arrive(chain, g, halo, head, after, new):
        return call(
            functools.partial(arrive_kernel, tiles, halves, chain), (hold(19, rows, *slab), hold(5, *slab)),
            (g, fac, halo, head, after, new), free=(4, 5), name=f"arrive{chain}", aliases={5: 0},
        )

    def far(chain, g, ghost, after):
        return call(
            functools.partial(far_kernel, tiles, halves, chain), (hold(19, *slab), hold(14, *slab)),
            (g, fac, ghost, slabs, after), scratch=(pltpu.VMEM((19, *slab), F32),), free=(4,), name=f"far{chain}",
        )

    def rim(chain, g, ghost, halo, after):
        return call(
            functools.partial(rim_kernel, tiles, halves, ends, chain),
            (hold(2, 3, *slab), hold(2, 2, *slab), hold(5, *slab)),
            (g, fac, ghost, u, slabs, halo, after), free=(6,), name=f"rim{chain}",
        )

    after = slabs
    for pair in range(LBM_STEPS // 2):
        new = inner_rows(g, after)
        if pair < LBM_STEPS // 2 - 1:
            later, ghost1 = arrive(1, g, halo1, head1, g, new)
            row1, send1 = far(1, later, ghost1, ghost1)
            halo1 = swap(1, send1)
            later, ghost0 = arrive(0, g, halo0, head0, send1, later)
            row0, send0 = far(0, later, ghost0, ghost0)
            halo0 = swap(0, send0)
            new = inner_rows(later, send0)
            g = call(
                put_kernel, hold(19, rows, *slab), (new, row0, row1), name="put", aliases={0: 0}, free=(0,)
            )
            after = g
    u = call(
        functools.partial(inner_speed_kernel, tiles, halves), hold(3, rows - 4, *slab), (new, fac, new),
        free=(2,), name="inner_speed",
    )
    later, ghost1 = arrive(1, g, halo1, head1, u, new)
    ue1, rim1, send1 = rim(1, later, ghost1, halo1, ghost1)
    there1 = swap(1, send1)
    g, ghost0 = arrive(0, g, halo0, head0, send1, later)
    ue0, rim0, send0 = rim(0, g, ghost0, halo0, ghost0)
    there0 = swap(0, send0)
    inner = call(
        functools.partial(early_kernel, tiles, halves), hold(2, rows - 4, *slab), (slabs, u, ue0, ue1),
        name="early",
    )
    mid = call(
        functools.partial(middle_kernel, tiles, halves), hold(rows - 6, *slab), (slabs, u, inner, rim0, rim1),
        name="middle",
    )
    out, token = call(
        functools.partial(final_kernel, tiles, halves),
        (jax.ShapeDtypeStruct((19, *flat), F32), hold(SUBS, LANES)),
        (g, fac, ghost0, ghost1, start, mid),
        scratch=(pltpu.VMEM((19, *flat), F32), pltpu.SemaphoreType.DMA((19,))),
        free=(5,), hbm_out=(0,), name="final",
    )
    late1 = call(
        functools.partial(late_kernel, tiles, halves, ends, 1), hold(4, *slab),
        (slabs, u, ue1, inner, rim1, halo1, open_ends, there1, token), free=(8,), name="late1",
    )
    late0 = call(
        functools.partial(late_kernel, tiles, halves, ends, 0), hold(4, *slab),
        (slabs, u, ue0, inner, rim0, halo0, open_ends, there0, late1), free=(8,), name="late0",
    )
    block = (2, layers, run, LANES)
    blocks = call(
        functools.partial(deal_kernel, tiles, halves, parts), tuple(hold(*block) for _ in range(parts)),
        (inner, rim0, rim1, late0, late1, mid),
        scratch=(pltpu.VMEM((parts, *block), F32),), name="deal",
    )
    order = [0, *range(2, parts), 1]
    came = [blocks[0]]
    for k in order[1:]:
        came.append(lax.ppermute(blocks[k], "narrow", [(i, i ^ k) for i in range(parts)]))
    tile = (layers, parts, run, LANES)
    conc_out, napl_out = call(
        functools.partial(gather_kernel, parts, order),
        (jax.ShapeDtypeStruct(tile, F32), jax.ShapeDtypeStruct(tile, F32)),
        came, scratch=(pltpu.SemaphoreType.DMA((2, parts)),), hbm_out=(0, 1), name="gather",
    )
    shape = (layers, rows * parts, width // parts)

    def tile_of(a):
        return from_view(a.reshape(layers * parts * run, LANES), shape)

    return from_view(out, populations.shape), tile_of(conc_out), tile_of(napl_out)


def solution(mesh):
    strip = P(None, ("wide", "narrow"), None)
    in_specs = (P(None, None, ("wide", "narrow"), None), strip, strip, strip, strip, P())
    tile = P(None, "wide", "narrow")
    out_specs = (P(None, None, ("wide", "narrow"), None), tile, tile)
    return jax.shard_map(local, mesh=mesh, in_specs=in_specs, out_specs=out_specs, check_vma=False)
```

```python
import functools

import jax
import jax.numpy as jnp
import numpy as np
from jax import lax
from jax.experimental import pallas as pl
from jax.experimental.pallas import tpu as pltpu
from jax.sharding import PartitionSpec as P

LBM_STEPS = 4
F32 = jnp.float32

DIRS = [
    (0, 0, 0), (1, 0, 0), (-1, 0, 0), (0, 1, 0), (0, -1, 0), (0, 0, 1), (0, 0, -1),
    (1, 1, 0), (-1, -1, 0), (1, -1, 0), (-1, 1, 0), (1, 0, 1), (-1, 0, -1), (1, 0, -1),
    (-1, 0, 1), (0, 1, 1), (0, -1, -1), (0, 1, -1), (0, -1, 1),
]
OPP = [0, 2, 1, 4, 3, 6, 5, 8, 7, 10, 9, 12, 11, 14, 13, 16, 15, 18, 17]
UP = [1, 7, 9, 11, 13]
DOWN = [2, 8, 10, 12, 14]
DIFFUSION = 0.15
TRANSFER = 0.3
DEPLETION = 0.5
FLOOR = 0.3
SUBS = 8
LANES = 128
VMEM_LIMIT = 16 * 1024 * 1024


def to_view(array):
    *lead, rows, width = array.shape
    n = len(lead)
    t = array.reshape(*lead, rows // SUBS, SUBS, width // LANES, LANES)
    t = t.transpose(*range(n), n, n + 2, n + 1, n + 3)
    return t.reshape(*lead[:-1], lead[-1] * rows * width // LANES, LANES)


def from_view(view, shape):
    *lead, rows, width = shape
    n = len(lead)
    t = view.reshape(*lead, rows // SUBS, width // LANES, SUBS, LANES)
    t = t.transpose(*range(n), n, n + 2, n + 1, n + 3)
    return t.reshape(shape)


def iotas():
    lane = lax.broadcasted_iota(jnp.int32, (SUBS, LANES), 1)
    sub = lax.broadcasted_iota(jnp.int32, (SUBS, LANES), 0)
    return lane, sub


def cut(c):
    return slice(c * LANES, (c + 1) * LANES)


def strided(tiles, c, x):
    return pl.ds(c * SUBS + x, SUBS, stride=tiles * SUBS)


def collide(f, fac):
    s = [f[2 * p + 1] + f[2 * p + 2] for p in range(9)]
    d = [f[2 * p + 1] - f[2 * p + 2] for p in range(9)]
    rho = f[0] + (((s[0] + s[1]) + (s[2] + s[3])) + ((s[4] + s[5]) + (s[6] + s[7])) + s[8])
    jx = d[0] + ((d[3] + d[4]) + (d[5] + d[6]))
    jy = d[1] + ((d[3] - d[4]) + (d[7] + d[8]))
    jz = d[2] + ((d[5] - d[6]) + (d[7] - d[8]))
    inv = fac / rho
    vx, vy, vz = jx * inv, jy * inv, jz * inv
    w1 = rho * np.float32(1.25 / 18)
    w2 = rho * np.float32(1.25 / 36)
    w4 = rho * np.float32(1.25 / 72)
    a1 = w1 - w1 * ((vx * vx + vy * vy + vz * vz) * np.float32(1.0 / 6))
    a2 = a1 * np.float32(0.5)
    post = [a1 * np.float32(6.0) - f[0] * np.float32(0.25)]
    axes = [vx, vy, vz, vx + vy, vx - vy, vx + vz, vx - vz, vy + vz, vy - vz]
    for p, v in enumerate(axes):
        wa, wh, base = (w1, w2, a1) if p < 3 else (w2, w4, a2)
        even = (base + (wh * v) * v) - s[p] * np.float32(0.125)
        odd = wa * v - d[p] * np.float32(0.125)
        post += [even + odd, even - odd]
    return post


def pull(load, q, c, tiles, halves, lane, sub):
    _, cross, layer = DIRS[q]
    v = load(q, c)
    if cross == 1:
        if c > 0:
            side = load(q, c - 1)
        else:
            side = jnp.where(sub % halves == 0, jnp.nan, pltpu.roll(load(q, tiles - 1), 1, 0))
        v = pltpu.roll(jnp.where(lane == LANES - 1, side, v), 1, 1)
    elif cross == -1:
        if c < tiles - 1:
            side = load(q, c + 1)
        else:
            side = jnp.where(sub % halves == halves - 1, jnp.nan, pltpu.roll(load(q, 0), SUBS - 1, 0))
        v = pltpu.roll(jnp.where(lane == 0, side, v), LANES - 1, 1)
    if layer:
        v = pltpu.roll(v, (layer * halves) % SUBS, 0)
    return v


def stream(g, lo, hi, x, c, tiles, halves, lane, sub, place):
    def load(q, cc):
        flow = DIRS[q][0]
        if flow == 1 and place == "first":
            return lo[UP.index(q), :, cut(cc)]
        if flow == -1 and place == "last":
            return hi[DOWN.index(q), :, cut(cc)]
        return g[q, x - flow, :, cut(cc)]

    f = [g[0, x, :, cut(c)]]
    for q in range(1, 19):
        v = pull(load, q, c, tiles, halves, lane, sub)
        f.append(jnp.where(v != v, g[OPP[q], x, :, cut(c)], v))
    return f


def drag(ph):
    return jnp.where(ph == 2, jnp.nan, jnp.where(ph == 1, np.float32(1.5), np.float32(3.0)))


def swap_tile(v, sub):
    v = list(v)
    for k in (4, 2, 1):
        low = sub & k == 0
        for i in range(SUBS):
            if not i & k:
                a, b = v[i], v[i + k]
                v[i] = jnp.where(low, a, pltpu.roll(b, k, 0))
                v[i + k] = jnp.where(low, pltpu.roll(a, SUBS - k, 0), b)
    return v


def upper(chain):
    odd = lax.rem(lax.axis_index("narrow"), 2) == 1
    return odd if chain else jnp.logical_not(odd)


def by_side(chain, side):
    pl.when(upper(chain))(lambda: side(True))
    pl.when(jnp.logical_not(upper(chain)))(lambda: side(False))


def pick(flag, a, b):
    return [jnp.where(flag, x, y) for x, y in zip(a, b)]


def start_row(tiles, pop, phase, x, row, c):
    at = strided(tiles, c, x)
    fc = drag(phase[at, :])
    post = collide([pop[q, at, :] for q in range(19)], fc)
    for q in range(19):
        row[q, :, cut(c)] = post[q]
    return fc


def look_ahead(tiles, halves, up, edge, beside, send):
    lane, sub = iotas()
    toward, back = (UP, DOWN) if up else (DOWN, UP)
    for c in range(tiles):
        sums = [None] * 3
        for q in range(19):
            if q in back:
                continue
            if q == 0:
                f = edge(0, c)
            else:
                f = pull(beside if q in toward else edge, q, c, tiles, halves, lane, sub)
                f = jnp.where(f != f, edge(OPP[q], c), f)
            if q in toward:
                i = toward.index(q)
                send[i, :, cut(c)] = edge(q, c)
                send[5 + i, :, cut(c)] = f
            else:
                for k, e in enumerate((1, *DIRS[q][1:])):
                    if e:
                        t = f if e > 0 else -f
                        sums[k] = t if sums[k] is None else sums[k] + t
        for k in range(3):
            send[10 + k, :, cut(c)] = sums[k]


def start_rows(tiles, halves, chain, pop, phase, row, send, beside, ready=None):
    def tile(c, up):
        x, inwards = (SUBS - 1, SUBS - 2) if up else (0, 1)
        send[13, :, cut(c)] = start_row(tiles, pop, phase, x, row, c)
        start_row(tiles, pop, phase, inwards, beside, c)

    for c in range(tiles):
        if ready is not None:
            ready(c)
        by_side(chain, functools.partial(tile, c))

    def side(up):
        look_ahead(
            tiles, halves, up, lambda q, c: row[q, :, cut(c)], lambda q, c: beside[q, :, cut(c)], send
        )

    by_side(chain, side)


def first_kernel(
    tiles, halves, pop_h, phase_h, conc_h, napl_h, poro_h, flags_h,
    pop, phase, conc, napl, poro, flags, row, send, beside, sems,
):
    small = [
        pltpu.make_async_copy(a, b, sems.at[4 * tiles + i])
        for i, (a, b) in enumerate(
            ((phase_h, phase), (conc_h, conc), (poro_h, poro), (napl_h, napl), (flags_h, flags))
        )
    ]
    groups = [pl.ds(q, min(5, 19 - q)) for q in range(0, 19, 5)]
    large = [
        [pltpu.make_async_copy(pop_h.at[qs, :, c], pop.at[qs, :, c], sems.at[4 * c + i]) for i, qs in enumerate(groups)]
        for c in range(tiles)
    ]
    small[0].start()
    for copy in sum(large, []) + small[1:]:
        copy.start()
    small[0].wait()
    flat = pop.reshape(pop.shape[0], SUBS * tiles * SUBS, LANES)
    start_rows(tiles, halves, 1, flat, phase, row, send, beside, ready=lambda c: [copy.wait() for copy in large[c]])
    for copy in small[1:]:
        copy.wait()


def second_kernel(tiles, halves, pop, phase, after, row, send, beside):
    start_rows(tiles, halves, 0, pop, phase, row, send, beside)


def merge_rows(out, row0, row1, count):
    rows = out.shape[1]

    def side(up):
        for k in range(count):
            out[k, 0] = (row0 if up else row1)[k]
            out[k, rows - 1] = (row1 if up else row0)[k]

    by_side(1, side)


def first_inner_kernel(
    tiles, halves, pop, phase, conc, napl, poro, flags, row0, row1, g, fac, start, slabs, open_ends
):
    rows = g.shape[1]
    length = tiles * LANES
    _, sub = iotas()

    def to_slabs(read, write):
        for c in range(tiles):
            v = [read(pl.ds((i * tiles + c) * SUBS, SUBS)) for i in range(SUBS)]
            for x, t in enumerate(swap_tile(v, sub)):
                write(x, cut(c), t)

    def store(ref, k):
        def write(x, at, t):
            ref[k, x, :, at] = t

        return write

    def store_fac(x, at, t):
        fac[x, :, at] = t

    to_slabs(lambda at: drag(phase[at, :]), store_fac)

    def direction(q, _):
        to_slabs(lambda at: pop[q, at, :], store(start, q))
        return 0

    lax.fori_loop(0, 19, direction, 0)

    def row(x, _):
        for c in range(tiles):
            post = collide([start[q, x, :, cut(c)] for q in range(19)], fac[x, :, cut(c)])
            for q in range(19):
                g[q, x, :, cut(c)] = post[q]
        return 0

    lax.fori_loop(1, rows - 1, row, 0)
    merge_rows(g, row0, row1, 19)
    for k, ref in enumerate((conc, napl, poro)):
        to_slabs(lambda at, ref=ref: ref[at, :], store(slabs, k))
    for k in range(2):
        for z in range(SUBS // halves):
            for h in range(halves):
                line = flags[k, z : z + 1, h * length : (h + 1) * length]
                open_ends[k, z * halves + h : z * halves + h + 1, :] = line.astype(F32)


def inner_kernel(tiles, halves, g, fac, after, out):
    rows = g.shape[1]
    lane, sub = iotas()

    def row(x, _):
        for c in range(tiles):
            f = stream(g, None, None, x, c, tiles, halves, lane, sub, "mid")
            post = collide(f, fac[x, :, cut(c)])
            for q in range(19):
                out[q, x, :, cut(c)] = post[q]
        return 0

    lax.fori_loop(1, rows - 1, row, 0)


def put_kernel(inner, row0, row1, out):
    merge_rows(out, row0, row1, 19)


def arrive_kernel(tiles, halves, chain, g, fac, halo, first_halo, after, inner, out, ghost):
    rows = g.shape[1]
    lane, sub = iotas()

    def side(up):
        x = rows - 1 if up else 0
        lo, hi, place = (None, halo, "last") if up else (halo, None, "first")
        toward, back = (DOWN, UP) if up else (UP, DOWN)
        for c in range(tiles):
            post = collide(stream(g, lo, hi, x, c, tiles, halves, lane, sub, place), fac[x, :, cut(c)])
            for q in range(19):
                out[q, x, :, cut(c)] = post[q]
            near = [halo[5 + i, :, cut(c)] for i in range(5)]
            sums = [halo[10, :, cut(c)], None, halo[11, :, cut(c)], halo[12, :, cut(c)]]
            known = list(zip(toward, near))
            for i, q in enumerate(back):
                f = pull(lambda q, cc: g[q, x, :, cut(cc)], q, c, tiles, halves, lane, sub)
                known.append((q, jnp.where(f != f, halo[i, :, cut(c)], f)))
            for q, f in known:
                for k, e in enumerate((1, *DIRS[q])):
                    if e:
                        t = f if e > 0 else -f
                        sums[k] = t if sums[k] is None else sums[k] + t
            rho = sums[0]
            inv = first_halo[13, :, cut(c)] / rho
            v = [j * inv for j in sums[1:]]
            base = np.float32(1.0) - (v[0] * v[0] + v[1] * v[1] + v[2] * v[2]) * np.float32(1.0 / 6)
            for i, q in enumerate(toward):
                along = None
                for e, t in zip(DIRS[q], v):
                    if e:
                        t = t if e > 0 else -t
                        along = t if along is None else along + t
                weight = np.float32(1.25 / 18 if sum(map(abs, DIRS[q])) == 1 else 1.25 / 36)
                feq = (rho * weight) * (base + along * (along * np.float32(0.5) + np.float32(1.0)))
                ghost[i, :, cut(c)] = feq - near[i] * np.float32(0.25)

    by_side(chain, side)


def far_kernel(tiles, halves, chain, g, fac, halo, slabs, after, row, send, beside):
    rows = g.shape[1]
    lane, sub = iotas()

    def side(up):
        x, inwards = (rows - 1, rows - 2) if up else (0, 1)
        lo, hi, place = (None, halo, "last") if up else (halo, None, "first")
        for c in range(tiles):
            for at, ref, where in ((x, row, place), (inwards, beside, "mid")):
                f = stream(g, lo, hi, at, c, tiles, halves, lane, sub, where)
                post = collide(f, fac[at, :, cut(c)])
                for q in range(19):
                    ref[q, :, cut(c)] = post[q]
        look_ahead(
            tiles, halves, up, lambda q, c: row[q, :, cut(c)], lambda q, c: beside[q, :, cut(c)], send
        )
        send[13] = slabs[0, x]

    by_side(chain, side)


def speed(f, fc):
    s = [f[2 * p + 1] + f[2 * p + 2] for p in range(9)]
    d = [f[2 * p + 1] - f[2 * p + 2] for p in range(9)]
    rho = f[0] + (((s[0] + s[1]) + (s[2] + s[3])) + ((s[4] + s[5]) + (s[6] + s[7])) + s[8])
    jx = d[0] + ((d[3] + d[4]) + (d[5] + d[6]))
    jy = d[1] + ((d[3] - d[4]) + (d[7] + d[8]))
    jz = d[2] + ((d[5] - d[6]) + (d[7] - d[8]))
    inv = np.float32(1.0) / rho
    return [jnp.where(fc != fc, np.float32(0.0), j * inv) for j in (jz, jx, jy)]


def inner_speed_kernel(tiles, halves, g, fac, after, u):
    rows = g.shape[1]
    lane, sub = iotas()

    def row(x, _):
        for c in range(tiles):
            f = stream(g, None, None, x, c, tiles, halves, lane, sub, "mid")
            for i, v in enumerate(speed(f, fac[x, :, cut(c)])):
                u[i, x - 2, :, cut(c)] = v
        return 0

    lax.fori_loop(2, rows - 2, row, 0)


def final_kernel(tiles, halves, g, fac, halo0, halo1, start, after, out, token, buf, sems):
    rows = g.shape[1]
    lane, sub = iotas()
    odd = upper(1)
    token[...] = jnp.zeros(token.shape, F32)

    def row_of(q, x):
        at = x - DIRS[q][0]
        if at < 0:
            return lambda qq, cc: jnp.where(
                odd, halo0[UP.index(qq), :, cut(cc)], halo1[UP.index(qq), :, cut(cc)]
            )
        if at >= rows:
            return lambda qq, cc: jnp.where(
                odd, halo1[DOWN.index(qq), :, cut(cc)], halo0[DOWN.index(qq), :, cut(cc)]
            )
        return lambda qq, cc: g[qq, at, :, cut(cc)]

    copies = []
    for q in range(19):
        for c in range(tiles):
            new = []
            for x in range(rows):
                fc = fac[x, :, cut(c)]
                if q == 0:
                    v = g[0, x, :, cut(c)]
                else:
                    v = pull(row_of(q, x), q, c, tiles, halves, lane, sub)
                    v = jnp.where(v != v, g[OPP[q], x, :, cut(c)], v)
                new.append(jnp.where(fc != fc, start[q, x, :, cut(c)], v))
            for i, t in enumerate(swap_tile(new, sub)):
                first = (i * tiles + c) * SUBS
                buf[q, first : first + SUBS, :] = t
        copy = pltpu.make_async_copy(buf.at[q], out.at[q], sems.at[q])
        copy.start()
        copies.append(copy)
    for copy in copies:
        copy.wait()


def slope(p, q):
    return np.float32(0.5) * (
        jnp.maximum(jnp.minimum(p, q), np.float32(0.0)) + jnp.minimum(jnp.maximum(p, q), np.float32(0.0))
    )


def loss(s, c):
    return [np.float32(TRANSFER) * a * (np.float32(1.0) - b) for a, b in zip(s, c)]


def ends_of(parts, strips):
    place = lax.axis_index("wide") * parts + lax.axis_index("narrow")
    return place == 0, place == strips - 1


ZERO = np.float32(0.0)


def each(f, *lists):
    return [f(*t) for t in zip(*lists)]


def less(a, b):
    return each(lambda x, y: x - y, a, b)


def times(a, b):
    return each(lambda x, y: x * y, a, b)


def face(w, va, vb, c, cn, sl, sn, dn):
    a = each(lambda w, x, y: w * np.float32(0.5) * (x + y), w, va, vb)
    return each(
        lambda a, w, c, cn, sl, sn, dn: a * jnp.where(a > 0, c + sl, cn - sn) - np.float32(DIFFUSION) * w * dn,
        a, w, c, cn, sl, sn, dn,
    )


def floored(p):
    return [jnp.maximum(t, np.float32(FLOOR)) for t in p]


class Step:
    def __init__(self, tiles, halves, conc, poro, flow, cross, napl):
        self.tiles, self.halves = tiles, halves
        self.lane, self.sub = iotas()
        self.conc, self.poro, self.flow = (self.keep(f) for f in (conc, poro, flow))
        self.cross, self.napl = cross, napl
        self.gap = self.keep(lambda r: less(self.conc(r + 1), self.conc(r)))
        self.lean = self.keep(lambda r: each(slope, self.gap(r - 1), self.gap(r)))

    @staticmethod
    def keep(f):
        seen = {}

        def get(r):
            if r not in seen:
                seen[r] = f(r)
            return seen[r]

        return get

    def after(self, v):
        out = []
        for c in range(self.tiles):
            if c < self.tiles - 1:
                side = v[c + 1]
            else:
                edge = self.sub % self.halves == self.halves - 1
                side = jnp.where(edge, ZERO, pltpu.roll(v[0], SUBS - 1, 0))
            out.append(pltpu.roll(jnp.where(self.lane == 0, side, v[c]), LANES - 1, 1))
        return out

    def before(self, v):
        out = []
        for c in range(self.tiles):
            if c > 0:
                side = v[c - 1]
            else:
                edge = self.sub % self.halves == 0
                side = jnp.where(edge, ZERO, pltpu.roll(v[self.tiles - 1], 1, 0))
            out.append(pltpu.roll(jnp.where(self.lane == LANES - 1, side, v[c]), 1, 1))
        return out

    def above(self, v):
        return [pltpu.roll(t, SUBS - self.halves, 0) for t in v]

    def below(self, v):
        return [pltpu.roll(t, self.halves, 0) for t in v]

    def flow_face(self, r):
        return face(
            times(self.poro(r), self.poro(r + 1)), self.flow(r), self.flow(r + 1), self.conc(r), self.conc(r + 1),
            self.lean(r), self.lean(r + 1), self.gap(r),
        )

    def run(self, r, low=True, high=True):
        c, p, s = self.conc(r), self.poro(r), self.napl(r)
        change = None
        if low:
            change = self.flow_face(r - 1)
        if high:
            out = self.flow_face(r)
            change = [-t for t in out] if change is None else less(change, out)
        vel = self.cross(r)
        for after, before, v, open_ends in (
            (self.after, self.before, vel[0], True), (self.above, self.below, vel[1], False),
        ):
            cn = after(c)
            dn = less(cn, c)
            dm = less(c, before(c)) if open_ends else before(dn)
            s0 = each(slope, dm, dn)
            flux = face(times(p, after(p)), v, after(v), c, cn, s0, after(s0), dn)
            change = each(lambda t, a, b: t + (a - b), change, before(flux), flux)
        rate = loss(s, c)
        cnew = each(lambda c, t, k, p: c + (t + k) / p, c, change, rate, floored(p))
        return cnew, each(lambda s, k: s - np.float32(DEPLETION) * k, s, rate)


def read(slab):
    return [slab[:, cut(c)] for c in range(slab.shape[1] // LANES)]


def write(slab, tiles):
    for c, t in enumerate(tiles):
        slab[:, cut(c)] = t


def early_kernel(tiles, halves, slabs, u, ue0, ue1, cs):
    rows = slabs.shape[1]
    odd = upper(1)

    def flow(r):
        if r == 1:
            return pick(odd, read(ue0.at[1, 1]), read(ue1.at[1, 1]))
        if r == rows - 2:
            return pick(odd, read(ue1.at[1, 1]), read(ue0.at[1, 1]))
        return read(u.at[1, r - 2])

    step = Step(
        tiles, halves, lambda r: read(slabs.at[0, r]), lambda r: read(slabs.at[2, r]), flow,
        lambda r: (read(u.at[2, r - 2]), read(u.at[0, r - 2])), lambda r: read(slabs.at[1, r]),
    )
    for r in range(2, rows - 2):
        for k, v in enumerate(step.run(r)):
            write(cs.at[k, r - 2], v)


def static_readers(ends, up, slabs, halo, there, flags):
    rows = slabs.shape[1]
    first, last = ends_of(*ends)

    def conc(r):
        if 0 <= r < rows:
            return read(slabs.at[0, r])
        beyond = read(halo.at[13] if r in (-1, rows) else there.at[3])
        return pick(last, read(slabs.at[0, rows - 1]), beyond) if up else [jnp.where(first, ZERO, t) for t in beyond]

    def poro(r):
        if 0 <= r < rows:
            return read(slabs.at[2, r])
        return pick(last if up else first, read(flags.at[1 if up else 0]), read(there.at[4]))

    return conc, poro


def rim_kernel(tiles, halves, ends, chain, g, fac, ghost, u, slabs, halo, after, ue, cs, send):
    rows = g.shape[1]
    lane, sub = iotas()

    def side(up):
        x, beside = (rows - 1, rows - 2) if up else (0, 1)
        lo, hi, place = (None, ghost, "last") if up else (ghost, None, "first")
        for n, (at, where) in enumerate(((x, place), (beside, "mid"))):
            for c in range(tiles):
                f = stream(g, lo, hi, at, c, tiles, halves, lane, sub, where)
                for i, v in enumerate(speed(f, fac[at, :, cut(c)])):
                    ue[n, i, :, cut(c)] = v
        conc, poro = static_readers(ends, up, slabs, halo, None, None)

        def vel(k, r):
            return read(ue.at[0 if r == x else 1, k] if r in (x, beside) else u.at[k, r - 2])

        step = Step(
            tiles, halves, conc, poro, lambda r: vel(1, r), lambda r: (vel(2, r), vel(0, r)),
            lambda r: read(slabs.at[1, r]),
        )
        edge = step.run(x, low=up, high=not up)
        inward = step.run(beside)
        for i, new in enumerate((edge, inward)):
            for k in range(2):
                write(cs.at[i, k], new[k])
            write(send.at[1 + i], new[0])
        send[0] = ue[0, 1]
        send[3] = slabs[0, beside]
        send[4] = slabs[2, x]

    by_side(chain, side)


def state_reader(rows, edge, inner, rims):
    def state(k, r):
        if r in (0, rows - 1):
            return edge(k, r)
        if r in (1, rows - 2):
            return rims(k, r)
        return read(inner.at[k, r - 2])

    return state


def middle_kernel(tiles, halves, slabs, u, inner, rim0, rim1, out):
    rows = slabs.shape[1]
    odd = upper(1)

    def rims(k, r):
        a, b = (rim0, rim1) if r == 1 else (rim1, rim0)
        return pick(odd, read(a.at[1, k]), read(b.at[1, k]))

    state = state_reader(rows, None, inner, rims)
    step = Step(
        tiles, halves, lambda r: state(0, r), lambda r: read(slabs.at[2, r]), lambda r: read(u.at[1, r - 2]),
        lambda r: (read(u.at[2, r - 2]), read(u.at[0, r - 2])), lambda r: state(1, r),
    )
    for r in range(3, rows - 3):
        write(out.at[r - 3], step.run(r)[0])


def late_kernel(
    tiles, halves, ends, chain, slabs, u, ue, inner, rim, halo, flags, there, after, out
):
    rows = slabs.shape[1]
    first, last = ends_of(*ends)

    def side(up):
        x = rows - 1 if up else 0
        beyond = rows if up else -1
        ghost = last if up else first
        conc, poro = static_readers(ends, up, slabs, halo, there, flags)

        def vel(k, r):
            if r == beyond:
                return pick(ghost, read(ue.at[0, 1]), read(there.at[0]))
            if r in (x, x - 1 if up else x + 1):
                return read(ue.at[0 if r == x else 1, k])
            return read(u.at[k, r - 2])

        def cross(r):
            return vel(2, r), vel(0, r)

        one = Step(tiles, halves, conc, poro, lambda r: vel(1, r), cross, None)
        flux = one.flow_face(x if up else -1)
        sign = np.float32(-1.0 if up else 1.0)
        edge = each(lambda c, f, p: c + sign * f / p, read(rim.at[0, 0]), flux, floored(poro(x)))
        outer = each(lambda c, f, p: c - sign * f / p, read(there.at[1]), flux, floored(poro(beyond)))
        second = read(there.at[2])
        if up:
            outer, second = pick(ghost, edge, outer), pick(ghost, edge, second)
        else:
            outer, second = ([jnp.where(ghost, ZERO, t) for t in v] for v in (outer, second))
        state = state_reader(
            rows, lambda k, r: read(rim.at[0, k]) if k else edge, inner, lambda k, r: read(rim.at[1, k])
        )

        def after_one(r):
            if r < 0 or r >= rows:
                return outer if r == beyond else second
            return state(0, r)

        two = Step(tiles, halves, after_one, poro, lambda r: vel(1, r), cross, lambda r: state(1, r))
        for i in range(3):
            new = two.run(rows - 1 - i if up else i)
            write(out.at[i], new[0])
            if i == 0:
                write(out.at[3], new[1])

    by_side(chain, side)


def deal_kernel(tiles, halves, parts, inner, rim0, rim1, late0, late1, mid, *refs):
    *blocks, whole = refs
    rows = inner.shape[1] + 4
    odd = upper(1)
    _, sub = iotas()
    for c in range(tiles):

        def ends_pick(a, b):
            return jnp.where(odd, a, b)

        lo = [ends_pick(late0[i, :, cut(c)], late1[i, :, cut(c)]) for i in range(4)]
        hi = [ends_pick(late1[i, :, cut(c)], late0[i, :, cut(c)]) for i in range(4)]
        conc = lo[:3] + [mid[r, :, cut(c)] for r in range(rows - 6)] + hi[2::-1]
        left = [lo[3]]
        for r in range(1, rows - 1):
            if r in (1, rows - 2):
                a, b = (rim0, rim1) if r == 1 else (rim1, rim0)
                cc, ss = (ends_pick(a[1, k, :, cut(c)], b[1, k, :, cut(c)]) for k in range(2))
            else:
                cc, ss = (inner[k, r - 2, :, cut(c)] for k in range(2))
            left.append(ss - np.float32(DEPLETION) * loss([ss], [cc])[0])
        left.append(hi[3])
        run = whole.shape[3]
        for k, tile in enumerate((conc, left)):
            for i, t in enumerate(swap_tile(tile, sub)):
                column = (i % halves * tiles + c) * SUBS
                at = column % run
                whole[column // run, k, i // halves, at : at + SUBS, :] = t
    for k in range(parts):
        blocks[k][...] = whole[lax.axis_index("narrow") ^ k]


def gather_kernel(parts, order, *refs):
    blocks = refs[:parts]
    *outs, sems = refs[parts:]
    copies = []
    for k, block in zip(order, blocks):
        origin = lax.axis_index("narrow") ^ k
        for i, out in enumerate(outs):
            copies.append(pltpu.make_async_copy(block.at[i], out.at[:, origin], sems.at[i, k]))
            copies[-1].start()
    for copy in copies:
        copy.wait()


def call(kernel, out_shape, args, scratch=(), hbm=(), free=(), hbm_out=(), name=None, aliases=None):
    def spec(i, hbm, free=()):
        return pl.BlockSpec(memory_space=pltpu.HBM if i in hbm else pl.ANY if i in free else pltpu.VMEM)

    single = not isinstance(out_shape, tuple)
    shapes = (out_shape,) if single else out_shape
    out = pl.pallas_call(
        kernel,
        out_shape=shapes,
        in_specs=[spec(i, hbm, free) for i in range(len(args))],
        out_specs=tuple(spec(i, hbm_out) for i in range(len(shapes))),
        scratch_shapes=list(scratch),
        name=name,
        input_output_aliases=aliases or {},
        compiler_params=pltpu.CompilerParams(vmem_limit_bytes=VMEM_LIMIT),
        cost_estimate=pl.CostEstimate(flops=1024, bytes_accessed=1024, transcendentals=0),
    )(*args)
    return out[0] if single else out


def local(populations, phase, porosity, napl, concentration, flags):
    layers, rows, width = phase.shape
    halves = SUBS // layers
    length = width // halves
    tiles = length // LANES
    parts = lax.axis_size("narrow")
    strips = lax.axis_size("wide") * parts
    both = ("wide", "narrow")
    pairs = (
        [(i, i ^ 1) for i in range(strips)],
        [(i, (i + 1 if i % 2 else i - 1) % strips) for i in range(strips)],
    )
    slab = (SUBS, length)
    ends = (parts, strips)
    run = width // LANES * SUBS // parts

    def hold(*shape, dtype=F32):
        return pltpu.VMEM(shape, dtype)

    def swap(chain, array):
        return lax.ppermute(array, both, pairs[chain])

    pop = to_view(populations)
    views = [to_view(a) for a in (phase, concentration, napl, porosity)]
    flat = views[0].shape
    chunks = pop.reshape(19, SUBS, tiles, SUBS, LANES)
    given = [pltpu.with_memory_space_constraint(a, pltpu.HBM) for a in (chunks, *views, flags)]
    popv, phv, cov, nav, pov, flv, row1, send = call(
        functools.partial(first_kernel, tiles, halves),
        (
            hold(*chunks.shape), hold(*flat, dtype=jnp.int32), hold(*flat), hold(*flat), hold(*flat),
            hold(*flags.shape, dtype=jnp.int32), hold(19, *slab), hold(14, *slab),
        ),
        given, scratch=(pltpu.VMEM((19, *slab), F32), pltpu.SemaphoreType.DMA((4 * tiles + 5,))),
        hbm=range(6), name="first",
    )
    popv = popv.reshape(pop.shape)
    halo1 = head1 = swap(1, send)
    row0, send = call(
        functools.partial(second_kernel, tiles, halves), (hold(19, *slab), hold(14, *slab)), (popv, phv, send),
        scratch=(pltpu.VMEM((19, *slab), F32),), free=(2,), name="second",
    )
    halo0 = head0 = swap(0, send)
    g, fac, start, slabs, open_ends = call(
        functools.partial(first_inner_kernel, tiles, halves),
        (
            hold(19, rows, *slab), hold(rows, *slab), hold(19, rows, *slab), hold(3, rows, *slab),
            hold(2, *slab),
        ),
        (popv, phv, cov, nav, pov, flv, row0, row1), name="first_inner",
    )

    def inner_rows(g, after):
        return call(
            functools.partial(inner_kernel, tiles, halves), hold(19, rows, *slab), (g, fac, after), free=(2,),
            name="inner",
        )

    def arrive(chain, g, halo, head, after, new):
        return call(
            functools.partial(arrive_kernel, tiles, halves, chain), (hold(19, rows, *slab), hold(5, *slab)),
            (g, fac, halo, head, after, new), free=(4, 5), name=f"arrive{chain}", aliases={5: 0},
        )

    def far(chain, g, ghost, after):
        return call(
            functools.partial(far_kernel, tiles, halves, chain), (hold(19, *slab), hold(14, *slab)),
            (g, fac, ghost, slabs, after), scratch=(pltpu.VMEM((19, *slab), F32),), free=(4,), name=f"far{chain}",
        )

    def rim(chain, g, ghost, halo, after):
        return call(
            functools.partial(rim_kernel, tiles, halves, ends, chain),
            (hold(2, 3, *slab), hold(2, 2, *slab), hold(5, *slab)),
            (g, fac, ghost, u, slabs, halo, after), free=(6,), name=f"rim{chain}",
        )

    after = slabs
    for pair in range(LBM_STEPS // 2):
        new = inner_rows(g, after)
        if pair < LBM_STEPS // 2 - 1:
            later, ghost1 = arrive(1, g, halo1, head1, g, new)
            row1, send1 = far(1, later, ghost1, ghost1)
            halo1 = swap(1, send1)
            later, ghost0 = arrive(0, g, halo0, head0, send1, later)
            row0, send0 = far(0, later, ghost0, ghost0)
            halo0 = swap(0, send0)
            new = inner_rows(later, send0)
            g = call(
                put_kernel, hold(19, rows, *slab), (new, row0, row1), name="put", aliases={0: 0}, free=(0,)
            )
            after = g
    u = call(
        functools.partial(inner_speed_kernel, tiles, halves), hold(3, rows - 4, *slab), (new, fac, new),
        free=(2,), name="inner_speed",
    )
    later, ghost1 = arrive(1, g, halo1, head1, u, new)
    ue1, rim1, send1 = rim(1, later, ghost1, halo1, ghost1)
    there1 = swap(1, send1)
    g, ghost0 = arrive(0, g, halo0, head0, send1, later)
    ue0, rim0, send0 = rim(0, g, ghost0, halo0, ghost0)
    there0 = swap(0, send0)
    inner = call(
        functools.partial(early_kernel, tiles, halves), hold(2, rows - 4, *slab), (slabs, u, ue0, ue1),
        name="early",
    )
    mid = call(
        functools.partial(middle_kernel, tiles, halves), hold(rows - 6, *slab), (slabs, u, inner, rim0, rim1),
        name="middle",
    )
    out, token = call(
        functools.partial(final_kernel, tiles, halves),
        (jax.ShapeDtypeStruct((19, *flat), F32), hold(SUBS, LANES)),
        (g, fac, ghost0, ghost1, start, mid),
        scratch=(pltpu.VMEM((19, *flat), F32), pltpu.SemaphoreType.DMA((19,))),
        free=(5,), hbm_out=(0,), name="final",
    )
    late1 = call(
        functools.partial(late_kernel, tiles, halves, ends, 1), hold(4, *slab),
        (slabs, u, ue1, inner, rim1, halo1, open_ends, there1, token), free=(8,), name="late1",
    )
    late0 = call(
        functools.partial(late_kernel, tiles, halves, ends, 0), hold(4, *slab),
        (slabs, u, ue0, inner, rim0, halo0, open_ends, there0, late1), free=(8,), name="late0",
    )
    block = (2, layers, run, LANES)
    blocks = call(
        functools.partial(deal_kernel, tiles, halves, parts), tuple(hold(*block) for _ in range(parts)),
        (inner, rim0, rim1, late0, late1, mid),
        scratch=(pltpu.VMEM((parts, *block), F32),), name="deal",
    )
    order = [0, *range(2, parts), 1]
    came = [blocks[0]]
    for k in order[1:]:
        came.append(lax.ppermute(blocks[k], "narrow", [(i, i ^ k) for i in range(parts)]))
    tile = (layers, parts, run, LANES)
    conc_out, napl_out = call(
        functools.partial(gather_kernel, parts, order),
        (jax.ShapeDtypeStruct(tile, F32), jax.ShapeDtypeStruct(tile, F32)),
        came, scratch=(pltpu.SemaphoreType.DMA((2, parts)),), hbm_out=(0, 1), name="gather",
    )
    shape = (layers, rows * parts, width // parts)

    def tile_of(a):
        return from_view(a.reshape(layers * parts * run, LANES), shape)

    return from_view(out, populations.shape), tile_of(conc_out), tile_of(napl_out)


def solution(mesh):
    strip = P(None, ("wide", "narrow"), None)
    in_specs = (P(None, None, ("wide", "narrow"), None), strip, strip, strip, strip, P())
    tile = P(None, "wide", "narrow")
    out_specs = (P(None, None, ("wide", "narrow"), None), tile, tile)
    return jax.shard_map(local, mesh=mesh, in_specs=in_specs, out_specs=out_specs, check_vma=False)
```
